768 devices in a mesh: gx: 24 (over z, core), gy: 8 (over y), gz: 4 (over x).
Axes of the slice: x: 4, y: 8, z: 12, core: 2. Of those that a mesh axis runs over, the one named last changes fastest.
Arguments:
- right_side: float32 [384, 256, 512], P('gx', 'gy', 'gz'), may hold values from -8 to 8
- diagonal: float32 [384, 256, 512], P('gx', 'gy', 'gz'), may hold values from 0.05 to 2
Outputs:
- solution_field: float32 [384, 256, 512], P('gx', 'gy', 'gz')
- residual: float32 [384, 256, 512], P('gx', 'gy', 'gz')
The draws below stay inside these ranges and needn't reach their ends.
All inputs are finite; a program needn't handle non-finite values.
Results may differ from the reference program's by a relative error of at most 0.00018.
Values sent between devices are 32-bit elements; how exact they have to be, the bound alone decides.
No kernel may reach another device: no remote copies, remote signals or barrier semaphores. Data moves between devices by JAX's collectives and lax.ppermute only.
A program may use at most 64 MiB of HBM per device.

```python
import math
import jax
import jax.numpy as jnp

ITERS = 2
FSWEEPS = 3
CSWEEPS = 4
COARSEN = 4
NX = 384
NY = 256
NZ = 512


def draw_right_side(key, part):
    key = jax.random.fold_in(key, 7)
    second_key = jax.random.fold_in(key, 1)
    position = jnp.arange(NX, dtype=jnp.float32) / max(NX - 1, 1)
    growth = jnp.power(3.0, position)[:, None, None]
    jitter = jax.random.truncated_normal(second_key, -2.5, 2.5, (NX, NY, NZ), jnp.float32)
    return jitter * growth


def block_scale(stream_key, shape, cuts, least, largest):
    level, own = 1.0, jax.random.fold_in(stream_key, 6)
    for axis_at, blocks in cuts:
        heights = jnp.exp(jax.random.uniform(jax.random.fold_in(own, axis_at), (blocks,), jnp.float32, least / len(cuts), largest / len(cuts)))
        level = level * jnp.repeat(heights, shape[axis_at] // blocks).reshape([-1 if axis == axis_at else 1 for axis in range(len(shape))])
    return level


def setup_inputs(seed: int = 0) -> dict:
    seeds = jax.random.split(jax.random.key(seed), 3)
    right_side = draw_right_side(jax.random.fold_in(seeds[2], 71), 0)
    diagonal = jnp.clip(jnp.exp(math.log(2.0) - 3.6888794 * jax.random.uniform(seeds[1], (NX, NY, NZ), jnp.float32) ** block_scale(seeds[1], (NX, NY, NZ), ((0, 24), (1, 8), (2, 4)), -0.2, 0.2)), 0.05, 2.0)
    return {"right_side": right_side, "diagonal": diagonal}


damping = 2.0 / 3.0


def apply_operator(field, diag_plus):
    padded = jnp.pad(field, 1)
    beside = padded[2:, 1:-1, 1:-1] + padded[:-2, 1:-1, 1:-1]
    beside = beside + padded[1:-1, 2:, 1:-1] + padded[1:-1, :-2, 1:-1]
    beside = beside + padded[1:-1, 1:-1, 2:] + padded[1:-1, 1:-1, :-2]
    return diag_plus * field - beside


def block_mean(field):
    first, second, third = field.shape
    shaped = field.reshape(first // COARSEN, COARSEN, second // COARSEN, COARSEN, third // COARSEN, COARSEN)
    return jnp.mean(shaped, axis=(1, 3, 5))


def expand_blocks(field):
    first, second, third = field.shape
    wide = jnp.broadcast_to(field[:, None, :, None, :, None], (first, COARSEN, second, COARSEN, third, COARSEN))
    return wide.reshape(first * COARSEN, second * COARSEN, third * COARSEN)


def precondition(vector, fine_diag, coarse_diag):
    smooth = damping * vector / fine_diag
    for sweep_index in range(FSWEEPS - 1):
        smooth = smooth + damping * (vector - apply_operator(smooth, fine_diag)) / fine_diag
    coarse_rhs = (COARSEN * COARSEN) * block_mean(vector)
    coarse = damping * coarse_rhs / coarse_diag
    for sweep_index in range(CSWEEPS - 1):
        coarse = coarse + damping * (coarse_rhs - apply_operator(coarse, coarse_diag)) / coarse_diag
    return smooth + expand_blocks(coarse)


def reference(right_side, diagonal):
    fine_diag = 6.0 + diagonal
    coarse_diag = 6.0 + (COARSEN * COARSEN) * block_mean(diagonal)
    solution = jnp.zeros_like(right_side)
    residual = right_side
    precond = precondition(residual, fine_diag, coarse_diag)
    direction = precond
    rho_value = jnp.sum(residual * precond)
    for iter_index in range(ITERS):
        image = apply_operator(direction, fine_diag)
        step_length = rho_value / jnp.sum(direction * image)
        solution = solution + step_length * direction
        residual = residual - step_length * image
        if iter_index + 1 < ITERS:
            precond = precondition(residual, fine_diag, coarse_diag)
            rho_next = jnp.sum(residual * precond)
            direction = precond + (rho_next / rho_value) * direction
            rho_value = rho_next
    return solution, residual
```

```python
import functools

import jax
import jax.numpy as jnp
from jax import lax
from jax.experimental import pallas as pl
from jax.experimental.pallas import tpu as pltpu
from jax.sharding import PartitionSpec as P

ITERS = 2
FSWEEPS = 3
CSWEEPS = 4
COARSEN = 4
damping = 2.0 / 3.0
keep = 1.0 - damping

NX, NY, NZ = 16, 32, 128
HF = 3
HC = 4
CX, CY = NX // COARSEN, NY // COARSEN
EX = NX + 2 * HF
EY = 40
EC = CX + 2 * HC
ER = CY + 2 * HC
FACE = HF * NY
VMEM = pl.BlockSpec(memory_space=pltpu.VMEM)
F32 = jnp.float32


def lanes(shape):
    return lax.broadcasted_iota(jnp.int32, shape, len(shape) - 1)


def roll(x, shift, axis=-1):
    axis = axis % x.ndim
    return pltpu.roll(x, shift % x.shape[axis], axis)


def group_sum(x):
    lane = lanes(x.shape)
    x = x + jnp.where(lane % 2 == 0, roll(x, -1), roll(x, 1))
    return x + jnp.where(lane % 4 < 2, roll(x, -2), roll(x, 2))


def block_sums(planes, tmp):
    tmp[...] = group_sum(planes[0] + planes[1] + planes[2] + planes[3])
    rows = [tmp[pl.ds(k, CY, stride=COARSEN), :] for k in range(COARSEN)]
    return rows[0] + rows[1] + rows[2] + rows[3]


def start_kernel(b_ref, d_ref, v_ref, up_ref, down_ref, tmp):
    for c in range(CX):
        fine = []
        for i in range(COARSEN * c, COARSEN * (c + 1)):
            v_ref[i] = damping / (6.0 + d_ref[i])
        g = block_sums([b_ref[COARSEN * c + k] for k in range(COARSEN)], tmp) * 0.25
        cd = 6.0 + block_sums([d_ref[COARSEN * c + k] for k in range(COARSEN)], tmp) * 0.25
        vc = damping / cd
        for ref in (up_ref, down_ref):
            ref[2 * FACE + CY * c : 2 * FACE + CY * (c + 1)] = g
            ref[2 * FACE + CY * (CX + c) : 2 * FACE + CY * (CX + c + 1)] = vc
    for k in range(HF):
        for f, ref in enumerate((b_ref, v_ref)):
            down_ref[FACE * f + NY * k : FACE * f + NY * (k + 1)] = ref[k]
            up_ref[FACE * f + NY * k : FACE * f + NY * (k + 1)] = ref[NX - HF + k]


def fine_plane(k, f, own, before, after):
    if k < HF:
        return before[FACE * f + NY * k : FACE * f + NY * (k + 1)]
    if k < HF + NX:
        return own[f][k - HF]
    k = k - HF - NX
    return after[FACE * f + NY * k : FACE * f + NY * (k + 1)]


def coarse_plane(c, f, fields, mine, before, after):
    ref, c = (before, c) if c < HC else (mine, c - HC) if c < HC + CX else (after, c - HC - CX)
    at = FACE * fields + CY * (CX * f + c)
    return ref[at : at + CY]


def rows_kernel(fields, *refs):
    own, (mine, before, after, up_ref, down_ref) = refs[:fields], refs[fields:]
    for k in range(EX):
        for f in range(fields):
            plane = fine_plane(k, f, own, before, after)
            down_ref[k, 4 * f : 4 * f + HF] = plane[:HF]
            up_ref[k, 4 * f : 4 * f + HF] = plane[NY - HF :]
    for c in range(EC):
        for f in range(fields):
            plane = coarse_plane(c, f, fields, mine, before, after)
            at, row = (EX + c, 4 * f) if fields == 2 else (c, 4)
            down_ref[at, row : row + HC] = plane[:HC]
            up_ref[at, row : row + HC] = plane[CY - HC :]


def lanes_kernel(fields, *refs):
    own, refs = refs[:fields], refs[fields:]
    mine, before, after, low, high = refs[:5]
    fine, coarse, (up_ref, down_ref) = refs[5 : 5 + fields], refs[5 + fields : 5 + 2 * fields], refs[5 + 2 * fields :]
    lane = lanes((EY, NZ))
    for f in range(fields):
        up = jnp.zeros((EY, NZ), F32)
        down = jnp.zeros((EY, NZ), F32)
        for k in range(EX):
            fine[f][k, 0:8] = jnp.zeros((8, NZ), F32)
            fine[f][k, EY - 8 : EY] = jnp.zeros((8, NZ), F32)
            fine[f][k, 4 - HF : 4] = low[k, 4 * f : 4 * f + HF]
            fine[f][k, 4 : 4 + NY] = fine_plane(k, f, own, before, after)
            fine[f][k, 4 + NY : 4 + NY + HF] = high[k, 4 * f : 4 * f + HF]
            plane = fine[f][k]
            here = lane // 4 == k
            up = jnp.where(here, roll(plane, 4 * k - (NZ - 4)), up)
            down = jnp.where(here, roll(plane, 4 * k), down)
        up_ref[EY * f : EY * (f + 1)] = up
        down_ref[EY * f : EY * (f + 1)] = down
    lane = lanes((ER, NZ))
    for f in range(fields):
        for half in range(2):
            up = jnp.zeros((ER, NZ), F32)
            down = jnp.zeros((ER, NZ), F32)
            for c in range(8 * half, min(EC, 8 * half + 8)):
                at, row = (EX + c, 4 * f) if fields == 2 else (c, 4)
                coarse[f][c, 0:HC] = low[at, row : row + HC]
                coarse[f][c, HC : HC + CY] = coarse_plane(c, f, fields, mine, before, after)
                coarse[f][c, HC + CY : ER] = high[at, row : row + HC]
                plane = coarse[f][c]
                here = lane // 16 == c - 8 * half
                up = jnp.where(here, roll(plane, 16 * (c - 8 * half) - (NZ - 16)), up)
                down = jnp.where(here, roll(plane, 16 * (c - 8 * half)), down)
            at = EY * fields + ER * (2 * f + half)
            up_ref[at : at + ER] = up
            down_ref[at : at + ER] = down


def spread_fine(k, f, before, after):
    lane = lanes((EY, NZ))
    right = roll(after[EY * f : EY * (f + 1)], -4 * k)
    left = roll(before[EY * f : EY * (f + 1)], NZ - 4 - 4 * k)
    return jnp.where(lane < 4, right, jnp.where(lane >= NZ - 4, left, 0.0))


def spread_coarse(c, f, fields, before, after):
    lane = lanes((ER, NZ))
    at, place = EY * fields + ER * (2 * f + c // 8), 16 * (c % 8)
    right = roll(after[at : at + ER], -place)
    left = roll(before[at : at + ER], NZ - 16 - place)
    return jnp.where(lane < 16, right, jnp.where(lane >= NZ - 16, left, 0.0))


def crossed(block, beyond, step):
    lane = lanes(block.shape)
    below, below_beyond = roll(block, step), roll(beyond, step)
    above, above_beyond = roll(block, -step), roll(beyond, -step)
    low, high = lane < step, lane >= NZ - step
    return (
        jnp.where(low, below_beyond, below) + jnp.where(high, above_beyond, above),
        jnp.where(low, below, below_beyond) + jnp.where(high, above, above_beyond),
    )


PAD = 8


def neighbours(src, k, rows, step=1):
    at = PAD
    here = [src[part, k, at : at + rows] for part in range(2)]
    along = crossed(here[0], here[1], step)
    out = []
    for part in range(2):
        beside = src[part, k - 1, at : at + rows] + src[part, k + 1, at : at + rows]
        beside = beside + (src[part, k, at - 1 : at - 1 + rows] + src[part, k, at + 1 : at + 1 + rows])
        out.append(beside + along[part])
    return here, out


def expand(coarse, part, k, lo):
    c = (k - HF) // COARSEN + HC
    first = lax.broadcasted_iota(jnp.int32, (8, NZ), 0) < 4
    groups = []
    for j in range(EY // 8):
        row = PAD + 3 + 2 * j
        a = jnp.broadcast_to(coarse[part, c, row : row + 1], (8, NZ))
        b = jnp.broadcast_to(coarse[part, c, row + 1 : row + 2], (8, NZ))
        groups.append(jnp.where(first, a, b))
    return jnp.concatenate(groups, axis=0)


def precondition(rhs, weight, crhs, cweight, fa, fb, ca, cb):
    for ref, rows in ((fa, EY), (fb, EY), (ca, ER), (cb, ER)):
        for part in range(2):
            for k in range(ref.shape[1]):
                ref[part, k, 0:PAD] = jnp.zeros((PAD, NZ), F32)
                ref[part, k, PAD + rows :] = jnp.zeros((PAD, NZ), F32)
    for k in range(EC):
        for part in range(2):
            ca[part, k, PAD : PAD + ER] = cweight[part][k] * crhs[part][k]
    src, dst = ca, cb
    for sweep in range(1, CSWEEPS):
        for k in range(sweep, EC - sweep):
            here, beside = neighbours(src, k, ER, COARSEN)
            for part in range(2):
                dst[part, k, PAD : PAD + ER] = keep * here[part] + cweight[part][k] * (crhs[part][k] + beside[part])
        src, dst = dst, src
    coarse = src
    for k in range(EX):
        for part in range(2):
            fa[part, k, PAD : PAD + EY] = weight[part][k] * rhs[part][k]
    src, dst = fa, fb
    for sweep in range(1, FSWEEPS):
        for k in range(sweep, EX - sweep):
            here, beside = neighbours(src, k, EY)
            for part in range(2):
                new = keep * here[part] + weight[part][k] * (rhs[part][k] + beside[part])
                if sweep == FSWEEPS - 1:
                    new = new + expand(coarse, part, k, 0)
                dst[part, k, PAD : PAD + EY] = new
        src, dst = dst, src


def image_plane(src, d_ref, i):
    k, at = i + HF, PAD + 4
    here = src[0, k, at : at + NY]
    beside = src[0, k - 1, at : at + NY] + src[0, k + 1, at : at + NY]
    beside = beside + (src[0, k, at - 1 : at - 1 + NY] + src[0, k, at + 1 : at + 1 + NY])
    along, _ = crossed(here, src[1, k, at : at + NY], 1)
    return here, (6.0 + d_ref[i]) * here - (beside + along)


def add_up(x):
    return (x[0:8] + x[8:16]) + (x[16:24] + x[24:32])


def store_sums(out_ref, totals):
    row = lax.broadcasted_iota(jnp.int32, (8, NZ), 0)
    out = jnp.zeros((8, NZ), F32)
    for i, total in enumerate(totals):
        out = jnp.where(row == i, jnp.broadcast_to(jnp.sum(total, axis=0, keepdims=True), (8, NZ)), out)
    out_ref[...] = out


def first_kernel(
    b_ref, d_ref, b, v, g, vc, before, after, p_ref, q_ref, vh_ref, vch_ref, up_ref, down_ref, sum_ref,
    bh_ref, gh_ref, fa, fb, ca, cb, tmp,
):
    for k in range(EX):
        bh_ref[k] = spread_fine(k, 0, before, after)
        vh_ref[k] = spread_fine(k, 1, before, after)
    for c in range(EC):
        gh_ref[c] = spread_coarse(c, 0, 2, before, after)
        vch_ref[c] = spread_coarse(c, 1, 2, before, after)
    precondition((b, bh_ref), (v, vh_ref), (g, gh_ref), (vc, vch_ref), fa, fb, ca, cb)
    rp = jnp.zeros((8, NZ), F32)
    pq = jnp.zeros((8, NZ), F32)
    for i in range(NX):
        p, q = image_plane(fa, d_ref, i)
        p_ref[i] = p
        q_ref[i] = q
        rp = rp + add_up(b_ref[i] * p)
        pq = pq + add_up(p * q)
    store_sums(sum_ref, [rp, pq])
    for c in range(CX):
        mean = block_sums([q_ref[COARSEN * c + k] for k in range(COARSEN)], tmp) * 0.25
        for ref in (up_ref, down_ref):
            ref[FACE + CY * c : FACE + CY * (c + 1)] = mean
    for k in range(HF):
        down_ref[NY * k : NY * (k + 1)] = q_ref[k]
        up_ref[NY * k : NY * (k + 1)] = q_ref[NX - HF + k]


def second_kernel(
    b_ref, d_ref, p_ref, q_ref, q, v, vh_ref, gq, vc, vch_ref, before, after, first_ref, m_ref, im_ref, sum_ref,
    qh_ref, gh_ref, fa, fb, ca, cb,
):
    for k in range(EX):
        qh_ref[k] = spread_fine(k, 0, before, after)
    for c in range(EC):
        gh_ref[c] = spread_coarse(c, 0, 1, before, after)
    precondition((q, qh_ref), (v, vh_ref), (gq, gh_ref), (vc, vch_ref), fa, fb, ca, cb)
    sums = [jnp.zeros((8, NZ), F32)] * 4
    for i in range(NX):
        m, im = image_plane(fa, d_ref, i)
        m_ref[i] = m
        im_ref[i] = im
        pairs = ((q_ref[i], m), (b_ref[i], m), (p_ref[i], im), (m, im))
        sums = [s + add_up(x * y) for s, (x, y) in zip(sums, pairs)]
    store_sums(sum_ref, [first_ref[0:1], first_ref[1:2]] + sums)


def last_kernel(b_ref, p_ref, q_ref, m_ref, im_ref, sum_ref, x_ref, r_ref):
    rp, pq, qm, rm, pim, mim = [jnp.sum(sum_ref[i : i + 1], axis=1, keepdims=True) for i in range(6)]
    alpha = rp / pq
    rho = rp - alpha * (pq + rm) + alpha * alpha * qm
    scale = 1.0 + rho / rp
    alpha_next = rho / (scale * scale * pq - scale * alpha * (pim + qm) + alpha * alpha * mim)
    along = alpha + alpha_next * scale
    across = alpha_next * alpha
    for i in range(NX):
        x_ref[i] = along * p_ref[i] - across * m_ref[i]
        r_ref[i] = b_ref[i] - along * q_ref[i] + across * im_ref[i]


def call(kernel, outs, scratch=(), name=None):
    def run(*args):
        return pl.pallas_call(
            kernel,
            out_shape=[jax.ShapeDtypeStruct(shape, F32) for shape in outs],
            in_specs=[VMEM] * len(args),
            out_specs=[VMEM] * len(outs),
            scratch_shapes=[pltpu.VMEM(shape, F32) for shape in scratch],
            compiler_params=pltpu.CompilerParams(vmem_limit_bytes=24 * 2**20),
            name=name,
        )(*args)

    return run


def both_ways(up, down, axis):
    count = lax.axis_size(axis)
    before = lax.ppermute(up, axis, [(i, i + 1) for i in range(count - 1)])
    after = lax.ppermute(down, axis, [(i + 1, i) for i in range(count - 1)])
    return before, after


def total(x, axis):
    count = lax.axis_size(axis)
    spread = jnp.broadcast_to(x[None], (count,) + x.shape)
    return jnp.sum(lax.all_to_all(spread, axis, 0, 0, tiled=True), axis=0)


def exchange(own, up, down, fields):
    mine = up
    before, after = both_ways(up, down, "gx")
    height = EX + EC if fields == 2 else EX
    up, down = call(functools.partial(rows_kernel, fields), [(height, 8, NZ)] * 2, name="rows")(*own, mine, before, after)
    low, high = both_ways(up, down, "gy")
    message = (EY + 2 * ER) * fields
    arrays = call(
        functools.partial(lanes_kernel, fields),
        [(EX, EY, NZ)] * fields + [(EC, ER, NZ)] * fields + [(message, NZ)] * 2,
        name="lanes",
    )(*own, mine, before, after, low, high)
    return list(arrays[:-2]) + list(both_ways(arrays[-2], arrays[-1], "gz"))


def on_device(b, d):
    block, fine, coarse = (NX, NY, NZ), (EX, EY, NZ), (EC, ER, NZ)
    work = [(2, EX, EY + 2 * PAD, NZ)] * 2 + [(2, EC, ER + 2 * PAD, NZ)] * 2
    face = FACE + CX * CY
    v, up, down = call(start_kernel, [block, (2 * face, NZ), (2 * face, NZ)], [(NY, NZ)], name="start")(b, d)
    be, ve, ge, vce, before, after = exchange((b, v), up, down, 2)
    p, q, vh, vch, up, down, sums = call(
        first_kernel,
        [block, block, fine, coarse, (face, NZ), (face, NZ), (8, NZ)],
        [fine, coarse] + work + [(NY, NZ)],
        name="first",
    )(b, d, be, ve, ge, vce, before, after)
    qe, gqe, before, after = exchange((q,), up, down, 1)
    m, im, sums = call(second_kernel, [block, block, (8, NZ)], [fine, coarse] + work, name="second")(
        b, d, p, q, qe, ve, vh, gqe, vce, vch, before, after, sums
    )
    for axis in ("gz", "gy", "gx"):
        sums = total(sums, axis)
    return call(last_kernel, [block, block], name="last")(b, p, q, m, im, sums)


def solution(mesh):
    spec = P("gx", "gy", "gz")
    return jax.shard_map(on_device, mesh=mesh, in_specs=(spec, spec), out_specs=(spec, spec), check_vma=False)
```

```python
import functools
import math

import jax
import jax.numpy as jnp
from jax import lax
from jax.experimental import pallas as pl
from jax.experimental.pallas import tpu as pltpu
from jax.sharding import PartitionSpec as P

ITERS = 2
FSWEEPS = 3
CSWEEPS = 4
COARSEN = 4
damping = 2.0 / 3.0
keep = 1.0 - damping

NX, NY, NZ = 16, 32, 128
HF = 3
HC = 4
CX, CY = NX // COARSEN, NY // COARSEN
EX = NX + 2 * HF
EY = 40
EC = CX + 2 * HC
ER = CY + 2 * HC
FACE = HF * NY
VMEM = pl.BlockSpec(memory_space=pltpu.VMEM)
F32 = jnp.float32


def lanes(shape):
    return lax.broadcasted_iota(jnp.int32, shape, len(shape) - 1)


def roll(x, shift, axis=-1):
    axis = axis % x.ndim
    return pltpu.roll(x, shift % x.shape[axis], axis)


def group_sum(x):
    lane = lanes(x.shape)
    x = x + jnp.where(lane % 2 == 0, roll(x, -1), roll(x, 1))
    return x + jnp.where(lane % 4 < 2, roll(x, -2), roll(x, 2))


def block_sums(planes, tmp):
    tmp[...] = group_sum(planes[0] + planes[1] + planes[2] + planes[3])
    rows = [tmp[pl.ds(k, CY, stride=COARSEN), :] for k in range(COARSEN)]
    return rows[0] + rows[1] + rows[2] + rows[3]


def start_kernel(b_hbm, d_hbm, b_ref, d_ref, v_ref, up_ref, down_ref, tmp, sems):
    copies = [
        pltpu.make_async_copy(src, dst, sems.at[i])
        for i, (src, dst) in enumerate(((b_hbm, b_ref), (d_hbm, d_ref)))
    ]
    for copy in copies:
        copy.start()
    for copy in copies:
        copy.wait()
    for c in range(CX):
        for i in range(COARSEN * c, COARSEN * (c + 1)):
            v_ref[i] = damping / (6.0 + d_ref[i])
        g = block_sums([b_ref[COARSEN * c + k] for k in range(COARSEN)], tmp) * 0.25
        cd = 6.0 + block_sums([d_ref[COARSEN * c + k] for k in range(COARSEN)], tmp) * 0.25
        vc = damping / cd
        for ref in (up_ref, down_ref):
            ref[2 * FACE + CY * c : 2 * FACE + CY * (c + 1)] = g
            ref[2 * FACE + CY * (CX + c) : 2 * FACE + CY * (CX + c + 1)] = vc
    for k in range(HF):
        for f, ref in enumerate((b_ref, v_ref)):
            down_ref[FACE * f + NY * k : FACE * f + NY * (k + 1)] = ref[k]
            up_ref[FACE * f + NY * k : FACE * f + NY * (k + 1)] = ref[NX - HF + k]


def inside():
    at = lax.axis_index("gx")
    return at > 0, at < lax.axis_size("gx") - 1


def fine_plane(k, f, own, before, after):
    if HF <= k < HF + NX:
        return own[f][k - HF]
    ref, ok, k = (before, inside()[0], k) if k < HF else (after, inside()[1], k - HF - NX)
    return jnp.where(ok, ref[FACE * f + NY * k : FACE * f + NY * (k + 1)], 0.0)


def coarse_plane(c, f, fields, mine, before, after):
    part, c = divmod(c, HC)
    at = FACE * fields + CY * (CX * f + c)
    plane = (before, mine, after)[part][at : at + CY]
    return plane if part == 1 else jnp.where(inside()[part // 2], plane, 0.0)


def rows_kernel(fields, *refs):
    own, (mine, before, after, up_ref, down_ref) = refs[:fields], refs[fields:]
    for k in range(EX):
        for f in range(fields):
            plane = fine_plane(k, f, own, before, after)
            down_ref[k, 4 * f : 4 * f + HF] = plane[:HF]
            up_ref[k, 4 * f : 4 * f + HF] = plane[NY - HF :]
    for c in range(EC):
        for f in range(fields):
            plane = coarse_plane(c, f, fields, mine, before, after)
            at, row = (EX + c, 4 * f) if fields == 2 else (c, 4)
            down_ref[at, row : row + HC] = plane[:HC]
            up_ref[at, row : row + HC] = plane[CY - HC :]


def lanes_kernel(fields, *refs):
    own, refs = refs[:fields], refs[fields:]
    mine, before, after, low, high = refs[:5]
    fine, coarse, (up_ref, down_ref) = refs[5 : 5 + fields], refs[5 + fields : 5 + 2 * fields], refs[5 + 2 * fields :]
    lane = lanes((EY, NZ))
    for f in range(fields):
        up = jnp.zeros((EY, NZ), F32)
        down = jnp.zeros((EY, NZ), F32)
        for k in range(EX):
            fine[f][k, 0:8] = jnp.zeros((8, NZ), F32)
            fine[f][k, EY - 8 : EY] = jnp.zeros((8, NZ), F32)
            fine[f][k, 4 - HF : 4] = low[k, 4 * f : 4 * f + HF]
            fine[f][k, 4 : 4 + NY] = fine_plane(k, f, own, before, after)
            fine[f][k, 4 + NY : 4 + NY + HF] = high[k, 4 * f : 4 * f + HF]
            plane = fine[f][k]
            here = lane // 4 == k
            up = jnp.where(here, roll(plane, 4 * k - (NZ - 4)), up)
            down = jnp.where(here, roll(plane, 4 * k), down)
        up_ref[EY * f : EY * (f + 1)] = up
        down_ref[EY * f : EY * (f + 1)] = down
    lane = lanes((ER, NZ))
    for f in range(fields):
        for half in range(2):
            up = jnp.zeros((ER, NZ), F32)
            down = jnp.zeros((ER, NZ), F32)
            for c in range(8 * half, min(EC, 8 * half + 8)):
                at, row = (EX + c, 4 * f) if fields == 2 else (c, 4)
                coarse[f][c, 0:HC] = low[at, row : row + HC]
                coarse[f][c, HC : HC + CY] = coarse_plane(c, f, fields, mine, before, after)
                coarse[f][c, HC + CY : ER] = high[at, row : row + HC]
                plane = coarse[f][c]
                here = lane // 16 == c - 8 * half
                up = jnp.where(here, roll(plane, 16 * (c - 8 * half) - (NZ - 16)), up)
                down = jnp.where(here, roll(plane, 16 * (c - 8 * half)), down)
            at = EY * fields + ER * (2 * f + half)
            up_ref[at : at + ER] = up
            down_ref[at : at + ER] = down


def spread_fine(k, f, before, after):
    lane = lanes((EY, NZ))
    right = roll(after[EY * f : EY * (f + 1)], -4 * k)
    left = roll(before[EY * f : EY * (f + 1)], NZ - 4 - 4 * k)
    return jnp.where(lane < 4, right, jnp.where(lane >= NZ - 4, left, 0.0))


def spread_coarse(c, f, fields, before, after):
    lane = lanes((ER, NZ))
    at, place = EY * fields + ER * (2 * f + c // 8), 16 * (c % 8)
    right = roll(after[at : at + ER], -place)
    left = roll(before[at : at + ER], NZ - 16 - place)
    return jnp.where(lane < 16, right, jnp.where(lane >= NZ - 16, left, 0.0))


def crossed(block, beyond, step):
    lane = lanes(block.shape)
    below, below_beyond = roll(block, step), roll(beyond, step)
    above, above_beyond = roll(block, -step), roll(beyond, -step)
    low, high = lane < step, lane >= NZ - step
    return (
        jnp.where(low, below_beyond, below) + jnp.where(high, above_beyond, above),
        jnp.where(low, below, below_beyond) + jnp.where(high, above, above_beyond),
    )


PAD = 8


def neighbours(src, k, rows, step=1):
    at = PAD
    here = [src[part, k, at : at + rows] for part in range(2)]
    along = crossed(here[0], here[1], step)
    out = []
    for part in range(2):
        beside = src[part, k - 1, at : at + rows] + src[part, k + 1, at : at + rows]
        beside = beside + (src[part, k, at - 1 : at - 1 + rows] + src[part, k, at + 1 : at + 1 + rows])
        out.append(beside + along[part])
    return here, out


def expand(coarse, part, k, lo):
    c = (k - HF) // COARSEN + HC
    first = lax.broadcasted_iota(jnp.int32, (8, NZ), 0) < 4
    groups = []
    for j in range(EY // 8):
        row = PAD + 3 + 2 * j
        a = jnp.broadcast_to(coarse[part, c, row : row + 1], (8, NZ))
        b = jnp.broadcast_to(coarse[part, c, row + 1 : row + 2], (8, NZ))
        groups.append(jnp.where(first, a, b))
    return jnp.concatenate(groups, axis=0)


def precondition(rhs, weight, crhs, cweight, fa, fb, ca, cb):
    for ref, rows in ((fa, EY), (fb, EY), (ca, ER), (cb, ER)):
        for part in range(2):
            for k in range(ref.shape[1]):
                ref[part, k, 0:PAD] = jnp.zeros((PAD, NZ), F32)
                ref[part, k, PAD + rows :] = jnp.zeros((PAD, NZ), F32)
    for k in range(EC):
        for part in range(2):
            ca[part, k, PAD : PAD + ER] = cweight[part][k] * crhs[part][k]
    src, dst = ca, cb
    for sweep in range(1, CSWEEPS):
        for k in range(sweep, EC - sweep):
            here, beside = neighbours(src, k, ER, COARSEN)
            for part in range(2):
                dst[part, k, PAD : PAD + ER] = keep * here[part] + cweight[part][k] * (crhs[part][k] + beside[part])
        src, dst = dst, src
    coarse = src
    for k in range(EX):
        for part in range(2):
            fa[part, k, PAD : PAD + EY] = weight[part][k] * rhs[part][k]
    src, dst = fa, fb
    for sweep in range(1, FSWEEPS):
        for k in range(sweep, EX - sweep):
            here, beside = neighbours(src, k, EY)
            for part in range(2):
                new = keep * here[part] + weight[part][k] * (rhs[part][k] + beside[part])
                if sweep == FSWEEPS - 1:
                    new = new + expand(coarse, part, k, 0)
                dst[part, k, PAD : PAD + EY] = new
        src, dst = dst, src


def image_plane(src, d_ref, i):
    k, at = i + HF, PAD + 4
    here = src[0, k, at : at + NY]
    beside = src[0, k - 1, at : at + NY] + src[0, k + 1, at : at + NY]
    beside = beside + (src[0, k, at - 1 : at - 1 + NY] + src[0, k, at + 1 : at + 1 + NY])
    along, _ = crossed(here, src[1, k, at : at + NY], 1)
    return here, (6.0 + d_ref[i]) * here - (beside + along)


def add_up(x):
    return (x[0:8] + x[8:16]) + (x[16:24] + x[24:32])


SHARE = NZ // 8


def store_sums(out_ref, totals, row=None):
    row = jnp.zeros((1, NZ), F32) if row is None else row
    for i, part in totals.items():
        part = jnp.sum(part, axis=0, keepdims=True)
        for step in (64, 32, 16):
            part = part + roll(part, step)
        row = jnp.where(lanes((1, NZ)) // SHARE == i, part, row)
    out_ref[...] = row


def first_kernel(
    b_ref, d_ref, b, v, g, vc, before, after, p_ref, q_ref, vh_ref, vch_ref, up_ref, down_ref, sum_ref,
    bh_ref, gh_ref, fa, fb, ca, cb, tmp,
):
    for k in range(EX):
        bh_ref[k] = spread_fine(k, 0, before, after)
        vh_ref[k] = spread_fine(k, 1, before, after)
    for c in range(EC):
        gh_ref[c] = spread_coarse(c, 0, 2, before, after)
        vch_ref[c] = spread_coarse(c, 1, 2, before, after)
    precondition((b, bh_ref), (v, vh_ref), (g, gh_ref), (vc, vch_ref), fa, fb, ca, cb)
    rp = jnp.zeros((8, NZ), F32)
    pq = jnp.zeros((8, NZ), F32)
    for i in range(NX):
        p, q = image_plane(fa, d_ref, i)
        p_ref[i] = p
        q_ref[i] = q
        rp = rp + add_up(b_ref[i] * p)
        pq = pq + add_up(p * q)
    store_sums(sum_ref, {0: rp, 1: pq})
    for c in range(CX):
        mean = block_sums([q_ref[COARSEN * c + k] for k in range(COARSEN)], tmp) * 0.25
        for ref in (up_ref, down_ref):
            ref[FACE + CY * c : FACE + CY * (c + 1)] = mean
    for k in range(HF):
        down_ref[NY * k : NY * (k + 1)] = q_ref[k]
        up_ref[NY * k : NY * (k + 1)] = q_ref[NX - HF + k]


def second_kernel(
    b_ref, d_ref, p_ref, q_ref, q, v, vh_ref, gq, vc, vch_ref, before, after, first_ref, m_ref, im_ref, sum_ref,
    qh_ref, gh_ref, fa, fb, ca, cb,
):
    for k in range(EX):
        qh_ref[k] = spread_fine(k, 0, before, after)
    for c in range(EC):
        gh_ref[c] = spread_coarse(c, 0, 1, before, after)
    precondition((q, qh_ref), (v, vh_ref), (gq, gh_ref), (vc, vch_ref), fa, fb, ca, cb)
    sums = [jnp.zeros((8, NZ), F32)] * 4
    for i in range(NX):
        m, im = image_plane(fa, d_ref, i)
        m_ref[i] = m
        im_ref[i] = im
        pairs = ((q_ref[i], m), (b_ref[i], m), (p_ref[i], im), (m, im))
        sums = [s + add_up(x * y) for s, (x, y) in zip(sums, pairs)]
    store_sums(sum_ref, dict(enumerate(sums, 2)), first_ref[...])


def last_kernel(b_ref, p_ref, q_ref, m_ref, im_ref, sum_ref, x_ref, r_ref):
    rp, pq, qm, rm, pim, mim = [
        jnp.sum(jnp.where(lanes((1, NZ)) // SHARE == i, sum_ref[...], 0.0), axis=1, keepdims=True) for i in range(6)
    ]
    alpha = rp / pq
    rho = rp - alpha * (pq + rm) + alpha * alpha * qm
    scale = 1.0 + rho / rp
    alpha_next = rho / (scale * scale * pq - scale * alpha * (pim + qm) + alpha * alpha * mim)
    along = alpha + alpha_next * scale
    across = alpha_next * alpha
    for i in range(NX):
        x_ref[i] = along * p_ref[i] - across * m_ref[i]
        r_ref[i] = b_ref[i] - along * q_ref[i] + across * im_ref[i]


def call(kernel, outs, scratch=(), name=None, space=pltpu.VMEM):
    def run(*args):
        return pl.pallas_call(
            kernel,
            out_shape=[jax.ShapeDtypeStruct(shape, F32) for shape in outs],
            in_specs=[pl.BlockSpec(memory_space=space)] * len(args),
            out_specs=[VMEM] * len(outs),
            scratch_shapes=[pltpu.VMEM(shape, F32) if isinstance(shape, tuple) else shape for shape in scratch],
            compiler_params=pltpu.CompilerParams(vmem_limit_bytes=24 * 2**20),
            name=name,
        )(*args)

    return run


def both_ways(up, down, axis):
    count = lax.axis_size(axis)
    steps = [(i, (i + 1) % count) for i in range(count if axis == "gx" else count - 1)]
    before = lax.ppermute(up, axis, steps)
    after = lax.ppermute(down, axis, [(j, i) for i, j in steps])
    return before, after


def total(x, axis):
    count = math.prod(lax.axis_size(name) for name in axis)
    spread = jnp.broadcast_to(x[None], (count,) + x.shape)
    return jnp.sum(lax.all_to_all(spread, axis, 0, 0, tiled=True), axis=0)


def exchange(own, up, down, fields):
    mine = up
    before, after = both_ways(up, down, "gx")
    height = EX + EC if fields == 2 else EX
    up, down = call(functools.partial(rows_kernel, fields), [(height, 8, NZ)] * 2, name="rows")(*own, mine, before, after)
    low, high = both_ways(up, down, "gy")
    message = (EY + 2 * ER) * fields
    arrays = call(
        functools.partial(lanes_kernel, fields),
        [(EX, EY, NZ)] * fields + [(EC, ER, NZ)] * fields + [(message, NZ)] * 2,
        name="lanes",
    )(*own, mine, before, after, low, high)
    return list(arrays[:-2]) + list(both_ways(arrays[-2], arrays[-1], "gz"))


def on_device(b, d):
    block, fine, coarse = (NX, NY, NZ), (EX, EY, NZ), (EC, ER, NZ)
    work = [(2, EX, EY + 2 * PAD, NZ)] * 2 + [(2, EC, ER + 2 * PAD, NZ)] * 2
    face = FACE + CX * CY
    b, d, v, up, down = call(
        start_kernel, [block] * 3 + [(2 * face, NZ)] * 2, [(NY, NZ), pltpu.SemaphoreType.DMA((2,))], name="start", space=pl.ANY
    )(b, d)
    be, ve, ge, vce, before, after = exchange((b, v), up, down, 2)
    p, q, vh, vch, up, down, sums = call(
        first_kernel,
        [block, block, fine, coarse, (face, NZ), (face, NZ), (1, NZ)],
        [fine, coarse] + work + [(NY, NZ)],
        name="first",
    )(b, d, be, ve, ge, vce, before, after)
    qe, gqe, before, after = exchange((q,), up, down, 1)
    m, im, sums = call(second_kernel, [block, block, (1, NZ)], [fine, coarse] + work, name="second")(
        b, d, p, q, qe, ve, vh, gqe, vce, vch, before, after, sums
    )
    for axis in (("gy", "gz"), ("gx",)):
        sums = total(sums, axis)
    return call(last_kernel, [block, block], name="last")(b, p, q, m, im, sums)


def solution(mesh):
    spec = P("gx", "gy", "gz")
    return jax.shard_map(on_device, mesh=mesh, in_specs=(spec, spec), out_specs=(spec, spec), check_vma=False)
```

```python
import functools
import math

import jax
import jax.numpy as jnp
from jax import lax
from jax.experimental import pallas as pl
from jax.experimental.pallas import tpu as pltpu
from jax.sharding import PartitionSpec as P

ITERS = 2
FSWEEPS = 3
CSWEEPS = 4
COARSEN = 4
damping = 2.0 / 3.0
keep = 1.0 - damping

NX, NY, NZ = 16, 32, 128
HF = 3
HC = 4
DEEP = 20
DEEPC = 32
CX, CY = NX // COARSEN, NY // COARSEN
EX = NX + 2 * HF
EY = 40
EC = CX + 2 * HC
ER = CY + 2 * HC
FACE = HF * NY
PER = NZ // DEEP
TILES = -(-EX // PER)
VMEM = pl.BlockSpec(memory_space=pltpu.VMEM)
F32 = jnp.float32


def lanes(shape):
    return lax.broadcasted_iota(jnp.int32, shape, len(shape) - 1)


def roll(x, shift, axis=-1):
    axis = axis % x.ndim
    return pltpu.roll(x, shift % x.shape[axis], axis)


def group_sum(x):
    lane = lanes(x.shape)
    x = x + jnp.where(lane % 2 == 0, roll(x, -1), roll(x, 1))
    return x + jnp.where(lane % 4 < 2, roll(x, -2), roll(x, 2))


def block_sums(planes, tmp):
    tmp[...] = group_sum(planes[0] + planes[1] + planes[2] + planes[3])
    rows = [tmp[pl.ds(k, CY, stride=COARSEN), :] for k in range(COARSEN)]
    return rows[0] + rows[1] + rows[2] + rows[3]


def merge(planes):
    lane = lanes(planes[0].shape)
    out = planes[0]
    for c in range(1, 4):
        out = jnp.where(lane % 4 == c, planes[c], out)
    return out


def unmerge(tile, c):
    return group_sum(jnp.where(lanes(tile.shape) % 4 == c, tile, 0.0))


def edges(x, width):
    lane = lanes(x.shape)
    return jnp.where((lane < width) | (lane >= NZ - width), x, 0.0)


def inside():
    at = lax.axis_index("gx")
    return at > 0, at < lax.axis_size("gx") - 1


def layer(k, f, own, before, after):
    if HF <= k < HF + NX:
        return own[f][k - HF]
    ref, ok, k = (before, inside()[0], k) if k < HF else (after, inside()[1], k - HF - NX)
    return jnp.where(ok, ref[FACE * f + NY * k : FACE * f + NY * (k + 1)], 0.0)


def tile_of(group, at, mine, before, after):
    tile = (before, mine, after)[group][at : at + CY]
    return tile if group == 1 else jnp.where(inside()[group // 2], tile, 0.0)


def with_rows(tile, low, high):
    return jnp.concatenate([low[CY - HC :], tile, high[:HC]], axis=0)


def start_kernel(b_ref, d_ref, v_ref, up_ref, down_ref, tmp):
    for i in range(NX):
        v_ref[i] = damping / (6.0 + d_ref[i])
    g, vc = [], []
    for c in range(CX):
        g.append(block_sums([b_ref[COARSEN * c + k] for k in range(COARSEN)], tmp) * 0.25)
        cd = 6.0 + block_sums([d_ref[COARSEN * c + k] for k in range(COARSEN)], tmp) * 0.25
        vc.append(damping / cd)
    for ref in (up_ref, down_ref):
        for f, planes in enumerate((g, vc)):
            ref[2 * FACE + CY * f : 2 * FACE + CY * (f + 1)] = merge(planes)
    for k in range(HF):
        for f, ref in enumerate((b_ref, v_ref)):
            down_ref[FACE * f + NY * k : FACE * f + NY * (k + 1)] = ref[k]
            up_ref[FACE * f + NY * k : FACE * f + NY * (k + 1)] = ref[NX - HF + k]


def rows_kernel(b, v, mine, before, after, up_ref, down_ref):
    for k in range(EX):
        for f in range(2):
            plane = layer(k, f, (b, v), before, after)
            down_ref[k, HF * f : HF * (f + 1)] = plane[:HF]
            up_ref[k, HF * f : HF * (f + 1)] = plane[NY - HF :]
    for f in range(2):
        for group in range(3):
            tile = tile_of(group, 2 * FACE + CY * f, mine, before, after)
            down_ref[EX + 3 * f + group] = tile
            up_ref[EX + 3 * f + group] = tile


def lanes_kernel(b, v, mine, before, after, low, high, be, ve, ge, vce, up_ref, down_ref):
    lane = lanes((EY, NZ))
    for f, out in enumerate((be, ve)):
        for tile in range(TILES):
            up = jnp.zeros((EY, NZ), F32)
            down = jnp.zeros((EY, NZ), F32)
            for k in range(PER * tile, min(EX, PER * (tile + 1))):
                out[k, 0:8] = jnp.zeros((8, NZ), F32)
                out[k, EY - 8 : EY] = jnp.zeros((8, NZ), F32)
                out[k, 4 - HF : 4] = low[k, HF * f : HF * (f + 1)]
                out[k, 4 : 4 + NY] = layer(k, f, (b, v), before, after)
                out[k, 4 + NY : 4 + NY + HF] = high[k, HF * f : HF * (f + 1)]
                plane, place = out[k], DEEP * (k % PER)
                here = (lane >= place) & (lane < place + DEEP)
                up = jnp.where(here, roll(plane, place - (NZ - DEEP)), up)
                down = jnp.where(here, roll(plane, place), down)
            at = EY * (TILES * f + tile)
            up_ref[at : at + EY] = up
            down_ref[at : at + EY] = down
    lane = lanes((ER, NZ))
    for f, out in enumerate((ge, vce)):
        up = jnp.zeros((ER, NZ), F32)
        down = jnp.zeros((ER, NZ), F32)
        for group in range(3):
            at = EX + 3 * f + group
            tile = with_rows(tile_of(group, 2 * FACE + CY * f, mine, before, after), low[at], high[at])
            out[group] = tile
            here = lane // DEEPC == group
            up = jnp.where(here, roll(tile, DEEPC * (group + 1) - NZ), up)
            down = jnp.where(here, roll(tile, DEEPC * group), down)
        at = 2 * EY * TILES + ER * f
        up_ref[at : at + ER] = up
        down_ref[at : at + ER] = down


def beyond_fine(k, f, before, after):
    lane = lanes((EY, NZ))
    at, place = EY * (TILES * f + k // PER), DEEP * (k % PER)
    right = roll(after[at : at + EY], -place)
    left = roll(before[at : at + EY], NZ - DEEP - place)
    return jnp.where(lane < DEEP, right, jnp.where(lane >= NZ - DEEP, left, 0.0))


def beyond_coarse(group, f, before, after):
    lane = lanes((ER, NZ))
    at = 2 * EY * TILES + ER * f
    right = roll(after[at : at + ER], -DEEPC * group)
    left = roll(before[at : at + ER], NZ - DEEPC * (group + 1))
    return jnp.where(lane < DEEPC, right, jnp.where(lane >= NZ - DEEPC, left, 0.0))


def crossed(block, beyond, step):
    lane = lanes(block.shape)
    below, below_beyond = roll(block, step), roll(beyond, step)
    above, above_beyond = roll(block, -step), roll(beyond, -step)
    low, high = lane < step, lane >= NZ - step
    return (
        jnp.where(low, below_beyond, below) + jnp.where(high, above_beyond, above),
        jnp.where(low, below, below_beyond) + jnp.where(high, above, above_beyond),
    )


PAD = 8


def neighbours(src, k, rows, step=1):
    at = PAD
    here = [src[part, k, at : at + rows] for part in range(2)]
    along = crossed(here[0], here[1], step)
    out = []
    for part in range(2):
        beside = src[part, k - 1, at : at + rows] + src[part, k + 1, at : at + rows]
        beside = beside + (src[part, k, at - 1 : at - 1 + rows] + src[part, k, at + 1 : at + 1 + rows])
        out.append(beside + along[part])
    return here, out


def expand(coarse, part, k, lo):
    c = (k - HF) // COARSEN + HC
    first = lax.broadcasted_iota(jnp.int32, (8, NZ), 0) < 4
    groups = []
    for j in range(EY // 8):
        row = PAD + 3 + 2 * j
        a = jnp.broadcast_to(coarse[part, c, row : row + 1], (8, NZ))
        b = jnp.broadcast_to(coarse[part, c, row + 1 : row + 2], (8, NZ))
        groups.append(jnp.where(first, a, b))
    return jnp.concatenate(groups, axis=0)


def precondition(rhs, weight, crhs, cweight, fa, fb, ca, cb):
    for ref, rows in ((fa, EY), (fb, EY), (ca, ER), (cb, ER)):
        for part in range(2):
            for k in range(ref.shape[1]):
                ref[part, k, 0:PAD] = jnp.zeros((PAD, NZ), F32)
                ref[part, k, PAD + rows :] = jnp.zeros((PAD, NZ), F32)
    for k in range(EC):
        for part in range(2):
            ca[part, k, PAD : PAD + ER] = cweight[part, k] * crhs[part, k]
    src, dst = ca, cb
    for sweep in range(1, CSWEEPS):
        for k in range(sweep, EC - sweep):
            here, beside = neighbours(src, k, ER, COARSEN)
            for part in range(2):
                dst[part, k, PAD : PAD + ER] = keep * here[part] + cweight[part, k] * (crhs[part, k] + beside[part])
        src, dst = dst, src
    coarse = src
    for k in range(EX):
        for part in range(2):
            fa[part, k, PAD : PAD + EY] = weight[part][k] * rhs[part][k]
    src, dst = fa, fb
    for sweep in range(1, FSWEEPS):
        for k in range(sweep, EX - sweep):
            here, beside = neighbours(src, k, EY)
            for part in range(2):
                new = keep * here[part] + weight[part][k] * (rhs[part][k] + beside[part])
                if sweep == FSWEEPS - 1:
                    new = new + expand(coarse, part, k, 0)
                dst[part, k, PAD : PAD + EY] = new
        src, dst = dst, src


def image_plane(src, i):
    k, at = i + HF, PAD + 4
    here = [src[part, k, at : at + NY] for part in range(2)]
    along = crossed(here[0], here[1], 1)
    out = []
    for part in range(2):
        beside = src[part, k - 1, at : at + NY] + src[part, k + 1, at : at + NY]
        beside = beside + (src[part, k, at - 1 : at - 1 + NY] + src[part, k, at + 1 : at + 1 + NY])
        out.append(beside + along[part])
    return here, out


def add_up(x):
    return (x[0:8] + x[8:16]) + (x[16:24] + x[24:32])


SHARE = NZ // 8


def store_sums(out_ref, totals, row=None):
    row = jnp.zeros((1, NZ), F32) if row is None else row
    for i, part in totals.items():
        part = jnp.sum(part, axis=0, keepdims=True)
        for step in (64, 32, 16):
            part = part + roll(part, step)
        row = jnp.where(lanes((1, NZ)) // SHARE == i, part, row)
    out_ref[...] = row


NEAR = 4
NEARC = 16


def first_kernel(
    b_ref, d_ref, b, v, gm, vcm, before, after, p_ref, q_ref, qh_ref, vh_ref, vcx_ref, up_ref, down_ref, sum_ref,
    bh, gx, fa, fb, ca, cb, tmp,
):
    for k in range(EX):
        bh[k] = beyond_fine(k, 0, before, after)
        vh_ref[k] = beyond_fine(k, 1, before, after)
    for f, (tiles, out) in enumerate(((gm, gx), (vcm, vcx_ref))):
        for group in range(3):
            for part, tile in enumerate((tiles[group], beyond_coarse(group, f, before, after))):
                for c in range(4):
                    out[part, 4 * group + c] = unmerge(tile, c)
    precondition((b, bh), (v, vh_ref), gx, vcx_ref, fa, fb, ca, cb)
    rp = jnp.zeros((8, NZ), F32)
    pq = jnp.zeros((8, NZ), F32)
    for i in range(NX):
        (p, ph), (beside, beside_h) = image_plane(fa, i)
        q = (6.0 + d_ref[i]) * p - beside
        weight = vh_ref[i + HF, 4 : 4 + NY]
        within = weight > 0.0
        p_ref[i] = p
        q_ref[i] = q
        qh_ref[i] = jnp.where(within, damping / jnp.where(within, weight, 1.0) * ph - beside_h, 0.0)
        rp = rp + add_up(b_ref[i] * p)
        pq = pq + add_up(p * q)
    store_sums(sum_ref, {0: rp, 1: pq})
    for part, field in enumerate((q_ref, qh_ref)):
        means = [
            block_sums([field[COARSEN * c + k] for k in range(COARSEN)], tmp) * 0.25 for c in range(CX)
        ]
        tile = merge(means)
        if part == 1:
            tile = roll(tile, NEARC)
        for ref in (up_ref, down_ref):
            ref[FACE + NY + CY * part : FACE + NY + CY * (part + 1)] = tile
    lane = lanes((NY, NZ))
    for ref, first in ((down_ref, 0), (up_ref, NX - HF)):
        packed = jnp.zeros((NY, NZ), F32)
        for k in range(HF):
            ref[NY * k : NY * (k + 1)] = q_ref[first + k]
            packed = jnp.where(lane // (2 * NEAR) == k, roll(qh_ref[first + k], NEAR + 2 * NEAR * k), packed)
        ref[FACE : FACE + NY] = packed


def layer_beyond(k, own, before, after):
    if HF <= k < HF + NX:
        return own[k - HF]
    ref, ok, k = (before, inside()[0], k) if k < HF else (after, inside()[1], k - HF - NX)
    return jnp.where(ok, edges(roll(ref[FACE : FACE + NY], -NEAR - 2 * NEAR * k), NEAR), 0.0)


SIDE = NZ // (2 * NEAR)
PAIRS = EX // 2


def second_rows_kernel(q, qh, mine, before, after, up_ref, down_ref):
    for k in range(EX):
        plane = layer(k, 0, (q,), before, after)
        row = HF * (k % 2)
        down_ref[k // 2, row : row + HF] = plane[:HF]
        up_ref[k // 2, row : row + HF] = plane[NY - HF :]
    lane = lanes((8, NZ))
    wide = jnp.zeros((8, NZ), F32)
    for group in range(3):
        tile = tile_of(group, FACE + NY, mine, before, after)
        beyond = tile_of(group, FACE + NY + CY, mine, before, after)
        wide = jnp.where(lane // (2 * NEARC) == group, roll(beyond, 2 * NEARC * group), wide)
        for ref in (up_ref, down_ref):
            ref[PAIRS + group] = tile
    for ref, rows in ((up_ref, slice(NY - 8, NY)), (down_ref, slice(0, 8))):
        ref[PAIRS + 5] = wide
        for half in range(2):
            packed = jnp.zeros((8, NZ), F32)
            for k in range(SIDE * half, min(EX, SIDE * (half + 1))):
                plane = layer_beyond(k, qh, before, after)[rows]
                packed = jnp.where(lane // (2 * NEAR) == k % SIDE, roll(plane, NEAR + 2 * NEAR * (k % SIDE)), packed)
            ref[PAIRS + 3 + half] = packed


def second_kernel(
    b_ref, d_ref, p_ref, q_ref, qh_ref, v, vh_ref, vcx_ref, mine, before, after, low, high, first_ref,
    m_ref, im_ref, sum_ref, q, qh, gx, fa, fb, ca, cb,
):
    for k in range(EX):
        row, place = HF * (k % 2), -NEAR - 2 * NEAR * (k % SIDE)
        for out in (q, qh):
            out[k, 0:8] = jnp.zeros((8, NZ), F32)
            out[k, EY - 8 : EY] = jnp.zeros((8, NZ), F32)
        q[k, 4 - HF : 4] = low[k // 2, row : row + HF]
        q[k, 4 : 4 + NY] = layer(k, 0, (q_ref,), before, after)
        q[k, 4 + NY : 4 + NY + HF] = high[k // 2, row : row + HF]
        tile = PAIRS + 3 + k // SIDE
        qh[k, 4 - HF : 4] = edges(roll(low[tile], place), NEAR)[8 - HF :]
        qh[k, 4 : 4 + NY] = layer_beyond(k, qh_ref, before, after)
        qh[k, 4 + NY : 4 + NY + HF] = edges(roll(high[tile], place), NEAR)[:HF]
    for group in range(3):
        at = FACE + NY
        tile = with_rows(tile_of(group, at, mine, before, after), low[PAIRS + group], high[PAIRS + group])
        wide = [roll(ref[PAIRS + 5], -2 * NEARC * group) for ref in (low, high)]
        beyond = with_rows(tile_of(group, at + CY, mine, before, after), *wide)
        for part, merged in enumerate((tile, edges(roll(beyond, -NEARC), NEARC))):
            for c in range(4):
                gx[part, 4 * group + c] = unmerge(merged, c)
    precondition((q, qh), (v, vh_ref), gx, vcx_ref, fa, fb, ca, cb)
    sums = [jnp.zeros((8, NZ), F32)] * 4
    for i in range(NX):
        (m, _), (beside, _) = image_plane(fa, i)
        im = (6.0 + d_ref[i]) * m - beside
        m_ref[i] = m
        im_ref[i] = im
        pairs = ((q_ref[i], m), (b_ref[i], m), (p_ref[i], im), (m, im))
        sums = [s + add_up(x * y) for s, (x, y) in zip(sums, pairs)]
    store_sums(sum_ref, dict(enumerate(sums, 2)), first_ref[...])


def last_kernel(b_ref, p_ref, q_ref, m_ref, im_ref, sum_ref, x_ref, r_ref):
    rp, pq, qm, rm, pim, mim = [
        jnp.sum(jnp.where(lanes((1, NZ)) // SHARE == i, sum_ref[...], 0.0), axis=1, keepdims=True) for i in range(6)
    ]
    alpha = rp / pq
    rho = rp - alpha * (pq + rm) + alpha * alpha * qm
    scale = 1.0 + rho / rp
    alpha_next = rho / (scale * scale * pq - scale * alpha * (pim + qm) + alpha * alpha * mim)
    along = alpha + alpha_next * scale
    across = alpha_next * alpha
    for i in range(NX):
        x_ref[i] = along * p_ref[i] - across * m_ref[i]
        r_ref[i] = b_ref[i] - along * q_ref[i] + across * im_ref[i]


def call(kernel, outs, scratch=(), name=None, space=pltpu.VMEM):
    def run(*args):
        return pl.pallas_call(
            kernel,
            out_shape=[jax.ShapeDtypeStruct(shape, F32) for shape in outs],
            in_specs=[pl.BlockSpec(memory_space=space)] * len(args),
            out_specs=[VMEM] * len(outs),
            scratch_shapes=[pltpu.VMEM(shape, F32) if isinstance(shape, tuple) else shape for shape in scratch],
            compiler_params=pltpu.CompilerParams(vmem_limit_bytes=24 * 2**20),
            name=name,
        )(*args)

    return run


def both_ways(up, down, axis):
    count = lax.axis_size(axis)
    steps = [(i, (i + 1) % count) for i in range(count if axis == "gx" else count - 1)]
    before = lax.ppermute(up, axis, steps)
    after = lax.ppermute(down, axis, [(j, i) for i, j in steps])
    return before, after


def total(x, axis):
    count = math.prod(lax.axis_size(name) for name in axis)
    spread = jnp.broadcast_to(x[None], (count,) + x.shape)
    return jnp.sum(lax.all_to_all(spread, axis, 0, 0, tiled=True), axis=0)


def on_device(b, d):
    block, fine, coarse = (NX, NY, NZ), (EX, EY, NZ), (2, EC, ER, NZ)
    work = [(2, EX, EY + 2 * PAD, NZ)] * 2 + [(2, EC, ER + 2 * PAD, NZ)] * 2
    v, up, down = call(start_kernel, [block] + [(2 * FACE + 2 * CY, NZ)] * 2, [(NY, NZ)], name="start")(b, d)
    mine = up
    before, after = both_ways(up, down, "gx")
    up, down = call(rows_kernel, [(EX + 6, 8, NZ)] * 2, name="rows")(b, v, mine, before, after)
    low, high = both_ways(up, down, "gy")
    be, ve, gm, vcm, up, down = call(
        lanes_kernel, [fine] * 2 + [(3, ER, NZ)] * 2 + [(2 * (EY * TILES + ER), NZ)] * 2, name="lanes"
    )(b, v, mine, before, after, low, high)
    before, after = both_ways(up, down, "gz")
    p, q, qh, vh, vcx, up, down, sums = call(
        first_kernel,
        [block] * 3 + [fine, coarse] + [(FACE + NY + 2 * CY, NZ)] * 2 + [(1, NZ)],
        [fine, coarse] + work + [(NY, NZ)],
        name="first",
    )(b, d, be, ve, gm, vcm, before, after)
    mine = up
    before, after = both_ways(up, down, "gx")
    up, down = call(second_rows_kernel, [(PAIRS + 6, 8, NZ)] * 2, name="second_rows")(q, qh, mine, before, after)
    low, high = both_ways(up, down, "gy")
    m, im, sums = call(second_kernel, [block, block, (1, NZ)], [fine, fine, coarse] + work, name="second")(
        b, d, p, q, qh, ve, vh, vcx, mine, before, after, low, high, sums
    )
    for axis in (("gy", "gz"), ("gx",)):
        sums = total(sums, axis)
    return call(last_kernel, [block, block], name="last")(b, p, q, m, im, sums)


def solution(mesh):
    spec = P("gx", "gy", "gz")
    return jax.shard_map(on_device, mesh=mesh, in_specs=(spec, spec), out_specs=(spec, spec), check_vma=False)
```

```python
import functools
import math

import jax
import jax.numpy as jnp
from jax import lax
from jax.experimental import pallas as pl
from jax.experimental.pallas import tpu as pltpu
from jax.sharding import PartitionSpec as P

ITERS = 2
FSWEEPS = 3
CSWEEPS = 4
COARSEN = 4
damping = 2.0 / 3.0
keep = 1.0 - damping

NX, NY, NZ = 16, 32, 128
HF = 3
HC = 4
DEEP = 20
DEEPC = 32
CX, CY = NX // COARSEN, NY // COARSEN
EX = NX + 2 * HF
EY = 40
EC = CX + 2 * HC
ER = CY + 2 * HC
FACE = HF * NY
PER = NZ // DEEP
TILES = -(-EX // PER)
VMEM = pl.BlockSpec(memory_space=pltpu.VMEM)
F32 = jnp.float32


def lanes(shape):
    return lax.broadcasted_iota(jnp.int32, shape, len(shape) - 1)


def roll(x, shift, axis=-1):
    axis = axis % x.ndim
    return pltpu.roll(x, shift % x.shape[axis], axis)


def group_sum(x):
    lane = lanes(x.shape)
    x = x + jnp.where(lane % 2 == 0, roll(x, -1), roll(x, 1))
    return x + jnp.where(lane % 4 < 2, roll(x, -2), roll(x, 2))


def block_sums(planes, tmp):
    tmp[...] = group_sum(planes[0] + planes[1] + planes[2] + planes[3])
    rows = [tmp[pl.ds(k, CY, stride=COARSEN), :] for k in range(COARSEN)]
    return rows[0] + rows[1] + rows[2] + rows[3]


def merge(planes):
    lane = lanes(planes[0].shape)
    out = planes[0]
    for c in range(1, 4):
        out = jnp.where(lane % 4 == c, planes[c], out)
    return out


def unmerge(tile):
    lane = lanes(tile.shape) % 4
    moved = {step: roll(tile, -step) if step else tile for step in range(-3, 4)}
    planes = []
    for c in range(4):
        out = moved[c]
        for at in range(1, 4):
            out = jnp.where(lane == at, moved[c - at], out)
        planes.append(out)
    return planes


def edges(x, width):
    lane = lanes(x.shape)
    return jnp.where((lane < width) | (lane >= NZ - width), x, 0.0)


def inside():
    at = lax.axis_index("gx")
    return at > 0, at < lax.axis_size("gx") - 1


def layer(k, f, own, before, after):
    if HF <= k < HF + NX:
        return own[f][k - HF]
    ref, ok, k = (before, inside()[0], k) if k < HF else (after, inside()[1], k - HF - NX)
    return jnp.where(ok, ref[FACE * f + NY * k : FACE * f + NY * (k + 1)], 0.0)


def tile_of(group, at, mine, before, after):
    tile = (before, mine, after)[group][at : at + CY]
    return tile if group == 1 else jnp.where(inside()[group // 2], tile, 0.0)


def with_rows(tile, low, high):
    return jnp.concatenate([low[CY - HC :], tile, high[:HC]], axis=0)


def start_kernel(bd_ref, v_ref, up_ref, down_ref, tmp):
    b_ref, d_ref = bd_ref.at[0], bd_ref.at[1]
    for i in range(NX):
        v_ref[i] = damping / (6.0 + d_ref[i])
    g, vc = [], []
    for c in range(CX):
        g.append(block_sums([b_ref[COARSEN * c + k] for k in range(COARSEN)], tmp) * 0.25)
        cd = 6.0 + block_sums([d_ref[COARSEN * c + k] for k in range(COARSEN)], tmp) * 0.25
        vc.append(damping / cd)
    for ref in (up_ref, down_ref):
        for f, planes in enumerate((g, vc)):
            ref[2 * FACE + CY * f : 2 * FACE + CY * (f + 1)] = merge(planes)
    for k in range(HF):
        for f, ref in enumerate((b_ref, v_ref)):
            down_ref[FACE * f + NY * k : FACE * f + NY * (k + 1)] = ref[k]
            up_ref[FACE * f + NY * k : FACE * f + NY * (k + 1)] = ref[NX - HF + k]


def rows_kernel(b, v, mine, before, after, up_ref, down_ref):
    for k in range(1, EX - 1):
        for f in range(2):
            plane = layer(k, f, (b, v), before, after)
            down_ref[k - 1, HF * f : HF * (f + 1)] = plane[:HF]
            up_ref[k - 1, HF * f : HF * (f + 1)] = plane[NY - HF :]
    for f in range(2):
        for group in range(3):
            tile = tile_of(group, 2 * FACE + CY * f, mine, before, after)
            down_ref[EX - 2 + 3 * f + group] = tile
            up_ref[EX - 2 + 3 * f + group] = tile


def slots(lane, width, place):
    first = (lane >= width * place) & (lane < width * (place + 1))
    last = lane >= NZ - width if place == 0 else (lane >= width * (place - 1)) & (lane < width * place)
    return first, last


def unpack(before, after, width, place):
    lane = lanes(after.shape)
    both = jnp.where(slots(lane, width, place)[0], after, before)
    return edges(roll(both, -width * place), width)


def lanes_kernel(b, v, mine, before, after, low, high, be, ve, ge, vce, up_ref, down_ref):
    lane = lanes((EY, NZ))
    for f, out in enumerate((be, ve)):
        for tile in range(TILES):
            up = jnp.zeros((EY, NZ), F32)
            down = jnp.zeros((EY, NZ), F32)
            for k in range(PER * tile, min(EX, PER * (tile + 1))):
                out[k, 0:8] = jnp.zeros((8, NZ), F32)
                out[k, EY - 8 : EY] = jnp.zeros((8, NZ), F32)
                out[k, 4 : 4 + NY] = layer(k, f, (b, v), before, after)
                if 0 < k < EX - 1:
                    out[k, 4 - HF : 4] = low[k - 1, HF * f : HF * (f + 1)]
                    out[k, 4 + NY : 4 + NY + HF] = high[k - 1, HF * f : HF * (f + 1)]
                moved = roll(out[k], DEEP * (k % PER))
                first, last = slots(lane, DEEP, k % PER)
                up = jnp.where(last, moved, up)
                down = jnp.where(first, moved, down)
            at = EY * (TILES * f + tile)
            up_ref[at : at + EY] = up
            down_ref[at : at + EY] = down
    lane = lanes((ER, NZ))
    for f, out in enumerate((ge, vce)):
        up = jnp.zeros((ER, NZ), F32)
        down = jnp.zeros((ER, NZ), F32)
        for group in range(3):
            at = EX - 2 + 3 * f + group
            tile = with_rows(tile_of(group, 2 * FACE + CY * f, mine, before, after), low[at], high[at])
            out[group] = tile
            moved = roll(tile, DEEPC * group)
            first, last = slots(lane, DEEPC, group)
            up = jnp.where(last, moved, up)
            down = jnp.where(first, moved, down)
        at = 2 * EY * TILES + ER * f
        up_ref[at : at + ER] = up
        down_ref[at : at + ER] = down


def beyond_fine(k, f, before, after):
    at = EY * (TILES * f + k // PER)
    return unpack(before[at : at + EY], after[at : at + EY], DEEP, k % PER)


def beyond_coarse(group, f, before, after):
    at = 2 * EY * TILES + ER * f
    return unpack(before[at : at + ER], after[at : at + ER], DEEPC, group)


def crossed(block, beyond, step):
    lane = lanes(block.shape)
    below, below_beyond = roll(block, step), roll(beyond, step)
    above, above_beyond = roll(block, -step), roll(beyond, -step)
    low, high = lane < step, lane >= NZ - step
    return (
        jnp.where(low, below_beyond, below) + jnp.where(high, above_beyond, above),
        jnp.where(low, below, below_beyond) + jnp.where(high, above, above_beyond),
    )


PAD = 8


def neighbours(src, k, rows, step=1):
    at = PAD
    here = [src[part, k, at : at + rows] for part in range(2)]
    along = crossed(here[0], here[1], step)
    out = []
    for part in range(2):
        beside = src[part, k - 1, at : at + rows] + src[part, k + 1, at : at + rows]
        beside = beside + (src[part, k, at - 1 : at - 1 + rows] + src[part, k, at + 1 : at + 1 + rows])
        out.append(beside + along[part])
    return here, out


def expand(coarse, part, k, lo):
    c = (k - HF) // COARSEN + HC
    first = lax.broadcasted_iota(jnp.int32, (8, NZ), 0) < 4
    groups = []
    for j in range(EY // 8):
        row = PAD + 3 + 2 * j
        a = jnp.broadcast_to(coarse[part, c, row : row + 1], (8, NZ))
        b = jnp.broadcast_to(coarse[part, c, row + 1 : row + 2], (8, NZ))
        groups.append(jnp.where(first, a, b))
    return jnp.concatenate(groups, axis=0)


def precondition(rhs, weight, crhs, cweight, fa, fb, ca, cb):
    for ref, rows in ((fa, EY), (fb, EY), (ca, ER), (cb, ER)):
        for part in range(2):
            for k in range(ref.shape[1]):
                ref[part, k, 0:PAD] = jnp.zeros((PAD, NZ), F32)
                ref[part, k, PAD + rows :] = jnp.zeros((PAD, NZ), F32)
    for k in range(EC):
        for part in range(2):
            ca[part, k, PAD : PAD + ER] = cweight[part, k] * crhs[part, k]
    src, dst = ca, cb
    for sweep in range(1, CSWEEPS):
        for k in range(sweep, EC - sweep):
            here, beside = neighbours(src, k, ER, COARSEN)
            for part in range(2):
                dst[part, k, PAD : PAD + ER] = keep * here[part] + cweight[part, k] * (crhs[part, k] + beside[part])
        src, dst = dst, src
    coarse = src
    for k in range(EX):
        for part in range(2):
            fa[part, k, PAD : PAD + EY] = weight[part][k] * rhs[part][k]
    src, dst = fa, fb
    for sweep in range(1, FSWEEPS):
        for k in range(sweep, EX - sweep):
            here, beside = neighbours(src, k, EY)
            for part in range(2):
                new = keep * here[part] + weight[part][k] * (rhs[part][k] + beside[part])
                if sweep == FSWEEPS - 1:
                    new = new + expand(coarse, part, k, 0)
                dst[part, k, PAD : PAD + EY] = new
        src, dst = dst, src


def image_plane(src, i):
    k, at = i + HF, PAD + 4
    here = [src[part, k, at : at + NY] for part in range(2)]
    along = crossed(here[0], here[1], 1)
    out = []
    for part in range(2):
        beside = src[part, k - 1, at : at + NY] + src[part, k + 1, at : at + NY]
        beside = beside + (src[part, k, at - 1 : at - 1 + NY] + src[part, k, at + 1 : at + 1 + NY])
        out.append(beside + along[part])
    return here, out


def add_up(x):
    return (x[0:8] + x[8:16]) + (x[16:24] + x[24:32])


SHARE = NZ // 8


def store_sums(out_ref, totals, row=None):
    row = jnp.zeros((1, NZ), F32) if row is None else row
    for i, part in totals.items():
        part = jnp.sum(part, axis=0, keepdims=True)
        for step in (64, 32, 16):
            part = part + roll(part, step)
        row = jnp.where(lanes((1, NZ)) // SHARE == i, part, row)
    out_ref[...] = row


NEAR = 4
NEARC = 16


def first_kernel(
    b_ref, d_ref, b, v, gm, vcm, before, after, p_ref, q_ref, qh_ref, vh_ref, vcx_ref, up_ref, down_ref, sum_ref,
    bh, gx, fa, fb, ca, cb, tmp,
):
    for k in range(EX):
        bh[k] = beyond_fine(k, 0, before, after)
        vh_ref[k] = beyond_fine(k, 1, before, after)
    for f, (tiles, out) in enumerate(((gm, gx), (vcm, vcx_ref))):
        for group in range(3):
            for part, tile in enumerate((tiles[group], beyond_coarse(group, f, before, after))):
                for c, plane in enumerate(unmerge(tile)):
                    out[part, 4 * group + c] = plane
    precondition((b, bh), (v, vh_ref), gx, vcx_ref, fa, fb, ca, cb)
    rp = jnp.zeros((8, NZ), F32)
    pq = jnp.zeros((8, NZ), F32)
    for i in range(NX):
        (p, ph), (beside, beside_h) = image_plane(fa, i)
        q = (6.0 + d_ref[i]) * p - beside
        weight = vh_ref[i + HF, 4 : 4 + NY]
        within = weight > 0.0
        p_ref[i] = p
        q_ref[i] = q
        qh_ref[i] = jnp.where(within, damping / jnp.where(within, weight, 1.0) * ph - beside_h, 0.0)
        rp = rp + add_up(b_ref[i] * p)
        pq = pq + add_up(p * q)
    store_sums(sum_ref, {0: rp, 1: pq})
    for part, field in enumerate((q_ref, qh_ref)):
        means = [
            block_sums([field[COARSEN * c + k] for k in range(COARSEN)], tmp) * 0.25 for c in range(CX)
        ]
        tile = merge(means)
        if part == 1:
            tile = roll(tile, NEARC)
        for ref in (up_ref, down_ref):
            ref[FACE + NY + CY * part : FACE + NY + CY * (part + 1)] = tile
    lane = lanes((NY, NZ))
    for ref, first in ((down_ref, 0), (up_ref, NX - HF)):
        packed = jnp.zeros((NY, NZ), F32)
        for k in range(HF):
            ref[NY * k : NY * (k + 1)] = q_ref[first + k]
            packed = jnp.where(lane // (2 * NEAR) == k, roll(qh_ref[first + k], NEAR + 2 * NEAR * k), packed)
        ref[FACE : FACE + NY] = packed


def layer_beyond(k, own, before, after):
    if HF <= k < HF + NX:
        return own[k - HF]
    ref, ok, k = (before, inside()[0], k) if k < HF else (after, inside()[1], k - HF - NX)
    return jnp.where(ok, edges(roll(ref[FACE : FACE + NY], -NEAR - 2 * NEAR * k), NEAR), 0.0)


SIDE = NZ // (2 * NEAR)
PAIRS = EX // 2 - 1


def second_rows_kernel(q, qh, mine, before, after, up_ref, down_ref):
    for k in range(1, EX - 1):
        plane = layer(k, 0, (q,), before, after)
        at, row = (k - 1) // 2, HF * ((k - 1) % 2)
        down_ref[at, row : row + HF] = plane[:HF]
        up_ref[at, row : row + HF] = plane[NY - HF :]
    lane = lanes((8, NZ))
    wide = jnp.zeros((8, NZ), F32)
    for group in range(3):
        tile = tile_of(group, FACE + NY, mine, before, after)
        beyond = tile_of(group, FACE + NY + CY, mine, before, after)
        wide = jnp.where(lane // (2 * NEARC) == group, roll(beyond, 2 * NEARC * group), wide)
        for ref in (up_ref, down_ref):
            ref[PAIRS + group] = tile
    for ref, rows in ((up_ref, slice(NY - 8, NY)), (down_ref, slice(0, 8))):
        ref[PAIRS + 5] = wide
        for half in range(2):
            packed = jnp.zeros((8, NZ), F32)
            for k in range(SIDE * half, min(EX, SIDE * (half + 1))):
                plane = layer_beyond(k, qh, before, after)[rows]
                packed = jnp.where(lane // (2 * NEAR) == k % SIDE, roll(plane, NEAR + 2 * NEAR * (k % SIDE)), packed)
            ref[PAIRS + 3 + half] = packed


def second_kernel(
    b_ref, d_ref, p_ref, q_ref, qh_ref, v, vh_ref, vcx_ref, mine, before, after, low, high, first_ref,
    m_ref, im_ref, sum_ref, q, qh, gx, fa, fb, ca, cb,
):
    for k in range(EX):
        at, row, place = (k - 1) // 2, HF * ((k - 1) % 2), -NEAR - 2 * NEAR * (k % SIDE)
        for out in (q, qh):
            out[k, 0:8] = jnp.zeros((8, NZ), F32)
            out[k, EY - 8 : EY] = jnp.zeros((8, NZ), F32)
        q[k, 4 : 4 + NY] = layer(k, 0, (q_ref,), before, after)
        if 0 < k < EX - 1:
            q[k, 4 - HF : 4] = low[at, row : row + HF]
            q[k, 4 + NY : 4 + NY + HF] = high[at, row : row + HF]
        tile = PAIRS + 3 + k // SIDE
        qh[k, 4 - HF : 4] = edges(roll(low[tile], place), NEAR)[8 - HF :]
        qh[k, 4 : 4 + NY] = layer_beyond(k, qh_ref, before, after)
        qh[k, 4 + NY : 4 + NY + HF] = edges(roll(high[tile], place), NEAR)[:HF]
    for group in range(3):
        at = FACE + NY
        tile = with_rows(tile_of(group, at, mine, before, after), low[PAIRS + group], high[PAIRS + group])
        wide = [roll(ref[PAIRS + 5], -2 * NEARC * group) for ref in (low, high)]
        beyond = with_rows(tile_of(group, at + CY, mine, before, after), *wide)
        for part, merged in enumerate((tile, edges(roll(beyond, -NEARC), NEARC))):
            for c, plane in enumerate(unmerge(merged)):
                gx[part, 4 * group + c] = plane
    precondition((q, qh), (v, vh_ref), gx, vcx_ref, fa, fb, ca, cb)
    sums = [jnp.zeros((8, NZ), F32)] * 4
    for i in range(NX):
        (m, _), (beside, _) = image_plane(fa, i)
        im = (6.0 + d_ref[i]) * m - beside
        m_ref[i] = m
        im_ref[i] = im
        pairs = ((q_ref[i], m), (b_ref[i], m), (p_ref[i], im), (m, im))
        sums = [s + add_up(x * y) for s, (x, y) in zip(sums, pairs)]
    store_sums(sum_ref, dict(enumerate(sums, 2)), first_ref[...])


PARTS = 4


def last_kernel(b_ref, p_ref, q_ref, m_ref, im_ref, sum_ref, x_out, r_out, x_ref, r_ref, sems):
    rp, pq, qm, rm, pim, mim = [
        jnp.sum(jnp.where(lanes((1, NZ)) // SHARE == i, sum_ref[...], 0.0), axis=1, keepdims=True) for i in range(6)
    ]
    alpha = rp / pq
    rho = rp - alpha * (pq + rm) + alpha * alpha * qm
    scale = 1.0 + rho / rp
    alpha_next = rho / (scale * scale * pq - scale * alpha * (pim + qm) + alpha * alpha * mim)
    along = alpha + alpha_next * scale
    across = alpha_next * alpha
    copies = []
    for part in range(PARTS):
        planes = range(NX // PARTS * part, NX // PARTS * (part + 1))
        for i in planes:
            x_ref[i] = along * p_ref[i] - across * m_ref[i]
            r_ref[i] = b_ref[i] - along * q_ref[i] + across * im_ref[i]
        at = pl.ds(planes[0], len(planes))
        for which, (src, dst) in enumerate(((x_ref, x_out), (r_ref, r_out))):
            copies.append(pltpu.make_async_copy(src.at[at], dst.at[at], sems.at[2 * part + which]))
            copies[-1].start()
    for copy in copies:
        copy.wait()


def call(kernel, outs, scratch=(), name=None, out_space=pltpu.VMEM):
    def run(*args):
        return pl.pallas_call(
            kernel,
            out_shape=[jax.ShapeDtypeStruct(shape, F32) for shape in outs],
            in_specs=[VMEM] * len(args),
            out_specs=[pl.BlockSpec(memory_space=out_space)] * len(outs),
            scratch_shapes=[pltpu.VMEM(shape, F32) if isinstance(shape, tuple) else shape for shape in scratch],
            compiler_params=pltpu.CompilerParams(vmem_limit_bytes=24 * 2**20),
            name=name,
        )(*args)

    return run


def both_ways(up, down, axis):
    count = lax.axis_size(axis)
    steps = [(i, (i + 1) % count) for i in range(count if axis == "gx" else count - 1)]
    before = lax.ppermute(up, axis, steps)
    after = lax.ppermute(down, axis, [(j, i) for i, j in steps])
    return before, after


def total(x, axis):
    count = math.prod(lax.axis_size(name) for name in axis)
    spread = jnp.broadcast_to(x[None], (count,) + x.shape)
    return jnp.sum(lax.all_to_all(spread, axis, 0, 0, tiled=True), axis=0)


def on_device(b, d):
    block, fine, coarse = (NX, NY, NZ), (EX, EY, NZ), (2, EC, ER, NZ)
    work = [(2, EX, EY + 2 * PAD, NZ)] * 2 + [(2, EC, ER + 2 * PAD, NZ)] * 2
    bd = lax.optimization_barrier(jnp.stack([b, d]))
    v, up, down = call(start_kernel, [block] + [(2 * FACE + 2 * CY, NZ)] * 2, [(NY, NZ)], name="start")(bd)
    mine = up
    before, after = both_ways(up, down, "gx")
    up, down = call(rows_kernel, [(EX + 4, 8, NZ)] * 2, name="rows")(b, v, mine, before, after)
    low, high = both_ways(up, down, "gy")
    be, ve, gm, vcm, up, down = call(
        lanes_kernel, [fine] * 2 + [(3, ER, NZ)] * 2 + [(2 * (EY * TILES + ER), NZ)] * 2, name="lanes"
    )(b, v, mine, before, after, low, high)
    before, after = both_ways(up, down, "gz")
    p, q, qh, vh, vcx, up, down, sums = call(
        first_kernel,
        [block] * 3 + [fine, coarse] + [(FACE + NY + 2 * CY, NZ)] * 2 + [(1, NZ)],
        [fine, coarse] + work + [(NY, NZ)],
        name="first",
    )(b, d, be, ve, gm, vcm, before, after)
    mine = up
    before, after = both_ways(up, down, "gx")
    up, down = call(second_rows_kernel, [(PAIRS + 6, 8, NZ)] * 2, name="second_rows")(q, qh, mine, before, after)
    low, high = both_ways(up, down, "gy")
    m, im, sums = call(second_kernel, [block, block, (1, NZ)], [fine, fine, coarse] + work, name="second")(
        b, d, p, q, qh, ve, vh, vcx, mine, before, after, low, high, sums
    )
    for axis in (("gy", "gz"), ("gx",)):
        sums = total(sums, axis)
    return call(
        last_kernel,
        [block, block],
        [block, block, pltpu.SemaphoreType.DMA((2 * PARTS,))],
        name="last",
        out_space=pl.ANY,
    )(b, p, q, m, im, sums)


def solution(mesh):
    spec = P("gx", "gy", "gz")
    return jax.shard_map(on_device, mesh=mesh, in_specs=(spec, spec), out_specs=(spec, spec), check_vma=False)
```

```python
import functools
import math

import jax
import jax.numpy as jnp
from jax import lax
from jax.experimental import pallas as pl
from jax.experimental.pallas import tpu as pltpu
from jax.sharding import PartitionSpec as P

ITERS = 2
FSWEEPS = 3
CSWEEPS = 4
COARSEN = 4
damping = 2.0 / 3.0
keep = 1.0 - damping

NX, NY, NZ = 16, 32, 128
HF = 3
HC = 4
DEEP = 20
DEEPC = 32
CX, CY = NX // COARSEN, NY // COARSEN
EX = NX + 2 * HF
EY = 40
EC = CX + 2 * HC
ER = CY + 2 * HC
FACE = HF * NY
PER = NZ // DEEP
TILES = -(-EX // PER)
VMEM = pl.BlockSpec(memory_space=pltpu.VMEM)
F32 = jnp.float32


def lanes(shape):
    return lax.broadcasted_iota(jnp.int32, shape, len(shape) - 1)


def roll(x, shift, axis=-1):
    axis = axis % x.ndim
    return pltpu.roll(x, shift % x.shape[axis], axis)


def group_sum(x):
    lane = lanes(x.shape)
    x = x + jnp.where(lane % 2 == 0, roll(x, -1), roll(x, 1))
    return x + jnp.where(lane % 4 < 2, roll(x, -2), roll(x, 2))


def block_sums(planes, tmp):
    tmp[...] = group_sum(planes[0] + planes[1] + planes[2] + planes[3])
    rows = [tmp[pl.ds(k, CY, stride=COARSEN), :] for k in range(COARSEN)]
    return rows[0] + rows[1] + rows[2] + rows[3]


def merge(planes):
    lane = lanes(planes[0].shape)
    out = planes[0]
    for c in range(1, 4):
        out = jnp.where(lane % 4 == c, planes[c], out)
    return out


def unmerge(tile):
    lane = lanes(tile.shape) % 4
    moved = {step: roll(tile, -step) if step else tile for step in range(-3, 4)}
    planes = []
    for c in range(4):
        out = moved[c]
        for at in range(1, 4):
            out = jnp.where(lane == at, moved[c - at], out)
        planes.append(out)
    return planes


def edges(x, width):
    lane = lanes(x.shape)
    return jnp.where((lane < width) | (lane >= NZ - width), x, 0.0)


def inside():
    at = lax.axis_index("gx")
    return at > 0, at < lax.axis_size("gx") - 1


def layer(k, f, own, before, after):
    if HF <= k < HF + NX:
        return own[f][k - HF]
    ref, ok, k = (before, inside()[0], k) if k < HF else (after, inside()[1], k - HF - NX)
    return jnp.where(ok, ref[FACE * f + NY * k : FACE * f + NY * (k + 1)], 0.0)


def tile_of(group, at, mine, before, after):
    tile = (before, mine, after)[group][at : at + CY]
    return tile if group == 1 else jnp.where(inside()[group // 2], tile, 0.0)


def with_rows(tile, low, high):
    return jnp.concatenate([low[CY - HC :], tile, high[:HC]], axis=0)


def start_kernel(bd_ref, v_ref, up_ref, down_ref, tmp):
    b_ref, d_ref = bd_ref.at[0], bd_ref.at[1]
    for i in range(NX):
        v_ref[i] = damping / (6.0 + d_ref[i])
    g, vc = [], []
    for c in range(CX):
        g.append(block_sums([b_ref[COARSEN * c + k] for k in range(COARSEN)], tmp) * 0.25)
        cd = 6.0 + block_sums([d_ref[COARSEN * c + k] for k in range(COARSEN)], tmp) * 0.25
        vc.append(damping / cd)
    for ref in (up_ref, down_ref):
        for f, planes in enumerate((g, vc)):
            ref[2 * FACE + CY * f : 2 * FACE + CY * (f + 1)] = merge(planes)
    for k in range(HF):
        for f, ref in enumerate((b_ref, v_ref)):
            down_ref[FACE * f + NY * k : FACE * f + NY * (k + 1)] = ref[k]
            up_ref[FACE * f + NY * k : FACE * f + NY * (k + 1)] = ref[NX - HF + k]


def rows_kernel(b, v, mine, before, after, up_ref, down_ref):
    for k in range(1, EX - 1):
        for f in range(2):
            plane = layer(k, f, (b, v), before, after)
            down_ref[k - 1, HF * f : HF * (f + 1)] = plane[:HF]
            up_ref[k - 1, HF * f : HF * (f + 1)] = plane[NY - HF :]
    for f in range(2):
        for group in range(3):
            tile = tile_of(group, 2 * FACE + CY * f, mine, before, after)
            down_ref[EX - 2 + 3 * f + group] = tile
            up_ref[EX - 2 + 3 * f + group] = tile


def slots(lane, width, place):
    first = (lane >= width * place) & (lane < width * (place + 1))
    last = lane >= NZ - width if place == 0 else (lane >= width * (place - 1)) & (lane < width * place)
    return first, last


def unpack(before, after, width, place):
    lane = lanes(after.shape)
    both = jnp.where(slots(lane, width, place)[0], after, before)
    return edges(roll(both, -width * place), width)


def lanes_kernel(b, v, mine, before, after, low, high, be, ve, ge, vce, up_ref, down_ref):
    lane = lanes((EY, NZ))
    for f, out in enumerate((be, ve)):
        for tile in range(TILES):
            up = jnp.zeros((EY, NZ), F32)
            down = jnp.zeros((EY, NZ), F32)
            for k in range(PER * tile, min(EX, PER * (tile + 1))):
                out[k, 0:8] = jnp.zeros((8, NZ), F32)
                out[k, EY - 8 : EY] = jnp.zeros((8, NZ), F32)
                out[k, 4 : 4 + NY] = layer(k, f, (b, v), before, after)
                if 0 < k < EX - 1:
                    out[k, 4 - HF : 4] = low[k - 1, HF * f : HF * (f + 1)]
                    out[k, 4 + NY : 4 + NY + HF] = high[k - 1, HF * f : HF * (f + 1)]
                moved = roll(out[k], DEEP * (k % PER))
                first, last = slots(lane, DEEP, k % PER)
                up = jnp.where(last, moved, up)
                down = jnp.where(first, moved, down)
            at = EY * (TILES * f + tile)
            up_ref[at : at + EY] = up
            down_ref[at : at + EY] = down
    lane = lanes((ER, NZ))
    for f, out in enumerate((ge, vce)):
        up = jnp.zeros((ER, NZ), F32)
        down = jnp.zeros((ER, NZ), F32)
        for group in range(3):
            at = EX - 2 + 3 * f + group
            tile = with_rows(tile_of(group, 2 * FACE + CY * f, mine, before, after), low[at], high[at])
            out[group] = tile
            moved = roll(tile, DEEPC * group)
            first, last = slots(lane, DEEPC, group)
            up = jnp.where(last, moved, up)
            down = jnp.where(first, moved, down)
        at = 2 * EY * TILES + ER * f
        up_ref[at : at + ER] = up
        down_ref[at : at + ER] = down


def beyond_fine(k, f, before, after):
    at = EY * (TILES * f + k // PER)
    return unpack(before[at : at + EY], after[at : at + EY], DEEP, k % PER)


def beyond_coarse(group, f, before, after):
    at = 2 * EY * TILES + ER * f
    return unpack(before[at : at + ER], after[at : at + ER], DEEPC, group)


def crossed(block, beyond, step):
    lane = lanes(block.shape)
    below, below_beyond = roll(block, step), roll(beyond, step)
    above, above_beyond = roll(block, -step), roll(beyond, -step)
    low, high = lane < step, lane >= NZ - step
    return (
        jnp.where(low, below_beyond, below) + jnp.where(high, above_beyond, above),
        jnp.where(low, below, below_beyond) + jnp.where(high, above, above_beyond),
    )


PAD = 8


def neighbours(src, k, rows, step=1):
    at = PAD
    here = [src[part, k, at : at + rows] for part in range(2)]
    along = crossed(here[0], here[1], step)
    out = []
    for part in range(2):
        beside = src[part, k - 1, at : at + rows] + src[part, k + 1, at : at + rows]
        beside = beside + (src[part, k, at - 1 : at - 1 + rows] + src[part, k, at + 1 : at + 1 + rows])
        out.append(beside + along[part])
    return here, out


def expand(coarse, part, k, lo):
    c = (k - HF) // COARSEN + HC
    first = lax.broadcasted_iota(jnp.int32, (8, NZ), 0) < 4
    groups = []
    for j in range(EY // 8):
        row = PAD + 3 + 2 * j
        a = jnp.broadcast_to(coarse[part, c, row : row + 1], (8, NZ))
        b = jnp.broadcast_to(coarse[part, c, row + 1 : row + 2], (8, NZ))
        groups.append(jnp.where(first, a, b))
    return jnp.concatenate(groups, axis=0)


def precondition(rhs, weight, crhs, cweight, fa, fb, ca, cb):
    for ref, rows in ((fa, EY), (fb, EY), (ca, ER), (cb, ER)):
        for part in range(2):
            for k in range(ref.shape[1]):
                ref[part, k, 0:PAD] = jnp.zeros((PAD, NZ), F32)
                ref[part, k, PAD + rows :] = jnp.zeros((PAD, NZ), F32)
    for k in range(EC):
        for part in range(2):
            ca[part, k, PAD : PAD + ER] = cweight[part, k] * crhs[part, k]
    src, dst = ca, cb
    for sweep in range(1, CSWEEPS):
        for k in range(sweep, EC - sweep):
            here, beside = neighbours(src, k, ER, COARSEN)
            for part in range(2):
                dst[part, k, PAD : PAD + ER] = keep * here[part] + cweight[part, k] * (crhs[part, k] + beside[part])
        src, dst = dst, src
    coarse = src
    for k in range(EX):
        for part in range(2):
            fa[part, k, PAD : PAD + EY] = weight[part][k] * rhs[part][k]
    src, dst = fa, fb
    for sweep in range(1, FSWEEPS):
        for k in range(sweep, EX - sweep):
            here, beside = neighbours(src, k, EY)
            for part in range(2):
                new = keep * here[part] + weight[part][k] * (rhs[part][k] + beside[part])
                if sweep == FSWEEPS - 1:
                    new = new + expand(coarse, part, k, 0)
                dst[part, k, PAD : PAD + EY] = new
        src, dst = dst, src


def image_plane(src, i):
    k, at = i + HF, PAD + 4
    here = [src[part, k, at : at + NY] for part in range(2)]
    along = crossed(here[0], here[1], 1)
    out = []
    for part in range(2):
        beside = src[part, k - 1, at : at + NY] + src[part, k + 1, at : at + NY]
        beside = beside + (src[part, k, at - 1 : at - 1 + NY] + src[part, k, at + 1 : at + 1 + NY])
        out.append(beside + along[part])
    return here, out


def add_up(x):
    return (x[0:8] + x[8:16]) + (x[16:24] + x[24:32])


SHARE = NZ // 8


def store_sums(out_ref, totals, row=None):
    row = jnp.zeros((1, NZ), F32) if row is None else row
    for i, part in totals.items():
        part = jnp.sum(part, axis=0, keepdims=True)
        for step in (64, 32, 16):
            part = part + roll(part, step)
        row = jnp.where(lanes((1, NZ)) // SHARE == i, part, row)
    out_ref[...] = row


NEAR = 4
NEARC = 16


def first_kernel(
    b_ref, d_ref, b, v, gm, vcm, before, after, p_ref, q_ref, qh_ref, vh_ref, vcx_ref, up_ref, down_ref, sum_ref,
    bh, gx, fa, fb, ca, cb, tmp,
):
    for k in range(EX):
        bh[k] = beyond_fine(k, 0, before, after)
        vh_ref[k] = beyond_fine(k, 1, before, after)
    for f, (tiles, out) in enumerate(((gm, gx), (vcm, vcx_ref))):
        for group in range(3):
            for part, tile in enumerate((tiles[group], beyond_coarse(group, f, before, after))):
                for c, plane in enumerate(unmerge(tile)):
                    out[part, 4 * group + c] = plane
    precondition((b, bh), (v, vh_ref), gx, vcx_ref, fa, fb, ca, cb)
    rp = jnp.zeros((8, NZ), F32)
    pq = jnp.zeros((8, NZ), F32)
    for i in range(NX):
        (p, ph), (beside, beside_h) = image_plane(fa, i)
        q = (6.0 + d_ref[i]) * p - beside
        weight = vh_ref[i + HF, 4 : 4 + NY]
        within = weight > 0.0
        p_ref[i] = p
        q_ref[i] = q
        qh_ref[i] = jnp.where(within, damping / jnp.where(within, weight, 1.0) * ph - beside_h, 0.0)
        rp = rp + add_up(b_ref[i] * p)
        pq = pq + add_up(p * q)
    store_sums(sum_ref, {0: rp, 1: pq})
    for part, field in enumerate((q_ref, qh_ref)):
        means = [
            block_sums([field[COARSEN * c + k] for k in range(COARSEN)], tmp) * 0.25 for c in range(CX)
        ]
        tile = merge(means)
        if part == 1:
            tile = roll(tile, NEARC)
        for ref in (up_ref, down_ref):
            ref[FACE + NY + CY * part : FACE + NY + CY * (part + 1)] = tile
    lane = lanes((NY, NZ))
    for ref, first in ((down_ref, 0), (up_ref, NX - HF)):
        packed = jnp.zeros((NY, NZ), F32)
        for k in range(HF):
            ref[NY * k : NY * (k + 1)] = q_ref[first + k]
            packed = jnp.where(lane // (2 * NEAR) == k, roll(qh_ref[first + k], NEAR + 2 * NEAR * k), packed)
        ref[FACE : FACE + NY] = packed


def layer_beyond(k, own, before, after):
    if HF <= k < HF + NX:
        return own[k - HF]
    ref, ok, k = (before, inside()[0], k) if k < HF else (after, inside()[1], k - HF - NX)
    return jnp.where(ok, edges(roll(ref[FACE : FACE + NY], -NEAR - 2 * NEAR * k), NEAR), 0.0)


SIDE = NZ // (2 * NEAR)
PAIRS = EX // 2 - 1


def second_rows_kernel(q, qh, mine, before, after, up_ref, down_ref):
    for k in range(1, EX - 1):
        plane = layer(k, 0, (q,), before, after)
        at, row = (k - 1) // 2, HF * ((k - 1) % 2)
        down_ref[at, row : row + HF] = plane[:HF]
        up_ref[at, row : row + HF] = plane[NY - HF :]
    lane = lanes((8, NZ))
    wide = jnp.zeros((8, NZ), F32)
    for group in range(3):
        tile = tile_of(group, FACE + NY, mine, before, after)
        beyond = tile_of(group, FACE + NY + CY, mine, before, after)
        wide = jnp.where(lane // (2 * NEARC) == group, roll(beyond, 2 * NEARC * group), wide)
        for ref in (up_ref, down_ref):
            ref[PAIRS + group] = tile
    for ref, rows in ((up_ref, slice(NY - 8, NY)), (down_ref, slice(0, 8))):
        ref[PAIRS + 5] = wide
        for half in range(2):
            packed = jnp.zeros((8, NZ), F32)
            for k in range(SIDE * half, min(EX, SIDE * (half + 1))):
                plane = layer_beyond(k, qh, before, after)[rows]
                packed = jnp.where(lane // (2 * NEAR) == k % SIDE, roll(plane, NEAR + 2 * NEAR * (k % SIDE)), packed)
            ref[PAIRS + 3 + half] = packed


def second_kernel(
    b_ref, d_ref, p_ref, q_ref, qh_ref, v, vh_ref, vcx_ref, mine, before, after, low, high, first_ref,
    m_ref, im_ref, sum_ref, q, qh, gx, fa, fb, ca, cb,
):
    for k in range(EX):
        at, row, place = (k - 1) // 2, HF * ((k - 1) % 2), -NEAR - 2 * NEAR * (k % SIDE)
        for out in (q, qh):
            out[k, 0:8] = jnp.zeros((8, NZ), F32)
            out[k, EY - 8 : EY] = jnp.zeros((8, NZ), F32)
        q[k, 4 : 4 + NY] = layer(k, 0, (q_ref,), before, after)
        if 0 < k < EX - 1:
            q[k, 4 - HF : 4] = low[at, row : row + HF]
            q[k, 4 + NY : 4 + NY + HF] = high[at, row : row + HF]
        tile = PAIRS + 3 + k // SIDE
        qh[k, 4 - HF : 4] = edges(roll(low[tile], place), NEAR)[8 - HF :]
        qh[k, 4 : 4 + NY] = layer_beyond(k, qh_ref, before, after)
        qh[k, 4 + NY : 4 + NY + HF] = edges(roll(high[tile], place), NEAR)[:HF]
    for group in range(3):
        at = FACE + NY
        tile = with_rows(tile_of(group, at, mine, before, after), low[PAIRS + group], high[PAIRS + group])
        wide = [roll(ref[PAIRS + 5], -2 * NEARC * group) for ref in (low, high)]
        beyond = with_rows(tile_of(group, at + CY, mine, before, after), *wide)
        for part, merged in enumerate((tile, edges(roll(beyond, -NEARC), NEARC))):
            for c, plane in enumerate(unmerge(merged)):
                gx[part, 4 * group + c] = plane
    precondition((q, qh), (v, vh_ref), gx, vcx_ref, fa, fb, ca, cb)
    sums = [jnp.zeros((8, NZ), F32)] * 4
    for i in range(NX):
        (m, _), (beside, _) = image_plane(fa, i)
        im = (6.0 + d_ref[i]) * m - beside
        m_ref[i] = m
        im_ref[i] = im
        pairs = ((q_ref[i], m), (b_ref[i], m), (p_ref[i], im), (m, im))
        sums = [s + add_up(x * y) for s, (x, y) in zip(sums, pairs)]
    store_sums(sum_ref, dict(enumerate(sums, 2)), first_ref[...])


PARTS = 4


def last_kernel(b_ref, p_ref, q_ref, m_ref, im_ref, sum_ref, x_out, r_out, x_ref, r_ref, sems):
    rp, pq, qm, rm, pim, mim = [
        jnp.sum(jnp.where(lanes((1, NZ)) // SHARE == i, sum_ref[...], 0.0), axis=1, keepdims=True) for i in range(6)
    ]
    alpha = rp / pq
    rho = rp - alpha * (pq + rm) + alpha * alpha * qm
    scale = 1.0 + rho / rp
    alpha_next = rho / (scale * scale * pq - scale * alpha * (pim + qm) + alpha * alpha * mim)
    along = alpha + alpha_next * scale
    across = alpha_next * alpha
    copies = []
    for part in range(PARTS):
        planes = range(NX // PARTS * part, NX // PARTS * (part + 1))
        for i in planes:
            x_ref[i] = along * p_ref[i] - across * m_ref[i]
            r_ref[i] = b_ref[i] - along * q_ref[i] + across * im_ref[i]
        at = pl.ds(planes[0], len(planes))
        for which, (src, dst) in enumerate(((x_ref, x_out), (r_ref, r_out))):
            copies.append(pltpu.make_async_copy(src.at[at], dst.at[at], sems.at[2 * part + which]))
            copies[-1].start()
    for copy in copies:
        copy.wait()


def call(kernel, outs, scratch=(), name=None, out_space=pltpu.VMEM):
    def run(*args):
        return pl.pallas_call(
            kernel,
            out_shape=[jax.ShapeDtypeStruct(shape, F32) for shape in outs],
            in_specs=[VMEM] * len(args),
            out_specs=[pl.BlockSpec(memory_space=out_space)] * len(outs),
            scratch_shapes=[pltpu.VMEM(shape, F32) if isinstance(shape, tuple) else shape for shape in scratch],
            compiler_params=pltpu.CompilerParams(vmem_limit_bytes=24 * 2**20),
            name=name,
        )(*args)

    return run


def both_ways(up, down, axis):
    count = lax.axis_size(axis)
    if axis == "gx":
        steps = [(i, (i + 1) % count) for i in range(count)]
        return lax.ppermute(up, axis, steps), lax.ppermute(down, axis, [(j, i) for i, j in steps])
    even = lax.axis_index(axis) % 2 == 0
    one = lax.ppermute(jnp.where(even, up, down), axis, [(i, i ^ 1) for i in range(count) if i ^ 1 < count])
    swaps = [(i, i + 1) for i in range(1, count - 1, 2)]
    two = lax.ppermute(jnp.where(even, down, up), axis, swaps + [(j, i) for i, j in swaps])
    return jnp.where(even, two, one), jnp.where(even, one, two)


def total(x, axis):
    count = math.prod(lax.axis_size(name) for name in axis)
    spread = jnp.broadcast_to(x[None], (count,) + x.shape)
    return jnp.sum(lax.all_to_all(spread, axis, 0, 0, tiled=True), axis=0)


def on_device(b, d):
    block, fine, coarse = (NX, NY, NZ), (EX, EY, NZ), (2, EC, ER, NZ)
    work = [(2, EX, EY + 2 * PAD, NZ)] * 2 + [(2, EC, ER + 2 * PAD, NZ)] * 2
    bd = lax.optimization_barrier(jnp.stack([b, d]))
    v, up, down = call(start_kernel, [block] + [(2 * FACE + 2 * CY, NZ)] * 2, [(NY, NZ)], name="start")(bd)
    mine = up
    before, after = both_ways(up, down, "gx")
    up, down = call(rows_kernel, [(EX + 4, 8, NZ)] * 2, name="rows")(b, v, mine, before, after)
    low, high = both_ways(up, down, "gy")
    be, ve, gm, vcm, up, down = call(
        lanes_kernel, [fine] * 2 + [(3, ER, NZ)] * 2 + [(2 * (EY * TILES + ER), NZ)] * 2, name="lanes"
    )(b, v, mine, before, after, low, high)
    before, after = both_ways(up, down, "gz")
    p, q, qh, vh, vcx, up, down, sums = call(
        first_kernel,
        [block] * 3 + [fine, coarse] + [(FACE + NY + 2 * CY, NZ)] * 2 + [(1, NZ)],
        [fine, coarse] + work + [(NY, NZ)],
        name="first",
    )(b, d, be, ve, gm, vcm, before, after)
    mine = up
    before, after = both_ways(up, down, "gx")
    up, down = call(second_rows_kernel, [(PAIRS + 6, 8, NZ)] * 2, name="second_rows")(q, qh, mine, before, after)
    low, high = both_ways(up, down, "gy")
    m, im, sums = call(second_kernel, [block, block, (1, NZ)], [fine, fine, coarse] + work, name="second")(
        b, d, p, q, qh, ve, vh, vcx, mine, before, after, low, high, sums
    )
    for axis in (("gy", "gz"), ("gx",)):
        sums = total(sums, axis)
    return call(
        last_kernel,
        [block, block],
        [block, block, pltpu.SemaphoreType.DMA((2 * PARTS,))],
        name="last",
        out_space=pl.ANY,
    )(b, p, q, m, im, sums)


def solution(mesh):
    spec = P("gx", "gy", "gz")
    return jax.shard_map(on_device, mesh=mesh, in_specs=(spec, spec), out_specs=(spec, spec), check_vma=False)
```

```python
import functools
import math

import jax
import jax.numpy as jnp
from jax import lax
from jax.experimental import pallas as pl
from jax.experimental.pallas import tpu as pltpu
from jax.sharding import PartitionSpec as P

ITERS = 2
FSWEEPS = 3
CSWEEPS = 4
COARSEN = 4
damping = 2.0 / 3.0
keep = 1.0 - damping

NX, NY, NZ = 16, 32, 128
HF = 3
HC = 4
DEEP = 20
DEEPC = 32
CX, CY = NX // COARSEN, NY // COARSEN
EX = NX + 2 * HF
EY = 40
EC = CX + 2 * HC
ER = CY + 2 * HC
FACE = HF * NY
COARSE = FACE + (HF - 1) * NY
PER = NZ // DEEP
PLACES = [(0, k) for k in range(EX)] + [(1, k) for k in range(1, EX - 1)]
TILES = -(-len(PLACES) // PER)
ROWS = HF * (EX - 2)
VMEM = pl.BlockSpec(memory_space=pltpu.VMEM)
F32 = jnp.float32


def lanes(shape):
    return lax.broadcasted_iota(jnp.int32, shape, len(shape) - 1)


def roll(x, shift, axis=-1):
    axis = axis % x.ndim
    return pltpu.roll(x, shift % x.shape[axis], axis)


def group_sum(x):
    lane = lanes(x.shape)
    x = x + jnp.where(lane % 2 == 0, roll(x, -1), roll(x, 1))
    return x + jnp.where(lane % 4 < 2, roll(x, -2), roll(x, 2))


def block_sums(planes, tmp):
    tmp[...] = group_sum(planes[0] + planes[1] + planes[2] + planes[3])
    rows = [tmp[pl.ds(k, CY, stride=COARSEN), :] for k in range(COARSEN)]
    return rows[0] + rows[1] + rows[2] + rows[3]


def merge(planes):
    lane = lanes(planes[0].shape)
    out = planes[0]
    for c in range(1, 4):
        out = jnp.where(lane % 4 == c, planes[c], out)
    return out


def unmerge(tile):
    lane = lanes(tile.shape) % 4
    moved = {step: roll(tile, -step) if step else tile for step in range(-3, 4)}
    planes = []
    for c in range(4):
        out = moved[c]
        for at in range(1, 4):
            out = jnp.where(lane == at, moved[c - at], out)
        planes.append(out)
    return planes


def edges(x, width):
    lane = lanes(x.shape)
    return jnp.where((lane < width) | (lane >= NZ - width), x, 0.0)


def inside():
    at = lax.axis_index("gx")
    return at > 0, at < lax.axis_size("gx") - 1


def layer(k, f, own, before, after):
    if HF <= k < HF + NX:
        return own[f][k - HF]
    ref, ok, k = (before, inside()[0], k - f) if k < HF else (after, inside()[1], k - HF - NX)
    return jnp.where(ok, ref[FACE * f + NY * k : FACE * f + NY * (k + 1)], 0.0)


def tile_of(group, at, mine, before, after):
    tile = (before, mine, after)[group][at : at + CY]
    return tile if group == 1 else jnp.where(inside()[group // 2], tile, 0.0)


def with_rows(tile, low, high):
    return jnp.concatenate([low, tile, high], axis=0)


def start_kernel(bd_ref, v_ref, up_ref, down_ref, tmp):
    b_ref, d_ref = bd_ref.at[0], bd_ref.at[1]
    for i in range(NX):
        v_ref[i] = damping / (6.0 + d_ref[i])
    g, vc = [], []
    for c in range(CX):
        g.append(block_sums([b_ref[COARSEN * c + k] for k in range(COARSEN)], tmp) * 0.25)
        cd = 6.0 + block_sums([d_ref[COARSEN * c + k] for k in range(COARSEN)], tmp) * 0.25
        vc.append(damping / cd)
    for ref in (up_ref, down_ref):
        for f, planes in enumerate((g, vc)):
            ref[COARSE + CY * f : COARSE + CY * (f + 1)] = merge(planes)
    for k in range(HF):
        for ref, plane, far in ((down_ref, k, HF - 1), (up_ref, NX - HF + k, 0)):
            value, weight = b_ref[plane], v_ref[plane]
            ref[NY * k : NY * (k + 1)] = weight * value if k == far else value
            if k != far:
                at = FACE + NY * (k if ref is down_ref else k - 1)
                ref[at : at + NY] = weight


def rows_kernel(b, v, mine, before, after, up_ref, down_ref):
    for k in range(1, EX - 1):
        for f in range(2):
            plane = layer(k, f, (b, v), before, after)
            at = ROWS * f + HF * (k - 1)
            down_ref[at : at + HF] = plane[:HF]
            up_ref[at : at + HF] = plane[NY - HF :]
    for f in range(2):
        for group in range(3):
            tile = tile_of(group, COARSE + CY * f, mine, before, after)
            at = 2 * ROWS + HC * (3 * f + group)
            down_ref[at : at + HC] = tile[:HC]
            up_ref[at : at + HC] = tile[CY - HC :]


def slots(lane, width, place):
    first = (lane >= width * place) & (lane < width * (place + 1))
    last = lane >= NZ - width if place == 0 else (lane >= width * (place - 1)) & (lane < width * place)
    return first, last


def unpack(before, after, width, place):
    lane = lanes(after.shape)
    both = jnp.where(slots(lane, width, place)[0], after, before)
    return edges(roll(both, -width * place), width)


def lanes_kernel(b, v, mine, before, after, low, high, be, ve, ge, vce, up_ref, down_ref):
    for f, k in PLACES:
        out = (be, ve)[f]
        out[k, 0:8] = jnp.zeros((8, NZ), F32)
        out[k, EY - 8 : EY] = jnp.zeros((8, NZ), F32)
        out[k, 4 : 4 + NY] = layer(k, f, (b, v), before, after)
        if 0 < k < EX - 1:
            at = ROWS * f + HF * (k - 1)
            out[k, 4 - HF : 4] = low[at : at + HF]
            out[k, 4 + NY : 4 + NY + HF] = high[at : at + HF]
    lane = lanes((EY, NZ))
    for tile in range(TILES):
        up = jnp.zeros((EY, NZ), F32)
        down = jnp.zeros((EY, NZ), F32)
        for place, (f, k) in enumerate(PLACES[PER * tile : PER * (tile + 1)]):
            moved = roll((be, ve)[f][k], DEEP * place)
            first, last = slots(lane, DEEP, place)
            up = jnp.where(last, moved, up)
            down = jnp.where(first, moved, down)
        up_ref[EY * tile : EY * (tile + 1)] = up
        down_ref[EY * tile : EY * (tile + 1)] = down
    lane = lanes((ER, NZ))
    for f, out in enumerate((ge, vce)):
        up = jnp.zeros((ER, NZ), F32)
        down = jnp.zeros((ER, NZ), F32)
        for group in range(3):
            at = 2 * ROWS + HC * (3 * f + group)
            tile = tile_of(group, COARSE + CY * f, mine, before, after)
            tile = with_rows(tile, low[at : at + HC], high[at : at + HC])
            out[group] = tile
            moved = roll(tile, DEEPC * group)
            first, last = slots(lane, DEEPC, group)
            up = jnp.where(last, moved, up)
            down = jnp.where(first, moved, down)
        at = EY * TILES + ER * f
        up_ref[at : at + ER] = up
        down_ref[at : at + ER] = down


def beyond_fine(k, f, before, after):
    tile, place = divmod(PLACES.index((f, k)), PER)
    return unpack(before[EY * tile : EY * (tile + 1)], after[EY * tile : EY * (tile + 1)], DEEP, place)


def beyond_coarse(group, f, before, after):
    at = EY * TILES + ER * f
    return unpack(before[at : at + ER], after[at : at + ER], DEEPC, group)


def crossed(block, beyond, step):
    lane = lanes(block.shape)
    below, below_beyond = roll(block, step), roll(beyond, step)
    above, above_beyond = roll(block, -step), roll(beyond, -step)
    low, high = lane < step, lane >= NZ - step
    return (
        jnp.where(low, below_beyond, below) + jnp.where(high, above_beyond, above),
        jnp.where(low, below, below_beyond) + jnp.where(high, above, above_beyond),
    )


PAD = 8


def neighbours(src, k, rows, step=1):
    at = PAD
    here = [src[part, k, at : at + rows] for part in range(2)]
    along = crossed(here[0], here[1], step)
    out = []
    for part in range(2):
        beside = src[part, k - 1, at : at + rows] + src[part, k + 1, at : at + rows]
        beside = beside + (src[part, k, at - 1 : at - 1 + rows] + src[part, k, at + 1 : at + 1 + rows])
        out.append(beside + along[part])
    return here, out


def expand(coarse, part, k, lo):
    c = (k - HF) // COARSEN + HC
    first = lax.broadcasted_iota(jnp.int32, (8, NZ), 0) < 4
    groups = []
    for j in range(EY // 8):
        row = PAD + 3 + 2 * j
        a = jnp.broadcast_to(coarse[part, c, row : row + 1], (8, NZ))
        b = jnp.broadcast_to(coarse[part, c, row + 1 : row + 2], (8, NZ))
        groups.append(jnp.where(first, a, b))
    return jnp.concatenate(groups, axis=0)


def precondition(rhs, weight, crhs, cweight, fa, fb, ca, cb):
    for ref, rows in ((fa, EY), (fb, EY), (ca, ER), (cb, ER)):
        for part in range(2):
            for k in range(ref.shape[1]):
                ref[part, k, 0:PAD] = jnp.zeros((PAD, NZ), F32)
                ref[part, k, PAD + rows :] = jnp.zeros((PAD, NZ), F32)
    for k in range(EC):
        for part in range(2):
            ca[part, k, PAD : PAD + ER] = cweight[part, k] * crhs[part, k]
    src, dst = ca, cb
    for sweep in range(1, CSWEEPS):
        for k in range(sweep, EC - sweep):
            here, beside = neighbours(src, k, ER, COARSEN)
            for part in range(2):
                dst[part, k, PAD : PAD + ER] = keep * here[part] + cweight[part, k] * (crhs[part, k] + beside[part])
        src, dst = dst, src
    coarse = src
    for k in range(EX):
        for part in range(2):
            value = rhs[part][k]
            fa[part, k, PAD : PAD + EY] = weight[part][k] * value if 0 < k < EX - 1 else value
    src, dst = fa, fb
    for sweep in range(1, FSWEEPS):
        for k in range(sweep, EX - sweep):
            here, beside = neighbours(src, k, EY)
            for part in range(2):
                new = keep * here[part] + weight[part][k] * (rhs[part][k] + beside[part])
                if sweep == FSWEEPS - 1:
                    new = new + expand(coarse, part, k, 0)
                dst[part, k, PAD : PAD + EY] = new
        src, dst = dst, src


def image_plane(src, i):
    k, at = i + HF, PAD + 4
    here = [src[part, k, at : at + NY] for part in range(2)]
    along = crossed(here[0], here[1], 1)
    out = []
    for part in range(2):
        beside = src[part, k - 1, at : at + NY] + src[part, k + 1, at : at + NY]
        beside = beside + (src[part, k, at - 1 : at - 1 + NY] + src[part, k, at + 1 : at + 1 + NY])
        out.append(beside + along[part])
    return here, out


def add_up(x):
    return (x[0:8] + x[8:16]) + (x[16:24] + x[24:32])


SHARE = NZ // 8


def store_sums(out_ref, totals, row=None):
    row = jnp.zeros((1, NZ), F32) if row is None else row
    for i, part in totals.items():
        part = jnp.sum(part, axis=0, keepdims=True)
        for step in (64, 32, 16):
            part = part + roll(part, step)
        row = jnp.where(lanes((1, NZ)) // SHARE == i, part, row)
    out_ref[...] = row


NEAR = 4
NEARC = 16


def first_kernel(
    b_ref, d_ref, b, v, gm, vcm, before, after, p_ref, q_ref, qh_ref, vh_ref, vcx_ref, up_ref, down_ref, sum_ref,
    bh, gx, fa, fb, ca, cb, tmp,
):
    for f, k in PLACES:
        (bh, vh_ref)[f][k] = beyond_fine(k, f, before, after)
    for f, (tiles, out) in enumerate(((gm, gx), (vcm, vcx_ref))):
        for group in range(3):
            for part, tile in enumerate((tiles[group], beyond_coarse(group, f, before, after))):
                for c, plane in enumerate(unmerge(tile)):
                    out[part, 4 * group + c] = plane
    precondition((b, bh), (v, vh_ref), gx, vcx_ref, fa, fb, ca, cb)
    rp = jnp.zeros((8, NZ), F32)
    pq = jnp.zeros((8, NZ), F32)
    for i in range(NX):
        (p, ph), (beside, beside_h) = image_plane(fa, i)
        q = (6.0 + d_ref[i]) * p - beside
        weight = vh_ref[i + HF, 4 : 4 + NY]
        within = weight > 0.0
        p_ref[i] = p
        q_ref[i] = q
        qh_ref[i] = jnp.where(within, damping / jnp.where(within, weight, 1.0) * ph - beside_h, 0.0)
        rp = rp + add_up(b_ref[i] * p)
        pq = pq + add_up(p * q)
    store_sums(sum_ref, {0: rp, 1: pq})
    for part, field in enumerate((q_ref, qh_ref)):
        means = [
            block_sums([field[COARSEN * c + k] for k in range(COARSEN)], tmp) * 0.25 for c in range(CX)
        ]
        tile = merge(means)
        if part == 1:
            tile = roll(tile, NEARC)
        for ref in (up_ref, down_ref):
            ref[FACE + NY + CY * part : FACE + NY + CY * (part + 1)] = tile
    lane = lanes((NY, NZ))
    for ref, first, far in ((down_ref, 0, HF - 1), (up_ref, NX - HF, 0)):
        packed = jnp.zeros((NY, NZ), F32)
        for k in range(HF):
            value, beyond = q_ref[first + k], qh_ref[first + k]
            if k == far:
                value = value * v[HF + first + k, 4 : 4 + NY]
                beyond = beyond * vh_ref[HF + first + k, 4 : 4 + NY]
            ref[NY * k : NY * (k + 1)] = value
            packed = jnp.where(lane // (2 * NEAR) == k, roll(beyond, NEAR + 2 * NEAR * k), packed)
        ref[FACE : FACE + NY] = packed


def layer_beyond(k, own, before, after):
    if HF <= k < HF + NX:
        return own[k - HF]
    ref, ok, k = (before, inside()[0], k) if k < HF else (after, inside()[1], k - HF - NX)
    return jnp.where(ok, edges(roll(ref[FACE : FACE + NY], -NEAR - 2 * NEAR * k), NEAR), 0.0)


SIDE = NZ // (2 * NEAR)
WIDE = ROWS + 3 * HC


def second_rows_kernel(q, qh, mine, before, after, up_ref, down_ref):
    for k in range(1, EX - 1):
        plane = layer(k, 0, (q,), before, after)
        at = HF * (k - 1)
        down_ref[at : at + HF] = plane[:HF]
        up_ref[at : at + HF] = plane[NY - HF :]
    lane = lanes((8, NZ))
    wide = jnp.zeros((8, NZ), F32)
    for group in range(3):
        tile = tile_of(group, FACE + NY, mine, before, after)
        beyond = tile_of(group, FACE + NY + CY, mine, before, after)
        wide = jnp.where(lane // (2 * NEARC) == group, roll(beyond, 2 * NEARC * group), wide)
        at = ROWS + HC * group
        down_ref[at : at + HC] = tile[:HC]
        up_ref[at : at + HC] = tile[CY - HC :]
    for ref, rows in ((up_ref, slice(NY - 8, NY)), (down_ref, slice(0, 8))):
        ref[WIDE + 16 : WIDE + 24] = wide
        for half in range(2):
            packed = jnp.zeros((8, NZ), F32)
            for k in range(SIDE * half, min(EX, SIDE * (half + 1))):
                plane = layer_beyond(k, qh, before, after)[rows]
                packed = jnp.where(lane // (2 * NEAR) == k % SIDE, roll(plane, NEAR + 2 * NEAR * (k % SIDE)), packed)
            ref[WIDE + 8 * half : WIDE + 8 * (half + 1)] = packed


def second_kernel(
    b_ref, d_ref, p_ref, q_ref, qh_ref, v, vh_ref, vcx_ref, mine, before, after, low, high, first_ref,
    m_ref, im_ref, sum_ref, q, qh, gx, fa, fb, ca, cb,
):
    for k in range(EX):
        at, place = HF * (k - 1), -NEAR - 2 * NEAR * (k % SIDE)
        for out in (q, qh):
            out[k, 0:8] = jnp.zeros((8, NZ), F32)
            out[k, EY - 8 : EY] = jnp.zeros((8, NZ), F32)
        q[k, 4 : 4 + NY] = layer(k, 0, (q_ref,), before, after)
        if 0 < k < EX - 1:
            q[k, 4 - HF : 4] = low[at : at + HF]
            q[k, 4 + NY : 4 + NY + HF] = high[at : at + HF]
        tile = slice(WIDE + 8 * (k // SIDE), WIDE + 8 * (k // SIDE + 1))
        qh[k, 4 - HF : 4] = edges(roll(low[tile], place), NEAR)[8 - HF :]
        qh[k, 4 : 4 + NY] = layer_beyond(k, qh_ref, before, after)
        qh[k, 4 + NY : 4 + NY + HF] = edges(roll(high[tile], place), NEAR)[:HF]
    for group in range(3):
        at, row = FACE + NY, ROWS + HC * group
        tile = with_rows(tile_of(group, at, mine, before, after), low[row : row + HC], high[row : row + HC])
        wide = [roll(ref[WIDE + 16 : WIDE + 24], -2 * NEARC * group) for ref in (low, high)]
        beyond = tile_of(group, at + CY, mine, before, after)
        beyond = with_rows(beyond, wide[0][CY - HC :], wide[1][:HC])
        for part, merged in enumerate((tile, edges(roll(beyond, -NEARC), NEARC))):
            for c, plane in enumerate(unmerge(merged)):
                gx[part, 4 * group + c] = plane
    precondition((q, qh), (v, vh_ref), gx, vcx_ref, fa, fb, ca, cb)
    sums = [jnp.zeros((8, NZ), F32)] * 4
    for i in range(NX):
        (m, _), (beside, _) = image_plane(fa, i)
        im = (6.0 + d_ref[i]) * m - beside
        m_ref[i] = m
        im_ref[i] = im
        pairs = ((q_ref[i], m), (b_ref[i], m), (p_ref[i], im), (m, im))
        sums = [s + add_up(x * y) for s, (x, y) in zip(sums, pairs)]
    store_sums(sum_ref, dict(enumerate(sums, 2)), first_ref[...])


PARTS = 4


def last_kernel(b_ref, p_ref, q_ref, m_ref, im_ref, sum_ref, x_out, r_out, x_ref, r_ref, sems):
    rp, pq, qm, rm, pim, mim = [
        jnp.sum(jnp.where(lanes((1, NZ)) // SHARE == i, sum_ref[...], 0.0), axis=1, keepdims=True) for i in range(6)
    ]
    alpha = rp / pq
    rho = rp - alpha * (pq + rm) + alpha * alpha * qm
    scale = 1.0 + rho / rp
    alpha_next = rho / (scale * scale * pq - scale * alpha * (pim + qm) + alpha * alpha * mim)
    along = alpha + alpha_next * scale
    across = alpha_next * alpha
    copies = []
    for part in range(PARTS):
        planes = range(NX // PARTS * part, NX // PARTS * (part + 1))
        for i in planes:
            x_ref[i] = along * p_ref[i] - across * m_ref[i]
            r_ref[i] = b_ref[i] - along * q_ref[i] + across * im_ref[i]
        at = pl.ds(planes[0], len(planes))
        for which, (src, dst) in enumerate(((x_ref, x_out), (r_ref, r_out))):
            copies.append(pltpu.make_async_copy(src.at[at], dst.at[at], sems.at[2 * part + which]))
            copies[-1].start()
    for copy in copies:
        copy.wait()


def call(kernel, outs, scratch=(), name=None, out_space=pltpu.VMEM):
    def run(*args):
        return pl.pallas_call(
            kernel,
            out_shape=[jax.ShapeDtypeStruct(shape, F32) for shape in outs],
            in_specs=[VMEM] * len(args),
            out_specs=[pl.BlockSpec(memory_space=out_space)] * len(outs),
            scratch_shapes=[pltpu.VMEM(shape, F32) if isinstance(shape, tuple) else shape for shape in scratch],
            compiler_params=pltpu.CompilerParams(vmem_limit_bytes=24 * 2**20),
            name=name,
        )(*args)

    return run


def both_ways(up, down, axis):
    count = lax.axis_size(axis)
    steps = [(i, (i + 1) % count) for i in range(count if axis == "gx" else count - 1)]
    before = lax.ppermute(up, axis, steps)
    after = lax.ppermute(down, axis, [(j, i) for i, j in steps])
    return before, after


def total(x, axis):
    count = math.prod(lax.axis_size(name) for name in axis)
    spread = jnp.broadcast_to(x[None], (count,) + x.shape)
    return jnp.sum(lax.all_to_all(spread, axis, 0, 0, tiled=True), axis=0)


def on_device(b, d):
    block, fine, coarse = (NX, NY, NZ), (EX, EY, NZ), (2, EC, ER, NZ)
    work = [(2, EX, EY + 2 * PAD, NZ)] * 2 + [(2, EC, ER + 2 * PAD, NZ)] * 2
    bd = lax.optimization_barrier(jnp.stack([b, d]))
    v, up, down = call(start_kernel, [block] + [(COARSE + 2 * CY, NZ)] * 2, [(NY, NZ)], name="start")(bd)
    mine = up
    before, after = both_ways(up, down, "gx")
    up, down = call(rows_kernel, [(2 * ROWS + 6 * HC, NZ)] * 2, name="rows")(b, v, mine, before, after)
    low, high = both_ways(up, down, "gy")
    be, ve, gm, vcm, up, down = call(
        lanes_kernel, [fine] * 2 + [(3, ER, NZ)] * 2 + [(EY * TILES + 2 * ER, NZ)] * 2, name="lanes"
    )(b, v, mine, before, after, low, high)
    before, after = both_ways(up, down, "gz")
    p, q, qh, vh, vcx, up, down, sums = call(
        first_kernel,
        [block] * 3 + [fine, coarse] + [(FACE + NY + 2 * CY, NZ)] * 2 + [(1, NZ)],
        [fine, coarse] + work + [(NY, NZ)],
        name="first",
    )(b, d, be, ve, gm, vcm, before, after)
    mine = up
    before, after = both_ways(up, down, "gx")
    up, down = call(second_rows_kernel, [(WIDE + 24, NZ)] * 2, name="second_rows")(q, qh, mine, before, after)
    low, high = both_ways(up, down, "gy")
    m, im, sums = call(second_kernel, [block, block, (1, NZ)], [fine, fine, coarse] + work, name="second")(
        b, d, p, q, qh, ve, vh, vcx, mine, before, after, low, high, sums
    )
    for axis in (("gy", "gz"), ("gx",)):
        sums = total(sums, axis)
    return call(
        last_kernel,
        [block, block],
        [block, block, pltpu.SemaphoreType.DMA((2 * PARTS,))],
        name="last",
        out_space=pl.ANY,
    )(b, p, q, m, im, sums)


def solution(mesh):
    spec = P("gx", "gy", "gz")
    return jax.shard_map(on_device, mesh=mesh, in_specs=(spec, spec), out_specs=(spec, spec), check_vma=False)
```

```python
import functools
import math

import jax
import jax.numpy as jnp
from jax import lax
from jax.experimental import pallas as pl
from jax.experimental.pallas import tpu as pltpu
from jax.sharding import PartitionSpec as P

ITERS = 2
FSWEEPS = 3
CSWEEPS = 4
COARSEN = 4
damping = 2.0 / 3.0
keep = 1.0 - damping

NX, NY, NZ = 16, 32, 128
HF = 3
HC = 4
DEEP = 20
DEEPC = 32
CX, CY = NX // COARSEN, NY // COARSEN
EX = NX + 2 * HF
EY = 40
EC = CX + 2 * HC
ER = CY + 2 * HC
FACE = HF * NY
COARSE = FACE + (HF - 1) * NY
PER = NZ // DEEP
PLACES = [(0, k) for k in range(EX)] + [(1, k) for k in range(1, EX - 1)]
TILES = -(-len(PLACES) // PER)
ROWS = HF * (EX - 2)
PARTS = CX
VMEM = pl.BlockSpec(memory_space=pltpu.VMEM)
F32 = jnp.float32


def lanes(shape):
    return lax.broadcasted_iota(jnp.int32, shape, len(shape) - 1)


def roll(x, shift, axis=-1):
    axis = axis % x.ndim
    return pltpu.roll(x, shift % x.shape[axis], axis)


def group_sum(x):
    lane = lanes(x.shape)
    x = x + jnp.where(lane % 2 == 0, roll(x, -1), roll(x, 1))
    return x + jnp.where(lane % 4 < 2, roll(x, -2), roll(x, 2))


def block_sums(planes, tmp):
    tmp[...] = group_sum(planes[0] + planes[1] + planes[2] + planes[3])
    rows = [tmp[pl.ds(k, CY, stride=COARSEN), :] for k in range(COARSEN)]
    return rows[0] + rows[1] + rows[2] + rows[3]


def merge(planes):
    lane = lanes(planes[0].shape)
    out = planes[0]
    for c in range(1, 4):
        out = jnp.where(lane % 4 == c, planes[c], out)
    return out


def unmerge(tile):
    lane = lanes(tile.shape) % 4
    moved = {step: roll(tile, -step) if step else tile for step in range(-3, 4)}
    planes = []
    for c in range(4):
        out = moved[c]
        for at in range(1, 4):
            out = jnp.where(lane == at, moved[c - at], out)
        planes.append(out)
    return planes


def edges(x, width):
    lane = lanes(x.shape)
    return jnp.where((lane < width) | (lane >= NZ - width), x, 0.0)


def inside():
    at = lax.axis_index("gx")
    return at > 0, at < lax.axis_size("gx") - 1


def layer(k, f, own, before, after):
    if HF <= k < HF + NX:
        return own[f][k - HF]
    ref, ok, k = (before, inside()[0], k - f) if k < HF else (after, inside()[1], k - HF - NX)
    return jnp.where(ok, ref[FACE * f + NY * k : FACE * f + NY * (k + 1)], 0.0)


def tile_of(group, at, mine, before, after):
    tile = (before, mine, after)[group][at : at + CY]
    return tile if group == 1 else jnp.where(inside()[group // 2], tile, 0.0)


def with_rows(tile, low, high):
    return jnp.concatenate([low, tile, high], axis=0)


def start_kernel(b_hbm, d_hbm, v_ref, up_ref, down_ref, b_ref, d_ref, tmp, sems):
    copies = []
    for part in range(PARTS):
        at = pl.ds(NX // PARTS * part, NX // PARTS)
        for which, (src, dst) in enumerate(((b_hbm, b_ref), (d_hbm, d_ref))):
            copies.append(pltpu.make_async_copy(src.at[at], dst.at[at], sems.at[2 * part + which]))
            copies[-1].start()
    g, vc = [], []
    for c in range(CX):
        copies[2 * c].wait()
        copies[2 * c + 1].wait()
        for i in range(COARSEN * c, COARSEN * (c + 1)):
            v_ref[i] = damping / (6.0 + d_ref[i])
        g.append(block_sums([b_ref[COARSEN * c + k] for k in range(COARSEN)], tmp) * 0.25)
        cd = 6.0 + block_sums([d_ref[COARSEN * c + k] for k in range(COARSEN)], tmp) * 0.25
        vc.append(damping / cd)
    for ref in (up_ref, down_ref):
        for f, planes in enumerate((g, vc)):
            ref[COARSE + CY * f : COARSE + CY * (f + 1)] = merge(planes)
    for k in range(HF):
        for ref, plane, far in ((down_ref, k, HF - 1), (up_ref, NX - HF + k, 0)):
            value, weight = b_ref[plane], v_ref[plane]
            ref[NY * k : NY * (k + 1)] = weight * value if k == far else value
            if k != far:
                at = FACE + NY * (k if ref is down_ref else k - 1)
                ref[at : at + NY] = weight


def rows_kernel(b, v, mine, before, after, up_ref, down_ref):
    for k in range(1, EX - 1):
        for f in range(2):
            plane = layer(k, f, (b, v), before, after)
            at = ROWS * f + HF * (k - 1)
            down_ref[at : at + HF] = plane[:HF]
            up_ref[at : at + HF] = plane[NY - HF :]
    for f in range(2):
        for group in range(3):
            tile = tile_of(group, COARSE + CY * f, mine, before, after)
            at = 2 * ROWS + HC * (3 * f + group)
            down_ref[at : at + HC] = tile[:HC]
            up_ref[at : at + HC] = tile[CY - HC :]


def slots(lane, width, place):
    first = (lane >= width * place) & (lane < width * (place + 1))
    last = lane >= NZ - width if place == 0 else (lane >= width * (place - 1)) & (lane < width * place)
    return first, last


def unpack(before, after, width, place):
    lane = lanes(after.shape)
    both = jnp.where(slots(lane, width, place)[0], after, before)
    return edges(roll(both, -width * place), width)


def lanes_kernel(b, v, mine, before, after, low, high, be, ve, ge, vce, up_ref, down_ref):
    for f, k in PLACES:
        out = (be, ve)[f]
        out[k, 0:8] = jnp.zeros((8, NZ), F32)
        out[k, EY - 8 : EY] = jnp.zeros((8, NZ), F32)
        out[k, 4 : 4 + NY] = layer(k, f, (b, v), before, after)
        if 0 < k < EX - 1:
            at = ROWS * f + HF * (k - 1)
            out[k, 4 - HF : 4] = low[at : at + HF]
            out[k, 4 + NY : 4 + NY + HF] = high[at : at + HF]
    lane = lanes((EY, NZ))
    for tile in range(TILES):
        up = jnp.zeros((EY, NZ), F32)
        down = jnp.zeros((EY, NZ), F32)
        for place, (f, k) in enumerate(PLACES[PER * tile : PER * (tile + 1)]):
            moved = roll((be, ve)[f][k], DEEP * place)
            first, last = slots(lane, DEEP, place)
            up = jnp.where(last, moved, up)
            down = jnp.where(first, moved, down)
        up_ref[EY * tile : EY * (tile + 1)] = up
        down_ref[EY * tile : EY * (tile + 1)] = down
    lane = lanes((ER, NZ))
    for f, out in enumerate((ge, vce)):
        up = jnp.zeros((ER, NZ), F32)
        down = jnp.zeros((ER, NZ), F32)
        for group in range(3):
            at = 2 * ROWS + HC * (3 * f + group)
            tile = tile_of(group, COARSE + CY * f, mine, before, after)
            tile = with_rows(tile, low[at : at + HC], high[at : at + HC])
            out[group] = tile
            moved = roll(tile, DEEPC * group)
            first, last = slots(lane, DEEPC, group)
            up = jnp.where(last, moved, up)
            down = jnp.where(first, moved, down)
        at = EY * TILES + ER * f
        up_ref[at : at + ER] = up
        down_ref[at : at + ER] = down


def beyond_fine(k, f, before, after):
    tile, place = divmod(PLACES.index((f, k)), PER)
    return unpack(before[EY * tile : EY * (tile + 1)], after[EY * tile : EY * (tile + 1)], DEEP, place)


def beyond_coarse(group, f, before, after):
    at = EY * TILES + ER * f
    return unpack(before[at : at + ER], after[at : at + ER], DEEPC, group)


def crossed(block, beyond, step):
    lane = lanes(block.shape)
    below, below_beyond = roll(block, step), roll(beyond, step)
    above, above_beyond = roll(block, -step), roll(beyond, -step)
    low, high = lane < step, lane >= NZ - step
    return (
        jnp.where(low, below_beyond, below) + jnp.where(high, above_beyond, above),
        jnp.where(low, below, below_beyond) + jnp.where(high, above, above_beyond),
    )


PAD = 8


def neighbours(src, k, rows, step=1):
    at = PAD
    here = [src[part, k, at : at + rows] for part in range(2)]
    along = crossed(here[0], here[1], step)
    out = []
    for part in range(2):
        beside = src[part, k - 1, at : at + rows] + src[part, k + 1, at : at + rows]
        beside = beside + (src[part, k, at - 1 : at - 1 + rows] + src[part, k, at + 1 : at + 1 + rows])
        out.append(beside + along[part])
    return here, out


def expand(coarse, part, k, lo):
    c = (k - HF) // COARSEN + HC
    first = lax.broadcasted_iota(jnp.int32, (8, NZ), 0) < 4
    groups = []
    for j in range(EY // 8):
        row = PAD + 3 + 2 * j
        a = jnp.broadcast_to(coarse[part, c, row : row + 1], (8, NZ))
        b = jnp.broadcast_to(coarse[part, c, row + 1 : row + 2], (8, NZ))
        groups.append(jnp.where(first, a, b))
    return jnp.concatenate(groups, axis=0)


def precondition(rhs, weight, crhs, cweight, fa, fb, ca, cb):
    for ref, rows in ((fa, EY), (fb, EY), (ca, ER), (cb, ER)):
        for part in range(2):
            for k in range(ref.shape[1]):
                ref[part, k, 0:PAD] = jnp.zeros((PAD, NZ), F32)
                ref[part, k, PAD + rows :] = jnp.zeros((PAD, NZ), F32)
    for k in range(EC):
        for part in range(2):
            ca[part, k, PAD : PAD + ER] = cweight[part, k] * crhs[part, k]
    src, dst = ca, cb
    for sweep in range(1, CSWEEPS):
        for k in range(sweep, EC - sweep):
            here, beside = neighbours(src, k, ER, COARSEN)
            for part in range(2):
                dst[part, k, PAD : PAD + ER] = keep * here[part] + cweight[part, k] * (crhs[part, k] + beside[part])
        src, dst = dst, src
    coarse = src
    for k in range(EX):
        for part in range(2):
            value = rhs[part][k]
            fa[part, k, PAD : PAD + EY] = weight[part][k] * value if 0 < k < EX - 1 else value
    src, dst = fa, fb
    for sweep in range(1, FSWEEPS):
        for k in range(sweep, EX - sweep):
            here, beside = neighbours(src, k, EY)
            for part in range(2):
                new = keep * here[part] + weight[part][k] * (rhs[part][k] + beside[part])
                if sweep == FSWEEPS - 1:
                    new = new + expand(coarse, part, k, 0)
                dst[part, k, PAD : PAD + EY] = new
        src, dst = dst, src


def image_plane(src, i):
    k, at = i + HF, PAD + 4
    here = [src[part, k, at : at + NY] for part in range(2)]
    along = crossed(here[0], here[1], 1)
    out = []
    for part in range(2):
        beside = src[part, k - 1, at : at + NY] + src[part, k + 1, at : at + NY]
        beside = beside + (src[part, k, at - 1 : at - 1 + NY] + src[part, k, at + 1 : at + 1 + NY])
        out.append(beside + along[part])
    return here, out


def add_up(x):
    return (x[0:8] + x[8:16]) + (x[16:24] + x[24:32])


SHARE = NZ // 8


def store_sums(out_ref, totals, row=None):
    row = jnp.zeros((1, NZ), F32) if row is None else row
    for i, part in totals.items():
        part = jnp.sum(part, axis=0, keepdims=True)
        for step in (64, 32, 16):
            part = part + roll(part, step)
        row = jnp.where(lanes((1, NZ)) // SHARE == i, part, row)
    out_ref[...] = row


NEAR = 4
NEARC = 16


def first_kernel(
    b_ref, d_ref, b, v, gm, vcm, before, after, p_ref, q_ref, qh_ref, vh_ref, vcx_ref, up_ref, down_ref, sum_ref,
    bh, gx, fa, fb, ca, cb, tmp,
):
    for f, k in PLACES:
        (bh, vh_ref)[f][k] = beyond_fine(k, f, before, after)
    for f, (tiles, out) in enumerate(((gm, gx), (vcm, vcx_ref))):
        for group in range(3):
            for part, tile in enumerate((tiles[group], beyond_coarse(group, f, before, after))):
                for c, plane in enumerate(unmerge(tile)):
                    out[part, 4 * group + c] = plane
    precondition((b, bh), (v, vh_ref), gx, vcx_ref, fa, fb, ca, cb)
    rp = jnp.zeros((8, NZ), F32)
    pq = jnp.zeros((8, NZ), F32)
    for i in range(NX):
        (p, ph), (beside, beside_h) = image_plane(fa, i)
        q = (6.0 + d_ref[i]) * p - beside
        weight = vh_ref[i + HF, 4 : 4 + NY]
        within = weight > 0.0
        p_ref[i] = p
        q_ref[i] = q
        qh_ref[i] = jnp.where(within, damping / jnp.where(within, weight, 1.0) * ph - beside_h, 0.0)
        rp = rp + add_up(b_ref[i] * p)
        pq = pq + add_up(p * q)
    store_sums(sum_ref, {0: rp, 1: pq})
    for part, field in enumerate((q_ref, qh_ref)):
        means = [
            block_sums([field[COARSEN * c + k] for k in range(COARSEN)], tmp) * 0.25 for c in range(CX)
        ]
        tile = merge(means)
        if part == 1:
            tile = roll(tile, NEARC)
        for ref in (up_ref, down_ref):
            ref[FACE + NY + CY * part : FACE + NY + CY * (part + 1)] = tile
    lane = lanes((NY, NZ))
    for ref, first, far in ((down_ref, 0, HF - 1), (up_ref, NX - HF, 0)):
        packed = jnp.zeros((NY, NZ), F32)
        for k in range(HF):
            value, beyond = q_ref[first + k], qh_ref[first + k]
            if k == far:
                value = value * v[HF + first + k, 4 : 4 + NY]
                beyond = beyond * vh_ref[HF + first + k, 4 : 4 + NY]
            ref[NY * k : NY * (k + 1)] = value
            packed = jnp.where(lane // (2 * NEAR) == k, roll(beyond, NEAR + 2 * NEAR * k), packed)
        ref[FACE : FACE + NY] = packed


def layer_beyond(k, own, before, after):
    if HF <= k < HF + NX:
        return own[k - HF]
    ref, ok, k = (before, inside()[0], k) if k < HF else (after, inside()[1], k - HF - NX)
    return jnp.where(ok, edges(roll(ref[FACE : FACE + NY], -NEAR - 2 * NEAR * k), NEAR), 0.0)


SIDE = NZ // (2 * NEAR)
WIDE = ROWS + 3 * HC


def second_rows_kernel(q, qh, mine, before, after, up_ref, down_ref):
    for k in range(1, EX - 1):
        plane = layer(k, 0, (q,), before, after)
        at = HF * (k - 1)
        down_ref[at : at + HF] = plane[:HF]
        up_ref[at : at + HF] = plane[NY - HF :]
    lane = lanes((8, NZ))
    wide = jnp.zeros((8, NZ), F32)
    for group in range(3):
        tile = tile_of(group, FACE + NY, mine, before, after)
        beyond = tile_of(group, FACE + NY + CY, mine, before, after)
        wide = jnp.where(lane // (2 * NEARC) == group, roll(beyond, 2 * NEARC * group), wide)
        at = ROWS + HC * group
        down_ref[at : at + HC] = tile[:HC]
        up_ref[at : at + HC] = tile[CY - HC :]
    for ref, rows in ((up_ref, slice(NY - 8, NY)), (down_ref, slice(0, 8))):
        ref[WIDE + 16 : WIDE + 24] = wide
        for half in range(2):
            packed = jnp.zeros((8, NZ), F32)
            for k in range(SIDE * half, min(EX, SIDE * (half + 1))):
                plane = layer_beyond(k, qh, before, after)[rows]
                packed = jnp.where(lane // (2 * NEAR) == k % SIDE, roll(plane, NEAR + 2 * NEAR * (k % SIDE)), packed)
            ref[WIDE + 8 * half : WIDE + 8 * (half + 1)] = packed


def second_kernel(
    b_ref, d_ref, p_ref, q_ref, qh_ref, v, vh_ref, vcx_ref, mine, before, after, low, high, first_ref,
    m_ref, im_ref, sum_ref, q, qh, gx, fa, fb, ca, cb,
):
    for k in range(EX):
        at, place = HF * (k - 1), -NEAR - 2 * NEAR * (k % SIDE)
        for out in (q, qh):
            out[k, 0:8] = jnp.zeros((8, NZ), F32)
            out[k, EY - 8 : EY] = jnp.zeros((8, NZ), F32)
        q[k, 4 : 4 + NY] = layer(k, 0, (q_ref,), before, after)
        if 0 < k < EX - 1:
            q[k, 4 - HF : 4] = low[at : at + HF]
            q[k, 4 + NY : 4 + NY + HF] = high[at : at + HF]
        tile = slice(WIDE + 8 * (k // SIDE), WIDE + 8 * (k // SIDE + 1))
        qh[k, 4 - HF : 4] = edges(roll(low[tile], place), NEAR)[8 - HF :]
        qh[k, 4 : 4 + NY] = layer_beyond(k, qh_ref, before, after)
        qh[k, 4 + NY : 4 + NY + HF] = edges(roll(high[tile], place), NEAR)[:HF]
    for group in range(3):
        at, row = FACE + NY, ROWS + HC * group
        tile = with_rows(tile_of(group, at, mine, before, after), low[row : row + HC], high[row : row + HC])
        wide = [roll(ref[WIDE + 16 : WIDE + 24], -2 * NEARC * group) for ref in (low, high)]
        beyond = tile_of(group, at + CY, mine, before, after)
        beyond = with_rows(beyond, wide[0][CY - HC :], wide[1][:HC])
        for part, merged in enumerate((tile, edges(roll(beyond, -NEARC), NEARC))):
            for c, plane in enumerate(unmerge(merged)):
                gx[part, 4 * group + c] = plane
    precondition((q, qh), (v, vh_ref), gx, vcx_ref, fa, fb, ca, cb)
    sums = [jnp.zeros((8, NZ), F32)] * 4
    for i in range(NX):
        (m, _), (beside, _) = image_plane(fa, i)
        im = (6.0 + d_ref[i]) * m - beside
        m_ref[i] = m
        im_ref[i] = im
        pairs = ((q_ref[i], m), (b_ref[i], m), (p_ref[i], im), (m, im))
        sums = [s + add_up(x * y) for s, (x, y) in zip(sums, pairs)]
    store_sums(sum_ref, dict(enumerate(sums, 2)), first_ref[...])


def last_kernel(b_ref, p_ref, q_ref, m_ref, im_ref, sum_ref, x_out, r_out, x_ref, r_ref, sems):
    rp, pq, qm, rm, pim, mim = [
        jnp.sum(jnp.where(lanes((1, NZ)) // SHARE == i, sum_ref[...], 0.0), axis=1, keepdims=True) for i in range(6)
    ]
    alpha = rp / pq
    rho = rp - alpha * (pq + rm) + alpha * alpha * qm
    scale = 1.0 + rho / rp
    alpha_next = rho / (scale * scale * pq - scale * alpha * (pim + qm) + alpha * alpha * mim)
    along = alpha + alpha_next * scale
    across = alpha_next * alpha
    copies = []
    for part in range(PARTS):
        planes = range(NX // PARTS * part, NX // PARTS * (part + 1))
        for i in planes:
            x_ref[i] = along * p_ref[i] - across * m_ref[i]
            r_ref[i] = b_ref[i] - along * q_ref[i] + across * im_ref[i]
        at = pl.ds(planes[0], len(planes))
        for which, (src, dst) in enumerate(((x_ref, x_out), (r_ref, r_out))):
            copies.append(pltpu.make_async_copy(src.at[at], dst.at[at], sems.at[2 * part + which]))
            copies[-1].start()
    for copy in copies:
        copy.wait()


def call(kernel, outs, scratch=(), name=None, in_space=pltpu.VMEM, out_space=pltpu.VMEM):
    def run(*args):
        return pl.pallas_call(
            kernel,
            out_shape=[jax.ShapeDtypeStruct(shape, F32) for shape in outs],
            in_specs=[pl.BlockSpec(memory_space=in_space)] * len(args),
            out_specs=[pl.BlockSpec(memory_space=out_space)] * len(outs),
            scratch_shapes=[pltpu.VMEM(shape, F32) if isinstance(shape, tuple) else shape for shape in scratch],
            compiler_params=pltpu.CompilerParams(vmem_limit_bytes=24 * 2**20),
            name=name,
        )(*args)

    return run


def both_ways(up, down, axis):
    count = lax.axis_size(axis)
    steps = [(i, (i + 1) % count) for i in range(count if axis == "gx" else count - 1)]
    before = lax.ppermute(up, axis, steps)
    after = lax.ppermute(down, axis, [(j, i) for i, j in steps])
    return before, after


def total(x, axis):
    count = math.prod(lax.axis_size(name) for name in axis)
    spread = jnp.broadcast_to(x[None], (count,) + x.shape)
    return jnp.sum(lax.all_to_all(spread, axis, 0, 0, tiled=True), axis=0)


def on_device(b, d):
    block, fine, coarse = (NX, NY, NZ), (EX, EY, NZ), (2, EC, ER, NZ)
    work = [(2, EX, EY + 2 * PAD, NZ)] * 2 + [(2, EC, ER + 2 * PAD, NZ)] * 2
    bh, dh = (pltpu.with_memory_space_constraint(x, pltpu.HBM) for x in (b, d))
    v, up, down = call(start_kernel, [block] + [(COARSE + 2 * CY, NZ)] * 2, [block, block, (NY, NZ), pltpu.SemaphoreType.DMA((2 * PARTS,))], name="start", in_space=pltpu.HBM)(bh, dh)
    mine = up
    before, after = both_ways(up, down, "gx")
    up, down = call(rows_kernel, [(2 * ROWS + 6 * HC, NZ)] * 2, name="rows")(b, v, mine, before, after)
    low, high = both_ways(up, down, "gy")
    be, ve, gm, vcm, up, down = call(
        lanes_kernel, [fine] * 2 + [(3, ER, NZ)] * 2 + [(EY * TILES + 2 * ER, NZ)] * 2, name="lanes"
    )(b, v, mine, before, after, low, high)
    before, after = both_ways(up, down, "gz")
    p, q, qh, vh, vcx, up, down, sums = call(
        first_kernel,
        [block] * 3 + [fine, coarse] + [(FACE + NY + 2 * CY, NZ)] * 2 + [(1, NZ)],
        [fine, coarse] + work + [(NY, NZ)],
        name="first",
    )(b, d, be, ve, gm, vcm, before, after)
    mine = up
    before, after = both_ways(up, down, "gx")
    up, down = call(second_rows_kernel, [(WIDE + 24, NZ)] * 2, name="second_rows")(q, qh, mine, before, after)
    low, high = both_ways(up, down, "gy")
    m, im, sums = call(second_kernel, [block, block, (1, NZ)], [fine, fine, coarse] + work, name="second")(
        b, d, p, q, qh, ve, vh, vcx, mine, before, after, low, high, sums
    )
    for axis in (("gy", "gz"), ("gx",)):
        sums = total(sums, axis)
    return call(
        last_kernel,
        [block, block],
        [block, block, pltpu.SemaphoreType.DMA((2 * PARTS,))],
        name="last",
        out_space=pl.ANY,
    )(b, p, q, m, im, sums)


def solution(mesh):
    spec = P("gx", "gy", "gz")
    return jax.shard_map(on_device, mesh=mesh, in_specs=(spec, spec), out_specs=(spec, spec), check_vma=False)
```

```python
import functools
import math

import jax
import jax.numpy as jnp
from jax import lax
from jax.experimental import pallas as pl
from jax.experimental.pallas import tpu as pltpu
from jax.sharding import PartitionSpec as P

ITERS = 2
FSWEEPS = 3
CSWEEPS = 4
COARSEN = 4
damping = 2.0 / 3.0
keep = 1.0 - damping

NX, NY, NZ = 16, 32, 128
HF = 3
HC = 4
DEEP = 20
DEEPC = 32
CX, CY = NX // COARSEN, NY // COARSEN
EX = NX + 2 * HF
EY = 40
EC = CX + 2 * HC
ER = CY + 2 * HC
FACE = HF * NY
COARSE = FACE + (HF - 1) * NY
PER = NZ // DEEP
PLACES = [(0, k) for k in range(EX)] + [(1, k) for k in range(1, EX - 1)]
TILES = -(-len(PLACES) // PER)
ROWS = HF * (EX - 2)
VMEM = pl.BlockSpec(memory_space=pltpu.VMEM)
F32 = jnp.float32


def lanes(shape):
    return lax.broadcasted_iota(jnp.int32, shape, len(shape) - 1)


def roll(x, shift, axis=-1):
    axis = axis % x.ndim
    return pltpu.roll(x, shift % x.shape[axis], axis)


def group_sum(x):
    lane = lanes(x.shape)
    x = x + jnp.where(lane % 2 == 0, roll(x, -1), roll(x, 1))
    return x + jnp.where(lane % 4 < 2, roll(x, -2), roll(x, 2))


def merge(planes):
    lane = lanes(planes[0].shape)
    out = planes[0]
    for c in range(1, 4):
        out = jnp.where(lane % 4 == c, planes[c], out)
    return out


def unmerge(tile, planes):
    lane = lanes(tile.shape) % 4
    out = []
    for c in planes:
        moved = [roll(tile, at - c) if at != c else tile for at in range(4)]
        plane = moved[0]
        for at in range(1, 4):
            plane = jnp.where(lane == at, moved[at], plane)
        out.append(plane)
    return out


def block_sums(field, tmp):
    rows = []
    for c in range(CX):
        first, second, third, fourth = [field[COARSEN * c + k] for k in range(COARSEN)]
        tmp[c] = (first + second) + (third + fourth)
        parts = [tmp[c, pl.ds(k, CY, stride=COARSEN), :] for k in range(COARSEN)]
        rows.append((parts[0] + parts[1]) + (parts[2] + parts[3]))
    sums = group_sum(jnp.concatenate(rows, axis=0))
    return merge([sums[CY * c : CY * (c + 1)] for c in range(CX)])


def edges(x, width):
    lane = lanes(x.shape)
    return jnp.where((lane < width) | (lane >= NZ - width), x, 0.0)


def inside():
    at = lax.axis_index("gx")
    return at > 0, at < lax.axis_size("gx") - 1


def layer(k, f, own, before, after):
    if HF <= k < HF + NX:
        return own[f][k - HF]
    ref, ok, k = (before, inside()[0], k - f) if k < HF else (after, inside()[1], k - HF - NX)
    return jnp.where(ok, ref[FACE * f + NY * k : FACE * f + NY * (k + 1)], 0.0)


def tile_of(group, at, mine, before, after):
    tile = (before, mine, after)[group][at : at + CY]
    return tile if group == 1 else jnp.where(inside()[group // 2], tile, 0.0)


def with_rows(tile, low, high):
    return jnp.concatenate([low, tile, high], axis=0)


def start_kernel(bd_ref, v_ref, up_ref, down_ref, tmp):
    b_ref, d_ref = bd_ref.at[0], bd_ref.at[1]
    for i in range(NX):
        v_ref[i] = damping / (6.0 + d_ref[i])
    g = block_sums(b_ref, tmp) * 0.25
    vc = damping / (6.0 + block_sums(d_ref, tmp) * 0.25)
    for ref in (up_ref, down_ref):
        ref[COARSE : COARSE + CY] = g
        ref[COARSE + CY : COARSE + 2 * CY] = vc
    for k in range(HF):
        for ref, plane, far in ((down_ref, k, HF - 1), (up_ref, NX - HF + k, 0)):
            value, weight = b_ref[plane], v_ref[plane]
            ref[NY * k : NY * (k + 1)] = weight * value if k == far else value
            if k != far:
                at = FACE + NY * (k if ref is down_ref else k - 1)
                ref[at : at + NY] = weight


def rows_kernel(b, v, mine, before, after, up_ref, down_ref):
    for k in range(1, EX - 1):
        for f in range(2):
            plane = layer(k, f, (b, v), before, after)
            at = ROWS * f + HF * (k - 1)
            down_ref[at : at + HF] = plane[:HF]
            up_ref[at : at + HF] = plane[NY - HF :]
    for f in range(2):
        for group in range(3):
            tile = tile_of(group, COARSE + CY * f, mine, before, after)
            at = 2 * ROWS + HC * (3 * f + group)
            down_ref[at : at + HC] = tile[:HC]
            up_ref[at : at + HC] = tile[CY - HC :]


def slots(lane, width, place):
    first = (lane >= width * place) & (lane < width * (place + 1))
    last = lane >= NZ - width if place == 0 else (lane >= width * (place - 1)) & (lane < width * place)
    return first, last


def unpack(before, after, width, place):
    lane = lanes(after.shape)
    both = jnp.where(slots(lane, width, place)[0], after, before)
    return edges(roll(both, -width * place), width)


def lanes_kernel(b, v, mine, before, after, low, high, be, ve, ge, vce, up_ref, down_ref):
    for f, k in PLACES:
        out = (be, ve)[f]
        out[k, 0:8] = jnp.zeros((8, NZ), F32)
        out[k, EY - 8 : EY] = jnp.zeros((8, NZ), F32)
        out[k, 4 : 4 + NY] = layer(k, f, (b, v), before, after)
        if 0 < k < EX - 1:
            at = ROWS * f + HF * (k - 1)
            out[k, 4 - HF : 4] = low[at : at + HF]
            out[k, 4 + NY : 4 + NY + HF] = high[at : at + HF]
    lane = lanes((EY, NZ))
    for tile in range(TILES):
        up = jnp.zeros((EY, NZ), F32)
        down = jnp.zeros((EY, NZ), F32)
        for place, (f, k) in enumerate(PLACES[PER * tile : PER * (tile + 1)]):
            moved = roll((be, ve)[f][k], DEEP * place)
            first, last = slots(lane, DEEP, place)
            up = jnp.where(last, moved, up)
            down = jnp.where(first, moved, down)
        up_ref[EY * tile : EY * (tile + 1)] = up
        down_ref[EY * tile : EY * (tile + 1)] = down
    lane = lanes((ER, NZ))
    for f, out in enumerate((ge, vce)):
        up = jnp.zeros((ER, NZ), F32)
        down = jnp.zeros((ER, NZ), F32)
        for group in range(3):
            at = 2 * ROWS + HC * (3 * f + group)
            tile = tile_of(group, COARSE + CY * f, mine, before, after)
            tile = with_rows(tile, low[at : at + HC], high[at : at + HC])
            out[group] = tile
            moved = roll(tile, DEEPC * group)
            first, last = slots(lane, DEEPC, group)
            up = jnp.where(last, moved, up)
            down = jnp.where(first, moved, down)
        at = EY * TILES + ER * f
        up_ref[at : at + ER] = up
        down_ref[at : at + ER] = down


def beyond_fine(k, f, before, after):
    tile, place = divmod(PLACES.index((f, k)), PER)
    return unpack(before[EY * tile : EY * (tile + 1)], after[EY * tile : EY * (tile + 1)], DEEP, place)


def beyond_coarse(group, f, before, after):
    at = EY * TILES + ER * f
    return unpack(before[at : at + ER], after[at : at + ER], DEEPC, group)


def crossed(block, beyond, step):
    lane = lanes(block.shape)
    below, below_beyond = roll(block, step), roll(beyond, step)
    above, above_beyond = roll(block, -step), roll(beyond, -step)
    low, high = lane < step, lane >= NZ - step
    return (
        jnp.where(low, below_beyond, below) + jnp.where(high, above_beyond, above),
        jnp.where(low, below, below_beyond) + jnp.where(high, above, above_beyond),
    )


PAD = 8


def neighbours(src, k, rows, step=1):
    at = PAD
    here = [src[part, k, at : at + rows] for part in range(2)]
    along = crossed(here[0], here[1], step)
    out = []
    for part in range(2):
        beside = src[part, k - 1, at : at + rows] + src[part, k + 1, at : at + rows]
        beside = beside + (src[part, k, at - 1 : at - 1 + rows] + src[part, k, at + 1 : at + 1 + rows])
        out.append(beside + along[part])
    return here, out


def expand(coarse, part, k, lo):
    c = (k - HF) // COARSEN + HC
    first = lax.broadcasted_iota(jnp.int32, (8, NZ), 0) < 4
    groups = []
    for j in range(EY // 8):
        row = 3 + 2 * j
        a = jnp.broadcast_to(coarse[part, c, row : row + 1], (8, NZ))
        b = jnp.broadcast_to(coarse[part, c, row + 1 : row + 2], (8, NZ))
        groups.append(jnp.where(first, a, b))
    return jnp.concatenate(groups, axis=0)


def coarse_neighbours(src, group):
    at = PAD
    here = [src[part, group, at : at + ER] for part in range(2)]
    along = crossed(here[0], here[1], COARSEN)
    lane = lanes((ER, NZ)) % 4
    out = []
    for part in range(2):
        below = roll(src[part, group - 1, at : at + ER], -3) if group > 0 else 0.0
        above = roll(src[part, group + 1, at : at + ER], 3) if group < 2 else 0.0
        beside = jnp.where(lane == 0, below, roll(here[part], 1)) + jnp.where(lane == 3, above, roll(here[part], -1))
        beside = beside + (src[part, group, at - 1 : at - 1 + ER] + src[part, group, at + 1 : at + 1 + ER])
        out.append(beside + along[part])
    return here, out


def precondition(rhs, weight, crhs, cweight, fa, fb, ca, cb, coarse):
    for ref, rows in ((fa, EY), (fb, EY), (ca, ER), (cb, ER)):
        for part in range(2):
            for k in range(ref.shape[1]):
                ref[part, k, 0:PAD] = jnp.zeros((PAD, NZ), F32)
                ref[part, k, PAD + rows :] = jnp.zeros((PAD, NZ), F32)
    for group in range(3):
        for part in range(2):
            ca[part, group, PAD : PAD + ER] = cweight[part][group] * crhs[part][group]
    src, dst = ca, cb
    for sweep in range(1, CSWEEPS):
        for group in range(3):
            here, beside = coarse_neighbours(src, group)
            for part in range(2):
                new = keep * here[part] + cweight[part][group] * (crhs[part][group] + beside[part])
                dst[part, group, PAD : PAD + ER] = new
        src, dst = dst, src
    for group, planes in enumerate(((3,), (0, 1, 2, 3), (0,))):
        for part in range(2):
            for c, plane in zip(planes, unmerge(src[part, group, PAD : PAD + ER], planes)):
                coarse[part, 4 * group + c] = plane
    for k in range(EX):
        for part in range(2):
            value = rhs[part][k]
            fa[part, k, PAD : PAD + EY] = weight[part][k] * value if 0 < k < EX - 1 else value
    src, dst = fa, fb
    for sweep in range(1, FSWEEPS):
        for k in range(sweep, EX - sweep):
            here, beside = neighbours(src, k, EY)
            for part in range(2):
                new = keep * here[part] + weight[part][k] * (rhs[part][k] + beside[part])
                if sweep == FSWEEPS - 1:
                    new = new + expand(coarse, part, k, 0)
                dst[part, k, PAD : PAD + EY] = new
        src, dst = dst, src


def image_plane(src, i):
    k, at = i + HF, PAD + 4
    here = [src[part, k, at : at + NY] for part in range(2)]
    along = crossed(here[0], here[1], 1)
    out = []
    for part in range(2):
        beside = src[part, k - 1, at : at + NY] + src[part, k + 1, at : at + NY]
        beside = beside + (src[part, k, at - 1 : at - 1 + NY] + src[part, k, at + 1 : at + 1 + NY])
        out.append(beside + along[part])
    return here, out


def add_up(x):
    return (x[0:8] + x[8:16]) + (x[16:24] + x[24:32])


SHARE = NZ // 8


def store_sums(out_ref, totals, row=None):
    row = jnp.zeros((1, NZ), F32) if row is None else row
    for i, part in totals.items():
        part = jnp.sum(part, axis=0, keepdims=True)
        for step in (64, 32, 16):
            part = part + roll(part, step)
        row = jnp.where(lanes((1, NZ)) // SHARE == i, part, row)
    out_ref[...] = row


NEAR = 4
NEARC = 16


def first_kernel(
    b_ref, d_ref, b, v, gm, vcm, before, after, p_ref, q_ref, qh_ref, vh_ref, vch_ref, up_ref, down_ref, sum_ref,
    bh, fa, fb, ca, cb, coarse, tmp,
):
    for f, k in PLACES:
        (bh, vh_ref)[f][k] = beyond_fine(k, f, before, after)
    gh = [beyond_coarse(group, 0, before, after) for group in range(3)]
    for group in range(3):
        vch_ref[group] = beyond_coarse(group, 1, before, after)
    precondition((b, bh), (v, vh_ref), (gm, gh), (vcm, vch_ref), fa, fb, ca, cb, coarse)
    rp = jnp.zeros((8, NZ), F32)
    pq = jnp.zeros((8, NZ), F32)
    for i in range(NX):
        (p, ph), (beside, beside_h) = image_plane(fa, i)
        q = (6.0 + d_ref[i]) * p - beside
        weight = vh_ref[i + HF, 4 : 4 + NY]
        within = weight > 0.0
        p_ref[i] = p
        q_ref[i] = q
        qh_ref[i] = jnp.where(within, damping / jnp.where(within, weight, 1.0) * ph - beside_h, 0.0)
        rp = rp + add_up(b_ref[i] * p)
        pq = pq + add_up(p * q)
    store_sums(sum_ref, {0: rp, 1: pq})
    for part, field in enumerate((q_ref, qh_ref)):
        tile = block_sums(field, tmp) * 0.25
        if part == 1:
            tile = roll(tile, NEARC)
        for ref in (up_ref, down_ref):
            ref[FACE + NY + CY * part : FACE + NY + CY * (part + 1)] = tile
    lane = lanes((NY, NZ))
    for ref, first, far in ((down_ref, 0, HF - 1), (up_ref, NX - HF, 0)):
        packed = jnp.zeros((NY, NZ), F32)
        for k in range(HF):
            value, beyond = q_ref[first + k], qh_ref[first + k]
            if k == far:
                value = value * v[HF + first + k, 4 : 4 + NY]
                beyond = beyond * vh_ref[HF + first + k, 4 : 4 + NY]
            ref[NY * k : NY * (k + 1)] = value
            packed = jnp.where(lane // (2 * NEAR) == k, roll(beyond, NEAR + 2 * NEAR * k), packed)
        ref[FACE : FACE + NY] = packed


def layer_beyond(k, own, before, after):
    if HF <= k < HF + NX:
        return own[k - HF]
    ref, ok, k = (before, inside()[0], k) if k < HF else (after, inside()[1], k - HF - NX)
    return jnp.where(ok, edges(roll(ref[FACE : FACE + NY], -NEAR - 2 * NEAR * k), NEAR), 0.0)


SIDE = NZ // (2 * NEAR)
WIDE = ROWS + 3 * HC


def second_rows_kernel(q, qh, mine, before, after, up_ref, down_ref):
    for k in range(1, EX - 1):
        plane = layer(k, 0, (q,), before, after)
        at = HF * (k - 1)
        down_ref[at : at + HF] = plane[:HF]
        up_ref[at : at + HF] = plane[NY - HF :]
    lane = lanes((8, NZ))
    wide = jnp.zeros((8, NZ), F32)
    for group in range(3):
        tile = tile_of(group, FACE + NY, mine, before, after)
        beyond = tile_of(group, FACE + NY + CY, mine, before, after)
        wide = jnp.where(lane // (2 * NEARC) == group, roll(beyond, 2 * NEARC * group), wide)
        at = ROWS + HC * group
        down_ref[at : at + HC] = tile[:HC]
        up_ref[at : at + HC] = tile[CY - HC :]
    for ref, rows in ((up_ref, slice(NY - 8, NY)), (down_ref, slice(0, 8))):
        ref[WIDE + 16 : WIDE + 24] = wide
        for half in range(2):
            packed = jnp.zeros((8, NZ), F32)
            for k in range(SIDE * half, min(EX, SIDE * (half + 1))):
                plane = layer_beyond(k, qh, before, after)[rows]
                packed = jnp.where(lane // (2 * NEAR) == k % SIDE, roll(plane, NEAR + 2 * NEAR * (k % SIDE)), packed)
            ref[WIDE + 8 * half : WIDE + 8 * (half + 1)] = packed


def second_kernel(
    b_ref, d_ref, p_ref, q_ref, qh_ref, v, vh_ref, vcm, vch, mine, before, after, low, high, first_ref,
    m_ref, im_ref, sum_ref, q, qh, fa, fb, ca, cb, coarse,
):
    for k in range(EX):
        at, place = HF * (k - 1), -NEAR - 2 * NEAR * (k % SIDE)
        for out in (q, qh):
            out[k, 0:8] = jnp.zeros((8, NZ), F32)
            out[k, EY - 8 : EY] = jnp.zeros((8, NZ), F32)
        q[k, 4 : 4 + NY] = layer(k, 0, (q_ref,), before, after)
        if 0 < k < EX - 1:
            q[k, 4 - HF : 4] = low[at : at + HF]
            q[k, 4 + NY : 4 + NY + HF] = high[at : at + HF]
        tile = slice(WIDE + 8 * (k // SIDE), WIDE + 8 * (k // SIDE + 1))
        qh[k, 4 - HF : 4] = edges(roll(low[tile], place), NEAR)[8 - HF :]
        qh[k, 4 : 4 + NY] = layer_beyond(k, qh_ref, before, after)
        qh[k, 4 + NY : 4 + NY + HF] = edges(roll(high[tile], place), NEAR)[:HF]
    g, gh = [], []
    for group in range(3):
        at, row = FACE + NY, ROWS + HC * group
        tile = with_rows(tile_of(group, at, mine, before, after), low[row : row + HC], high[row : row + HC])
        wide = [roll(ref[WIDE + 16 : WIDE + 24], -2 * NEARC * group) for ref in (low, high)]
        beyond = tile_of(group, at + CY, mine, before, after)
        beyond = with_rows(beyond, wide[0][CY - HC :], wide[1][:HC])
        g.append(tile)
        gh.append(edges(roll(beyond, -NEARC), NEARC))
    precondition((q, qh), (v, vh_ref), (g, gh), (vcm, vch), fa, fb, ca, cb, coarse)
    sums = [jnp.zeros((8, NZ), F32)] * 4
    for i in range(NX):
        (m, _), (beside, _) = image_plane(fa, i)
        im = (6.0 + d_ref[i]) * m - beside
        m_ref[i] = m
        im_ref[i] = im
        pairs = ((q_ref[i], m), (b_ref[i], m), (p_ref[i], im), (m, im))
        sums = [s + add_up(x * y) for s, (x, y) in zip(sums, pairs)]
    store_sums(sum_ref, dict(enumerate(sums, 2)), first_ref[...])


PARTS = 4


def last_kernel(b_ref, p_ref, q_ref, m_ref, im_ref, sum_ref, x_out, r_out, x_ref, r_ref, sems):
    rp, pq, qm, rm, pim, mim = [
        jnp.sum(jnp.where(lanes((1, NZ)) // SHARE == i, sum_ref[...], 0.0), axis=1, keepdims=True) for i in range(6)
    ]
    alpha = rp / pq
    rho = rp - alpha * (pq + rm) + alpha * alpha * qm
    scale = 1.0 + rho / rp
    alpha_next = rho / (scale * scale * pq - scale * alpha * (pim + qm) + alpha * alpha * mim)
    along = alpha + alpha_next * scale
    across = alpha_next * alpha
    copies = []
    for part in range(PARTS):
        planes = range(NX // PARTS * part, NX // PARTS * (part + 1))
        for i in planes:
            x_ref[i] = along * p_ref[i] - across * m_ref[i]
            r_ref[i] = b_ref[i] - along * q_ref[i] + across * im_ref[i]
        at = pl.ds(planes[0], len(planes))
        for which, (src, dst) in enumerate(((x_ref, x_out), (r_ref, r_out))):
            copies.append(pltpu.make_async_copy(src.at[at], dst.at[at], sems.at[2 * part + which]))
            copies[-1].start()
    for copy in copies:
        copy.wait()


def call(kernel, outs, scratch=(), name=None, out_space=pltpu.VMEM):
    def run(*args):
        return pl.pallas_call(
            kernel,
            out_shape=[jax.ShapeDtypeStruct(shape, F32) for shape in outs],
            in_specs=[VMEM] * len(args),
            out_specs=[pl.BlockSpec(memory_space=out_space)] * len(outs),
            scratch_shapes=[pltpu.VMEM(shape, F32) if isinstance(shape, tuple) else shape for shape in scratch],
            compiler_params=pltpu.CompilerParams(vmem_limit_bytes=24 * 2**20),
            name=name,
        )(*args)

    return run


def both_ways(up, down, axis):
    count = lax.axis_size(axis)
    steps = [(i, (i + 1) % count) for i in range(count if axis == "gx" else count - 1)]
    before = lax.ppermute(up, axis, steps)
    after = lax.ppermute(down, axis, [(j, i) for i, j in steps])
    return before, after


def total(x, axis):
    count = math.prod(lax.axis_size(name) for name in axis)
    spread = jnp.broadcast_to(x[None], (count,) + x.shape)
    return jnp.sum(lax.all_to_all(spread, axis, 0, 0, tiled=True), axis=0)


def on_device(b, d):
    block, fine, tiles = (NX, NY, NZ), (EX, EY, NZ), (3, ER, NZ)
    work = [(2, EX, EY + 2 * PAD, NZ)] * 2 + [(2, 3, ER + 2 * PAD, NZ)] * 2 + [(2, EC, ER, NZ)]
    bd = lax.optimization_barrier(jnp.stack([b, d]))
    v, up, down = call(start_kernel, [block] + [(COARSE + 2 * CY, NZ)] * 2, [(CX, NY, NZ)], name="start")(bd)
    mine = up
    before, after = both_ways(up, down, "gx")
    up, down = call(rows_kernel, [(2 * ROWS + 6 * HC, NZ)] * 2, name="rows")(b, v, mine, before, after)
    low, high = both_ways(up, down, "gy")
    be, ve, gm, vcm, up, down = call(
        lanes_kernel, [fine] * 2 + [tiles] * 2 + [(EY * TILES + 2 * ER, NZ)] * 2, name="lanes"
    )(b, v, mine, before, after, low, high)
    before, after = both_ways(up, down, "gz")
    p, q, qh, vh, vch, up, down, sums = call(
        first_kernel,
        [block] * 3 + [fine, tiles] + [(FACE + NY + 2 * CY, NZ)] * 2 + [(1, NZ)],
        [fine] + work + [(CX, NY, NZ)],
        name="first",
    )(b, d, be, ve, gm, vcm, before, after)
    mine = up
    before, after = both_ways(up, down, "gx")
    up, down = call(second_rows_kernel, [(WIDE + 24, NZ)] * 2, name="second_rows")(q, qh, mine, before, after)
    low, high = both_ways(up, down, "gy")
    m, im, sums = call(second_kernel, [block, block, (1, NZ)], [fine, fine] + work, name="second")(
        b, d, p, q, qh, ve, vh, vcm, vch, mine, before, after, low, high, sums
    )
    for axis in (("gy", "gz"), ("gx",)):
        sums = total(sums, axis)
    return call(
        last_kernel,
        [block, block],
        [block, block, pltpu.SemaphoreType.DMA((2 * PARTS,))],
        name="last",
        out_space=pl.ANY,
    )(b, p, q, m, im, sums)


def solution(mesh):
    spec = P("gx", "gy", "gz")
    return jax.shard_map(on_device, mesh=mesh, in_specs=(spec, spec), out_specs=(spec, spec), check_vma=False)
```

```python
import functools
import math

import jax
import jax.numpy as jnp
from jax import lax
from jax.experimental import pallas as pl
from jax.experimental.pallas import tpu as pltpu
from jax.sharding import PartitionSpec as P

ITERS = 2
FSWEEPS = 3
CSWEEPS = 4
COARSEN = 4
damping = 2.0 / 3.0
keep = 1.0 - damping

NX, NY, NZ = 16, 32, 128
HF = 3
HC = 4
DEEP = 20
DEEPC = 32
CX, CY = NX // COARSEN, NY // COARSEN
EX = NX + 2 * HF
EY = 40
EC = CX + 2 * HC
ER = CY + 2 * HC
FACE = HF * NY
COARSE = FACE + (HF - 1) * NY
PER = NZ // DEEP
PLACES = [(0, k) for k in range(EX)] + [(1, k) for k in range(1, EX - 1)]
TILES = -(-len(PLACES) // PER)
ROWS = HF * (EX - 2)
VMEM = pl.BlockSpec(memory_space=pltpu.VMEM)
F32 = jnp.float32


def lanes(shape):
    return lax.broadcasted_iota(jnp.int32, shape, len(shape) - 1)


def roll(x, shift, axis=-1):
    axis = axis % x.ndim
    return pltpu.roll(x, shift % x.shape[axis], axis)


def group_sum(x):
    lane = lanes(x.shape)
    x = x + jnp.where(lane % 2 == 0, roll(x, -1), roll(x, 1))
    return x + jnp.where(lane % 4 < 2, roll(x, -2), roll(x, 2))


def merge(planes):
    lane = lanes(planes[0].shape)
    out = planes[0]
    for c in range(1, 4):
        out = jnp.where(lane % 4 == c, planes[c], out)
    return out


def unmerge(tile, planes):
    lane = lanes(tile.shape) % 4
    out = []
    for c in planes:
        moved = [roll(tile, at - c) if at != c else tile for at in range(4)]
        plane = moved[0]
        for at in range(1, 4):
            plane = jnp.where(lane == at, moved[at], plane)
        out.append(plane)
    return out


def block_sums(field, tmp):
    rows = []
    for c in range(CX):
        first, second, third, fourth = [field[COARSEN * c + k] for k in range(COARSEN)]
        tmp[c] = (first + second) + (third + fourth)
        parts = [tmp[c, pl.ds(k, CY, stride=COARSEN), :] for k in range(COARSEN)]
        rows.append((parts[0] + parts[1]) + (parts[2] + parts[3]))
    sums = group_sum(jnp.concatenate(rows, axis=0))
    return merge([sums[CY * c : CY * (c + 1)] for c in range(CX)])


def edges(x, width):
    lane = lanes(x.shape)
    return jnp.where((lane < width) | (lane >= NZ - width), x, 0.0)


def inside():
    at = lax.axis_index("gx")
    return at > 0, at < lax.axis_size("gx") - 1


def layer(k, f, own, before, after):
    if HF <= k < HF + NX:
        return own[f][k - HF]
    ref, ok, k = (before, inside()[0], k - f) if k < HF else (after, inside()[1], k - HF - NX)
    return jnp.where(ok, ref[FACE * f + NY * k : FACE * f + NY * (k + 1)], 0.0)


def tile_of(group, at, mine, before, after):
    tile = (before, mine, after)[group][at : at + CY]
    return tile if group == 1 else jnp.where(inside()[group // 2], tile, 0.0)


def with_rows(tile, low, high):
    return jnp.concatenate([low, tile, high], axis=0)


def start_kernel(bd_ref, v_ref, up_ref, down_ref, tmp):
    b_ref, d_ref = bd_ref.at[0], bd_ref.at[1]
    for i in range(NX):
        v_ref[i] = damping / (6.0 + d_ref[i])
    g = block_sums(b_ref, tmp) * 0.25
    vc = damping / (6.0 + block_sums(d_ref, tmp) * 0.25)
    for ref in (up_ref, down_ref):
        ref[COARSE : COARSE + CY] = g
        ref[COARSE + CY : COARSE + 2 * CY] = vc
    for k in range(HF):
        for ref, plane, far in ((down_ref, k, HF - 1), (up_ref, NX - HF + k, 0)):
            value, weight = b_ref[plane], v_ref[plane]
            ref[NY * k : NY * (k + 1)] = weight * value if k == far else value
            if k != far:
                at = FACE + NY * (k if ref is down_ref else k - 1)
                ref[at : at + NY] = weight


def rows_kernel(b, v, mine, before, after, up_ref, down_ref):
    for k in range(1, EX - 1):
        for f in range(2):
            plane = layer(k, f, (b, v), before, after)
            at = ROWS * f + HF * (k - 1)
            down_ref[at : at + HF] = plane[:HF]
            up_ref[at : at + HF] = plane[NY - HF :]
    for f in range(2):
        for group in range(3):
            tile = tile_of(group, COARSE + CY * f, mine, before, after)
            at = 2 * ROWS + HC * (3 * f + group)
            down_ref[at : at + HC] = tile[:HC]
            up_ref[at : at + HC] = tile[CY - HC :]


def slots(lane, width, place):
    first = (lane >= width * place) & (lane < width * (place + 1))
    last = lane >= NZ - width if place == 0 else (lane >= width * (place - 1)) & (lane < width * place)
    return first, last


def unpack(before, after, width, place):
    lane = lanes(after.shape)
    both = jnp.where(slots(lane, width, place)[0], after, before)
    return edges(roll(both, -width * place), width)


def lanes_kernel(b, v, mine, before, after, low, high, be, ve, ge, vce, up_ref, down_ref):
    for f, k in PLACES:
        out = (be, ve)[f]
        out[k, 0:8] = jnp.zeros((8, NZ), F32)
        out[k, EY - 8 : EY] = jnp.zeros((8, NZ), F32)
        out[k, 4 : 4 + NY] = layer(k, f, (b, v), before, after)
        if 0 < k < EX - 1:
            at = ROWS * f + HF * (k - 1)
            out[k, 4 - HF : 4] = low[at : at + HF]
            out[k, 4 + NY : 4 + NY + HF] = high[at : at + HF]
    lane = lanes((EY, NZ))
    for tile in range(TILES):
        up = jnp.zeros((EY, NZ), F32)
        down = jnp.zeros((EY, NZ), F32)
        for place, (f, k) in enumerate(PLACES[PER * tile : PER * (tile + 1)]):
            moved = roll((be, ve)[f][k], DEEP * place)
            first, last = slots(lane, DEEP, place)
            up = jnp.where(last, moved, up)
            down = jnp.where(first, moved, down)
        up_ref[EY * tile : EY * (tile + 1)] = up
        down_ref[EY * tile : EY * (tile + 1)] = down
    lane = lanes((ER, NZ))
    for f, out in enumerate((ge, vce)):
        up = jnp.zeros((ER, NZ), F32)
        down = jnp.zeros((ER, NZ), F32)
        for group in range(3):
            at = 2 * ROWS + HC * (3 * f + group)
            tile = tile_of(group, COARSE + CY * f, mine, before, after)
            tile = with_rows(tile, low[at : at + HC], high[at : at + HC])
            out[group] = tile
            moved = roll(tile, DEEPC * group)
            first, last = slots(lane, DEEPC, group)
            up = jnp.where(last, moved, up)
            down = jnp.where(first, moved, down)
        at = EY * TILES + ER * f
        up_ref[at : at + ER] = up
        down_ref[at : at + ER] = down


def beyond_fine(k, f, before, after):
    tile, place = divmod(PLACES.index((f, k)), PER)
    return unpack(before[EY * tile : EY * (tile + 1)], after[EY * tile : EY * (tile + 1)], DEEP, place)


def beyond_coarse(group, f, before, after):
    at = EY * TILES + ER * f
    return unpack(before[at : at + ER], after[at : at + ER], DEEPC, group)


def crossed(block, beyond, step):
    lane = lanes(block.shape)
    below, below_beyond = roll(block, step), roll(beyond, step)
    above, above_beyond = roll(block, -step), roll(beyond, -step)
    low, high = lane < step, lane >= NZ - step
    return (
        jnp.where(low, below_beyond, below) + jnp.where(high, above_beyond, above),
        jnp.where(low, below, below_beyond) + jnp.where(high, above, above_beyond),
    )


PAD = 8


def neighbours(src, k, rows, step=1):
    at = PAD
    here = [src[part, k, at : at + rows] for part in range(2)]
    along = crossed(here[0], here[1], step)
    out = []
    for part in range(2):
        beside = src[part, k - 1, at : at + rows] + src[part, k + 1, at : at + rows]
        beside = beside + (src[part, k, at - 1 : at - 1 + rows] + src[part, k, at + 1 : at + 1 + rows])
        out.append(beside + along[part])
    return here, out


def expand(coarse, part, k, lo):
    c = (k - HF) // COARSEN + HC
    first = lax.broadcasted_iota(jnp.int32, (8, NZ), 0) < 4
    groups = []
    for j in range(EY // 8):
        row = 3 + 2 * j
        a = jnp.broadcast_to(coarse[part, c, row : row + 1], (8, NZ))
        b = jnp.broadcast_to(coarse[part, c, row + 1 : row + 2], (8, NZ))
        groups.append(jnp.where(first, a, b))
    return jnp.concatenate(groups, axis=0)


def coarse_neighbours(src, group):
    at = PAD
    here = [src[part, group, at : at + ER] for part in range(2)]
    along = crossed(here[0], here[1], COARSEN)
    lane = lanes((ER, NZ)) % 4
    out = []
    for part in range(2):
        below = roll(src[part, group - 1, at : at + ER], -3) if group > 0 else 0.0
        above = roll(src[part, group + 1, at : at + ER], 3) if group < 2 else 0.0
        beside = jnp.where(lane == 0, below, roll(here[part], 1)) + jnp.where(lane == 3, above, roll(here[part], -1))
        beside = beside + (src[part, group, at - 1 : at - 1 + ER] + src[part, group, at + 1 : at + 1 + ER])
        out.append(beside + along[part])
    return here, out


def precondition(rhs, weight, crhs, cweight, fa, fb, ca, cb, coarse):
    for ref, rows in ((fa, EY), (fb, EY), (ca, ER), (cb, ER)):
        for part in range(2):
            for k in range(ref.shape[1]):
                ref[part, k, 0:PAD] = jnp.zeros((PAD, NZ), F32)
                ref[part, k, PAD + rows :] = jnp.zeros((PAD, NZ), F32)
    for group in range(3):
        for part in range(2):
            ca[part, group, PAD : PAD + ER] = cweight[part][group] * crhs[part][group]
    src, dst = ca, cb
    for sweep in range(1, CSWEEPS):
        for group in range(3):
            here, beside = coarse_neighbours(src, group)
            for part in range(2):
                new = keep * here[part] + cweight[part][group] * (crhs[part][group] + beside[part])
                dst[part, group, PAD : PAD + ER] = new
        src, dst = dst, src
    for group, planes in enumerate(((3,), (0, 1, 2, 3), (0,))):
        for part in range(2):
            for c, plane in zip(planes, unmerge(src[part, group, PAD : PAD + ER], planes)):
                coarse[part, 4 * group + c] = plane
    for k in range(EX):
        for part in range(2):
            value = rhs[part][k]
            fa[part, k, PAD : PAD + EY] = weight[part][k] * value if 0 < k < EX - 1 else value
    src, dst = fa, fb
    for sweep in range(1, FSWEEPS):
        for k in range(sweep, EX - sweep):
            here, beside = neighbours(src, k, EY)
            for part in range(2):
                new = keep * here[part] + weight[part][k] * (rhs[part][k] + beside[part])
                if sweep == FSWEEPS - 1:
                    new = new + expand(coarse, part, k, 0)
                dst[part, k, PAD : PAD + EY] = new
        src, dst = dst, src


def image_plane(src, i):
    k, at = i + HF, PAD + 4
    here = [src[part, k, at : at + NY] for part in range(2)]
    along = crossed(here[0], here[1], 1)
    out = []
    for part in range(2):
        beside = src[part, k - 1, at : at + NY] + src[part, k + 1, at : at + NY]
        beside = beside + (src[part, k, at - 1 : at - 1 + NY] + src[part, k, at + 1 : at + 1 + NY])
        out.append(beside + along[part])
    return here, out


def add_up(x):
    return (x[0:8] + x[8:16]) + (x[16:24] + x[24:32])


SHARE = NZ // 8


def store_sums(out_ref, totals, row=None):
    row = jnp.zeros((1, NZ), F32) if row is None else row
    for i, part in totals.items():
        part = jnp.sum(part, axis=0, keepdims=True)
        for step in (64, 32, 16):
            part = part + roll(part, step)
        row = jnp.where(lanes((1, NZ)) // SHARE == i, part, row)
    out_ref[...] = row


NEAR = 4
NEARC = 16


def first_kernel(
    b_ref, d_ref, b, v, gm, vcm, before, after, p_ref, q_ref, qh_ref, vh_ref, vch_ref, up_ref, down_ref, sum_ref,
    bh, fa, fb, ca, cb, coarse, tmp,
):
    for f, k in PLACES:
        (bh, vh_ref)[f][k] = beyond_fine(k, f, before, after)
    gh = [beyond_coarse(group, 0, before, after) for group in range(3)]
    for group in range(3):
        vch_ref[group] = beyond_coarse(group, 1, before, after)
    precondition((b, bh), (v, vh_ref), (gm, gh), (vcm, vch_ref), fa, fb, ca, cb, coarse)
    rp = jnp.zeros((8, NZ), F32)
    pq = jnp.zeros((8, NZ), F32)
    for i in range(NX):
        (p, ph), (beside, beside_h) = image_plane(fa, i)
        q = (6.0 + d_ref[i]) * p - beside
        weight = vh_ref[i + HF, 4 : 4 + NY]
        within = weight > 0.0
        p_ref[i] = p
        q_ref[i] = q
        qh_ref[i] = jnp.where(within, damping / jnp.where(within, weight, 1.0) * ph - beside_h, 0.0)
        rp = rp + add_up(b_ref[i] * p)
        pq = pq + add_up(p * q)
    store_sums(sum_ref, {0: rp, 1: pq})
    for part, field in enumerate((q_ref, qh_ref)):
        tile = block_sums(field, tmp) * 0.25
        if part == 1:
            tile = roll(tile, NEARC)
        for ref in (up_ref, down_ref):
            ref[FACE + NY + CY * part : FACE + NY + CY * (part + 1)] = tile
    lane = lanes((NY, NZ))
    for ref, first, far in ((down_ref, 0, HF - 1), (up_ref, NX - HF, 0)):
        packed = jnp.zeros((NY, NZ), F32)
        for k in range(HF):
            value, beyond = q_ref[first + k], qh_ref[first + k]
            if k == far:
                value = value * v[HF + first + k, 4 : 4 + NY]
                beyond = beyond * vh_ref[HF + first + k, 4 : 4 + NY]
            ref[NY * k : NY * (k + 1)] = value
            packed = jnp.where(lane // (2 * NEAR) == k, roll(beyond, NEAR + 2 * NEAR * k), packed)
        ref[FACE : FACE + NY] = packed


def layer_beyond(k, own, before, after):
    if HF <= k < HF + NX:
        return own[k - HF]
    ref, ok, k = (before, inside()[0], k) if k < HF else (after, inside()[1], k - HF - NX)
    return jnp.where(ok, edges(roll(ref[FACE : FACE + NY], -NEAR - 2 * NEAR * k), NEAR), 0.0)


SIDE = NZ // (2 * NEAR)
WIDE = ROWS + 3 * HC


def second_rows_kernel(q, qh, mine, before, after, up_ref, down_ref):
    for k in range(1, EX - 1):
        plane = layer(k, 0, (q,), before, after)
        at = HF * (k - 1)
        down_ref[at : at + HF] = plane[:HF]
        up_ref[at : at + HF] = plane[NY - HF :]
    lane = lanes((8, NZ))
    wide = jnp.zeros((8, NZ), F32)
    for group in range(3):
        tile = tile_of(group, FACE + NY, mine, before, after)
        beyond = tile_of(group, FACE + NY + CY, mine, before, after)
        wide = jnp.where(lane // (2 * NEARC) == group, roll(beyond, 2 * NEARC * group), wide)
        at = ROWS + HC * group
        down_ref[at : at + HC] = tile[:HC]
        up_ref[at : at + HC] = tile[CY - HC :]
    for ref, rows in ((up_ref, slice(NY - 8, NY)), (down_ref, slice(0, 8))):
        ref[WIDE + 16 : WIDE + 24] = wide
        for half in range(2):
            packed = jnp.zeros((8, NZ), F32)
            for k in range(SIDE * half, min(EX, SIDE * (half + 1))):
                plane = layer_beyond(k, qh, before, after)[rows]
                packed = jnp.where(lane // (2 * NEAR) == k % SIDE, roll(plane, NEAR + 2 * NEAR * (k % SIDE)), packed)
            ref[WIDE + 8 * half : WIDE + 8 * (half + 1)] = packed


def second_kernel(
    b_ref, d_ref, p_ref, q_ref, qh_ref, v, vh_ref, vcm, vch, mine, before, after, low, high, first_ref,
    m_ref, im_ref, sum_ref, q, qh, fa, fb, ca, cb, coarse,
):
    for k in range(EX):
        at, place = HF * (k - 1), -NEAR - 2 * NEAR * (k % SIDE)
        for out in (q, qh):
            out[k, 0:8] = jnp.zeros((8, NZ), F32)
            out[k, EY - 8 : EY] = jnp.zeros((8, NZ), F32)
        q[k, 4 : 4 + NY] = layer(k, 0, (q_ref,), before, after)
        if 0 < k < EX - 1:
            q[k, 4 - HF : 4] = low[at : at + HF]
            q[k, 4 + NY : 4 + NY + HF] = high[at : at + HF]
        tile = slice(WIDE + 8 * (k // SIDE), WIDE + 8 * (k // SIDE + 1))
        qh[k, 4 - HF : 4] = edges(roll(low[tile], place), NEAR)[8 - HF :]
        qh[k, 4 : 4 + NY] = layer_beyond(k, qh_ref, before, after)
        qh[k, 4 + NY : 4 + NY + HF] = edges(roll(high[tile], place), NEAR)[:HF]
    g, gh = [], []
    for group in range(3):
        at, row = FACE + NY, ROWS + HC * group
        tile = with_rows(tile_of(group, at, mine, before, after), low[row : row + HC], high[row : row + HC])
        wide = [roll(ref[WIDE + 16 : WIDE + 24], -2 * NEARC * group) for ref in (low, high)]
        beyond = tile_of(group, at + CY, mine, before, after)
        beyond = with_rows(beyond, wide[0][CY - HC :], wide[1][:HC])
        g.append(tile)
        gh.append(edges(roll(beyond, -NEARC), NEARC))
    precondition((q, qh), (v, vh_ref), (g, gh), (vcm, vch), fa, fb, ca, cb, coarse)
    sums = [jnp.zeros((8, NZ), F32)] * 4
    for i in range(NX):
        (m, _), (beside, _) = image_plane(fa, i)
        im = (6.0 + d_ref[i]) * m - beside
        m_ref[i] = m
        im_ref[i] = im
        pairs = ((q_ref[i], m), (b_ref[i], m), (p_ref[i], im), (m, im))
        sums = [s + add_up(x * y) for s, (x, y) in zip(sums, pairs)]
    store_sums(sum_ref, dict(enumerate(sums, 2)), first_ref[...])


PARTS = 4


def last_kernel(b_ref, p_ref, q_ref, m_ref, im_ref, sum_ref, x_out, r_out, x_ref, r_ref, sems):
    rp, pq, qm, rm, pim, mim = [
        jnp.sum(jnp.where(lanes((1, NZ)) // SHARE == i, sum_ref[...], 0.0), axis=1, keepdims=True) for i in range(6)
    ]
    alpha = rp / pq
    rho = rp - alpha * (pq + rm) + alpha * alpha * qm
    scale = 1.0 + rho / rp
    alpha_next = rho / (scale * scale * pq - scale * alpha * (pim + qm) + alpha * alpha * mim)
    along = alpha + alpha_next * scale
    across = alpha_next * alpha
    copies = []
    for part in range(PARTS):
        planes = range(NX // PARTS * part, NX // PARTS * (part + 1))
        for i in planes:
            x_ref[i] = along * p_ref[i] - across * m_ref[i]
            r_ref[i] = b_ref[i] - along * q_ref[i] + across * im_ref[i]
        at = pl.ds(planes[0], len(planes))
        for which, (src, dst) in enumerate(((x_ref, x_out), (r_ref, r_out))):
            copies.append(pltpu.make_async_copy(src.at[at], dst.at[at], sems.at[2 * part + which]))
            copies[-1].start()
    for copy in copies:
        copy.wait()


def call(kernel, outs, scratch=(), name=None, out_space=pltpu.VMEM):
    def run(*args):
        return pl.pallas_call(
            kernel,
            out_shape=[jax.ShapeDtypeStruct(shape, F32) for shape in outs],
            in_specs=[VMEM] * len(args),
            out_specs=[pl.BlockSpec(memory_space=out_space)] * len(outs),
            scratch_shapes=[pltpu.VMEM(shape, F32) if isinstance(shape, tuple) else shape for shape in scratch],
            compiler_params=pltpu.CompilerParams(vmem_limit_bytes=24 * 2**20),
            name=name,
        )(*args)

    return run


def both_ways(up, down, axis):
    count = lax.axis_size(axis)
    steps = [(i, (i + 1) % count) for i in range(count if axis == "gx" else count - 1)]
    before = lax.ppermute(up, axis, steps)
    after = lax.ppermute(down, axis, [(j, i) for i, j in steps])
    return before, after


def total(x, axis):
    count = math.prod(lax.axis_size(name) for name in axis)
    spread = jnp.broadcast_to(x[None], (count,) + x.shape)
    return jnp.sum(lax.all_to_all(spread, axis, 0, 0, tiled=True), axis=0)


def on_device(b, d):
    block, fine, tiles = (NX, NY, NZ), (EX, EY, NZ), (3, ER, NZ)
    work = [(2, EX, EY + 2 * PAD, NZ)] * 2 + [(2, 3, ER + 2 * PAD, NZ)] * 2 + [(2, EC, ER, NZ)]
    bd = lax.optimization_barrier(jnp.stack([b, d]))
    v, up, down = call(start_kernel, [block] + [(COARSE + 2 * CY, NZ)] * 2, [(CX, NY, NZ)], name="start")(bd)
    mine = up
    before, after = both_ways(up, down, "gx")
    up, down = call(rows_kernel, [(2 * ROWS + 6 * HC, NZ)] * 2, name="rows")(b, v, mine, before, after)
    low, high = both_ways(up, down, "gy")
    be, ve, gm, vcm, up, down = call(
        lanes_kernel, [fine] * 2 + [tiles] * 2 + [(EY * TILES + 2 * ER, NZ)] * 2, name="lanes"
    )(b, v, mine, before, after, low, high)
    before, after = both_ways(up, down, "gz")
    p, q, qh, vh, vch, up, down, sums = call(
        first_kernel,
        [block] * 3 + [fine, tiles] + [(FACE + NY + 2 * CY, NZ)] * 2 + [(1, NZ)],
        [fine] + work + [(CX, NY, NZ)],
        name="first",
    )(b, d, be, ve, gm, vcm, before, after)
    mine = up
    before, after = both_ways(up, down, "gx")
    up, down = call(second_rows_kernel, [(WIDE + 24, NZ)] * 2, name="second_rows")(q, qh, mine, before, after)
    low, high = both_ways(up, down, "gy")
    m, im, sums = call(second_kernel, [block, block, (1, NZ)], [fine, fine] + work, name="second")(
        b, d, p, q, qh, ve, vh, vcm, vch, mine, before, after, low, high, sums
    )
    for axis in (("gx",), ("gy", "gz")):
        sums = total(sums, axis)
    return call(
        last_kernel,
        [block, block],
        [block, block, pltpu.SemaphoreType.DMA((2 * PARTS,))],
        name="last",
        out_space=pl.ANY,
    )(b, p, q, m, im, sums)


def solution(mesh):
    spec = P("gx", "gy", "gz")
    return jax.shard_map(on_device, mesh=mesh, in_specs=(spec, spec), out_specs=(spec, spec), check_vma=False)
```

```python
import functools
import math

import jax
import jax.numpy as jnp
from jax import lax
from jax.experimental import pallas as pl
from jax.experimental.pallas import tpu as pltpu
from jax.sharding import PartitionSpec as P

ITERS = 2
FSWEEPS = 3
CSWEEPS = 4
COARSEN = 4
damping = 2.0 / 3.0
keep = 1.0 - damping

NX, NY, NZ = 16, 32, 128
HF = 3
HC = 4
DEEP = 20
DEEPC = 32
CX, CY = NX // COARSEN, NY // COARSEN
EX = NX + 2 * HF
EY = 40
EC = CX + 2 * HC
ER = CY + 2 * HC
FACE = HF * NY
COARSE = FACE + (HF - 1) * NY
PER = NZ // DEEP
PLACES = [(0, k) for k in range(EX)] + [(1, k) for k in range(1, EX - 1)]
TILES = -(-len(PLACES) // PER)
ROWS = HF * (EX - 2)
VMEM = pl.BlockSpec(memory_space=pltpu.VMEM)
F32 = jnp.float32


def lanes(shape):
    return lax.broadcasted_iota(jnp.int32, shape, len(shape) - 1)


def roll(x, shift, axis=-1):
    axis = axis % x.ndim
    return pltpu.roll(x, shift % x.shape[axis], axis)


def group_sum(x):
    lane = lanes(x.shape)
    x = x + jnp.where(lane % 2 == 0, roll(x, -1), roll(x, 1))
    return x + jnp.where(lane % 4 < 2, roll(x, -2), roll(x, 2))


def merge(planes):
    lane = lanes(planes[0].shape)
    out = planes[0]
    for c in range(1, 4):
        out = jnp.where(lane % 4 == c, planes[c], out)
    return out


def unmerge(tile, planes):
    lane = lanes(tile.shape) % 4
    out = []
    for c in planes:
        moved = [roll(tile, at - c) if at != c else tile for at in range(4)]
        plane = moved[0]
        for at in range(1, 4):
            plane = jnp.where(lane == at, moved[at], plane)
        out.append(plane)
    return out


def block_sums(field, tmp):
    rows = []
    for c in range(CX):
        first, second, third, fourth = [field[COARSEN * c + k] for k in range(COARSEN)]
        tmp[c] = (first + second) + (third + fourth)
        parts = [tmp[c, pl.ds(k, CY, stride=COARSEN), :] for k in range(COARSEN)]
        rows.append((parts[0] + parts[1]) + (parts[2] + parts[3]))
    sums = group_sum(jnp.concatenate(rows, axis=0))
    return merge([sums[CY * c : CY * (c + 1)] for c in range(CX)])


def edges(x, width):
    lane = lanes(x.shape)
    return jnp.where((lane < width) | (lane >= NZ - width), x, 0.0)


def inside():
    at = lax.axis_index("gx")
    return at > 0, at < lax.axis_size("gx") - 1


def layer(k, f, own, before, after):
    if HF <= k < HF + NX:
        return own[f][k - HF]
    ref, ok, k = (before, inside()[0], k - f) if k < HF else (after, inside()[1], k - HF - NX)
    return jnp.where(ok, ref[FACE * f + NY * k : FACE * f + NY * (k + 1)], 0.0)


def tile_of(group, at, mine, before, after):
    tile = (before, mine, after)[group][at : at + CY]
    return tile if group == 1 else jnp.where(inside()[group // 2], tile, 0.0)


def with_rows(tile, low, high):
    return jnp.concatenate([low, tile, high], axis=0)


def start_kernel(bd_ref, v_ref, up_ref, down_ref, tmp):
    b_ref, d_ref = bd_ref.at[0], bd_ref.at[1]
    for i in range(NX):
        v_ref[i] = damping / (6.0 + d_ref[i])
    g = block_sums(b_ref, tmp) * 0.25
    vc = damping / (6.0 + block_sums(d_ref, tmp) * 0.25)
    for ref in (up_ref, down_ref):
        ref[COARSE : COARSE + CY] = g
        ref[COARSE + CY : COARSE + 2 * CY] = vc
    for k in range(HF):
        for ref, plane, far in ((down_ref, k, HF - 1), (up_ref, NX - HF + k, 0)):
            value, weight = b_ref[plane], v_ref[plane]
            ref[NY * k : NY * (k + 1)] = weight * value if k == far else value
            if k != far:
                at = FACE + NY * (k if ref is down_ref else k - 1)
                ref[at : at + NY] = weight


def rows_kernel(b, v, mine, before, after, up_ref, down_ref):
    for k in range(1, EX - 1):
        for f in range(2):
            plane = layer(k, f, (b, v), before, after)
            at = ROWS * f + HF * (k - 1)
            down_ref[at : at + HF] = plane[:HF]
            up_ref[at : at + HF] = plane[NY - HF :]
    for f in range(2):
        for group in range(3):
            tile = tile_of(group, COARSE + CY * f, mine, before, after)
            at = 2 * ROWS + HC * (3 * f + group)
            down_ref[at : at + HC] = tile[:HC]
            up_ref[at : at + HC] = tile[CY - HC :]


def slots(lane, width, place):
    first = (lane >= width * place) & (lane < width * (place + 1))
    last = lane >= NZ - width if place == 0 else (lane >= width * (place - 1)) & (lane < width * place)
    return first, last


def unpack(before, after, width, place):
    lane = lanes(after.shape)
    both = jnp.where(slots(lane, width, place)[0], after, before)
    return edges(roll(both, -width * place), width)


def lanes_kernel(b, v, mine, before, after, low, high, be, ve, ge, vce, up_ref, down_ref):
    for f, k in PLACES:
        out = (be, ve)[f]
        out[k, 0:8] = jnp.zeros((8, NZ), F32)
        out[k, EY - 8 : EY] = jnp.zeros((8, NZ), F32)
        out[k, 4 : 4 + NY] = layer(k, f, (b, v), before, after)
        if 0 < k < EX - 1:
            at = ROWS * f + HF * (k - 1)
            out[k, 4 - HF : 4] = low[at : at + HF]
            out[k, 4 + NY : 4 + NY + HF] = high[at : at + HF]
    lane = lanes((EY, NZ))
    for tile in range(TILES):
        up = jnp.zeros((EY, NZ), F32)
        down = jnp.zeros((EY, NZ), F32)
        for place, (f, k) in enumerate(PLACES[PER * tile : PER * (tile + 1)]):
            moved = roll((be, ve)[f][k], DEEP * place)
            first, last = slots(lane, DEEP, place)
            up = jnp.where(last, moved, up)
            down = jnp.where(first, moved, down)
        up_ref[EY * tile : EY * (tile + 1)] = up
        down_ref[EY * tile : EY * (tile + 1)] = down
    lane = lanes((ER, NZ))
    for f, out in enumerate((ge, vce)):
        up = jnp.zeros((ER, NZ), F32)
        down = jnp.zeros((ER, NZ), F32)
        for group in range(3):
            at = 2 * ROWS + HC * (3 * f + group)
            tile = tile_of(group, COARSE + CY * f, mine, before, after)
            tile = with_rows(tile, low[at : at + HC], high[at : at + HC])
            out[group] = tile
            moved = roll(tile, DEEPC * group)
            first, last = slots(lane, DEEPC, group)
            up = jnp.where(last, moved, up)
            down = jnp.where(first, moved, down)
        at = EY * TILES + ER * f
        up_ref[at : at + ER] = up
        down_ref[at : at + ER] = down


def beyond_fine(k, f, before, after):
    tile, place = divmod(PLACES.index((f, k)), PER)
    return unpack(before[EY * tile : EY * (tile + 1)], after[EY * tile : EY * (tile + 1)], DEEP, place)


def beyond_coarse(group, f, before, after):
    at = EY * TILES + ER * f
    return unpack(before[at : at + ER], after[at : at + ER], DEEPC, group)


def crossed(block, beyond, step):
    lane = lanes(block.shape)
    below, below_beyond = roll(block, step), roll(beyond, step)
    above, above_beyond = roll(block, -step), roll(beyond, -step)
    low, high = lane < step, lane >= NZ - step
    return (
        jnp.where(low, below_beyond, below) + jnp.where(high, above_beyond, above),
        jnp.where(low, below, below_beyond) + jnp.where(high, above, above_beyond),
    )


PAD = 8


def neighbours(src, k, rows, step=1):
    at = PAD
    here = [src[part, k, at : at + rows] for part in range(2)]
    along = crossed(here[0], here[1], step)
    out = []
    for part in range(2):
        beside = src[part, k - 1, at : at + rows] + src[part, k + 1, at : at + rows]
        beside = beside + (src[part, k, at - 1 : at - 1 + rows] + src[part, k, at + 1 : at + 1 + rows])
        out.append(beside + along[part])
    return here, out


def expand(coarse, part, k, lo):
    c = (k - HF) // COARSEN + HC
    first = lax.broadcasted_iota(jnp.int32, (8, NZ), 0) < 4
    groups = []
    for j in range(EY // 8):
        row = 3 + 2 * j
        a = jnp.broadcast_to(coarse[part, c, row : row + 1], (8, NZ))
        b = jnp.broadcast_to(coarse[part, c, row + 1 : row + 2], (8, NZ))
        groups.append(jnp.where(first, a, b))
    return jnp.concatenate(groups, axis=0)


def coarse_neighbours(src, group):
    at = PAD
    here = [src[part, group, at : at + ER] for part in range(2)]
    along = crossed(here[0], here[1], COARSEN)
    lane = lanes((ER, NZ)) % 4
    out = []
    for part in range(2):
        below = roll(src[part, group - 1, at : at + ER], -3) if group > 0 else 0.0
        above = roll(src[part, group + 1, at : at + ER], 3) if group < 2 else 0.0
        beside = jnp.where(lane == 0, below, roll(here[part], 1)) + jnp.where(lane == 3, above, roll(here[part], -1))
        beside = beside + (src[part, group, at - 1 : at - 1 + ER] + src[part, group, at + 1 : at + 1 + ER])
        out.append(beside + along[part])
    return here, out


def precondition(rhs, weight, crhs, cweight, fa, fb, ca, cb, coarse):
    for ref, rows in ((fa, EY), (fb, EY), (ca, ER), (cb, ER)):
        for part in range(2):
            for k in range(ref.shape[1]):
                ref[part, k, 0:PAD] = jnp.zeros((PAD, NZ), F32)
                ref[part, k, PAD + rows :] = jnp.zeros((PAD, NZ), F32)
    for group in range(3):
        for part in range(2):
            ca[part, group, PAD : PAD + ER] = cweight[part][group] * crhs[part][group]
    src, dst = ca, cb
    for sweep in range(1, CSWEEPS):
        for group in range(3):
            here, beside = coarse_neighbours(src, group)
            for part in range(2):
                new = keep * here[part] + cweight[part][group] * (crhs[part][group] + beside[part])
                dst[part, group, PAD : PAD + ER] = new
        src, dst = dst, src
    for group, planes in enumerate(((3,), (0, 1, 2, 3), (0,))):
        for part in range(2):
            for c, plane in zip(planes, unmerge(src[part, group, PAD : PAD + ER], planes)):
                coarse[part, 4 * group + c] = plane
    for k in range(EX):
        for part in range(2):
            value = rhs[part][k]
            fa[part, k, PAD : PAD + EY] = weight[part][k] * value if 0 < k < EX - 1 else value
    src, dst = fa, fb
    for sweep in range(1, FSWEEPS):
        for k in range(sweep, EX - sweep):
            here, beside = neighbours(src, k, EY)
            for part in range(2):
                new = keep * here[part] + weight[part][k] * (rhs[part][k] + beside[part])
                if sweep == FSWEEPS - 1:
                    new = new + expand(coarse, part, k, 0)
                dst[part, k, PAD : PAD + EY] = new
        src, dst = dst, src


def image_plane(src, i):
    k, at = i + HF, PAD + 4
    here = [src[part, k, at : at + NY] for part in range(2)]
    along = crossed(here[0], here[1], 1)
    out = []
    for part in range(2):
        beside = src[part, k - 1, at : at + NY] + src[part, k + 1, at : at + NY]
        beside = beside + (src[part, k, at - 1 : at - 1 + NY] + src[part, k, at + 1 : at + 1 + NY])
        out.append(beside + along[part])
    return here, out


def add_up(x):
    return (x[0:8] + x[8:16]) + (x[16:24] + x[24:32])


SHARE = NZ // 8


def store_sums(out_ref, totals, row=None):
    row = jnp.zeros((1, NZ), F32) if row is None else row
    for i, part in totals.items():
        part = jnp.sum(part, axis=0, keepdims=True)
        for step in (64, 32, 16):
            part = part + roll(part, step)
        row = jnp.where(lanes((1, NZ)) // SHARE == i, part, row)
    out_ref[...] = row


NEAR = 4
NEARC = 16


def first_kernel(
    b_ref, d_ref, b, v, gm, vcm, before, after, p_ref, q_ref, qh_ref, vh_ref, vch_ref, up_ref, down_ref, sum_ref,
    bh, fa, fb, ca, cb, coarse, tmp,
):
    for f, k in PLACES:
        (bh, vh_ref)[f][k] = beyond_fine(k, f, before, after)
    gh = [beyond_coarse(group, 0, before, after) for group in range(3)]
    for group in range(3):
        vch_ref[group] = beyond_coarse(group, 1, before, after)
    precondition((b, bh), (v, vh_ref), (gm, gh), (vcm, vch_ref), fa, fb, ca, cb, coarse)
    rp = jnp.zeros((8, NZ), F32)
    pq = jnp.zeros((8, NZ), F32)
    for i in range(NX):
        (p, ph), (beside, beside_h) = image_plane(fa, i)
        q = (6.0 + d_ref[i]) * p - beside
        weight = vh_ref[i + HF, 4 : 4 + NY]
        within = weight > 0.0
        p_ref[i] = p
        q_ref[i] = q
        qh_ref[i] = jnp.where(within, damping / jnp.where(within, weight, 1.0) * ph - beside_h, 0.0)
        rp = rp + add_up(b_ref[i] * p)
        pq = pq + add_up(p * q)
    store_sums(sum_ref, {0: rp, 1: pq})
    for part, field in enumerate((q_ref, qh_ref)):
        tile = block_sums(field, tmp) * 0.25
        if part == 1:
            tile = roll(tile, NEARC)
        for ref in (up_ref, down_ref):
            ref[FACE + NY + CY * part : FACE + NY + CY * (part + 1)] = tile
    lane = lanes((NY, NZ))
    for ref, first, far in ((down_ref, 0, HF - 1), (up_ref, NX - HF, 0)):
        packed = jnp.zeros((NY, NZ), F32)
        for k in range(HF):
            value, beyond = q_ref[first + k], qh_ref[first + k]
            if k == far:
                value = value * v[HF + first + k, 4 : 4 + NY]
                beyond = beyond * vh_ref[HF + first + k, 4 : 4 + NY]
            ref[NY * k : NY * (k + 1)] = value
            packed = jnp.where(lane // (2 * NEAR) == k, roll(beyond, NEAR + 2 * NEAR * k), packed)
        ref[FACE : FACE + NY] = packed


def layer_beyond(k, own, before, after):
    if HF <= k < HF + NX:
        return own[k - HF]
    ref, ok, k = (before, inside()[0], k) if k < HF else (after, inside()[1], k - HF - NX)
    return jnp.where(ok, edges(roll(ref[FACE : FACE + NY], -NEAR - 2 * NEAR * k), NEAR), 0.0)


SIDE = NZ // (2 * NEAR)
WIDE = ROWS + 3 * HC


def second_rows_kernel(q, qh, mine, before, after, up_ref, down_ref):
    for k in range(1, EX - 1):
        plane = layer(k, 0, (q,), before, after)
        at = HF * (k - 1)
        down_ref[at : at + HF] = plane[:HF]
        up_ref[at : at + HF] = plane[NY - HF :]
    lane = lanes((8, NZ))
    wide = jnp.zeros((8, NZ), F32)
    for group in range(3):
        tile = tile_of(group, FACE + NY, mine, before, after)
        beyond = tile_of(group, FACE + NY + CY, mine, before, after)
        wide = jnp.where(lane // (2 * NEARC) == group, roll(beyond, 2 * NEARC * group), wide)
        at = ROWS + HC * group
        down_ref[at : at + HC] = tile[:HC]
        up_ref[at : at + HC] = tile[CY - HC :]
    for ref, rows in ((up_ref, slice(NY - 8, NY)), (down_ref, slice(0, 8))):
        ref[WIDE + 16 : WIDE + 24] = wide
        for half in range(2):
            packed = jnp.zeros((8, NZ), F32)
            for k in range(SIDE * half, min(EX, SIDE * (half + 1))):
                plane = layer_beyond(k, qh, before, after)[rows]
                packed = jnp.where(lane // (2 * NEAR) == k % SIDE, roll(plane, NEAR + 2 * NEAR * (k % SIDE)), packed)
            ref[WIDE + 8 * half : WIDE + 8 * (half + 1)] = packed


def second_kernel(
    b_ref, d_ref, p_ref, q_ref, qh_ref, v, vh_ref, vcm, vch, mine, before, after, low, high, first_ref,
    m_ref, im_ref, sum_ref, q, qh, fa, fb, ca, cb, coarse,
):
    for k in range(EX):
        at, place = HF * (k - 1), -NEAR - 2 * NEAR * (k % SIDE)
        for out in (q, qh):
            out[k, 0:8] = jnp.zeros((8, NZ), F32)
            out[k, EY - 8 : EY] = jnp.zeros((8, NZ), F32)
        q[k, 4 : 4 + NY] = layer(k, 0, (q_ref,), before, after)
        if 0 < k < EX - 1:
            q[k, 4 - HF : 4] = low[at : at + HF]
            q[k, 4 + NY : 4 + NY + HF] = high[at : at + HF]
        tile = slice(WIDE + 8 * (k // SIDE), WIDE + 8 * (k // SIDE + 1))
        qh[k, 4 - HF : 4] = edges(roll(low[tile], place), NEAR)[8 - HF :]
        qh[k, 4 : 4 + NY] = layer_beyond(k, qh_ref, before, after)
        qh[k, 4 + NY : 4 + NY + HF] = edges(roll(high[tile], place), NEAR)[:HF]
    g, gh = [], []
    for group in range(3):
        at, row = FACE + NY, ROWS + HC * group
        tile = with_rows(tile_of(group, at, mine, before, after), low[row : row + HC], high[row : row + HC])
        wide = [roll(ref[WIDE + 16 : WIDE + 24], -2 * NEARC * group) for ref in (low, high)]
        beyond = tile_of(group, at + CY, mine, before, after)
        beyond = with_rows(beyond, wide[0][CY - HC :], wide[1][:HC])
        g.append(tile)
        gh.append(edges(roll(beyond, -NEARC), NEARC))
    precondition((q, qh), (v, vh_ref), (g, gh), (vcm, vch), fa, fb, ca, cb, coarse)
    sums = [jnp.zeros((8, NZ), F32)] * 4
    for i in range(NX):
        (m, _), (beside, _) = image_plane(fa, i)
        im = (6.0 + d_ref[i]) * m - beside
        m_ref[i] = m
        im_ref[i] = im
        pairs = ((q_ref[i], m), (b_ref[i], m), (p_ref[i], im), (m, im))
        sums = [s + add_up(x * y) for s, (x, y) in zip(sums, pairs)]
    store_sums(sum_ref, dict(enumerate(sums, 2)), first_ref[...])


PARTS = 4


def last_kernel(b_ref, p_ref, q_ref, m_ref, im_ref, sum_ref, x_out, r_out, x_ref, r_ref, sems):
    rp, pq, qm, rm, pim, mim = [
        jnp.sum(jnp.where(lanes((1, NZ)) // SHARE == i, sum_ref[...], 0.0), axis=1, keepdims=True) for i in range(6)
    ]
    alpha = rp / pq
    rho = rp - alpha * (pq + rm) + alpha * alpha * qm
    scale = 1.0 + rho / rp
    alpha_next = rho / (scale * scale * pq - scale * alpha * (pim + qm) + alpha * alpha * mim)
    along = alpha + alpha_next * scale
    across = alpha_next * alpha
    copies = []
    for part in range(PARTS):
        planes = range(NX // PARTS * part, NX // PARTS * (part + 1))
        for i in planes:
            x_ref[i] = along * p_ref[i] - across * m_ref[i]
            r_ref[i] = b_ref[i] - along * q_ref[i] + across * im_ref[i]
        at = pl.ds(planes[0], len(planes))
        for which, (src, dst) in enumerate(((x_ref, x_out), (r_ref, r_out))):
            copies.append(pltpu.make_async_copy(src.at[at], dst.at[at], sems.at[2 * part + which]))
            copies[-1].start()
    for copy in copies:
        copy.wait()


def call(kernel, outs, scratch=(), name=None, out_space=pltpu.VMEM):
    def run(*args):
        return pl.pallas_call(
            kernel,
            out_shape=[jax.ShapeDtypeStruct(shape, F32) for shape in outs],
            in_specs=[VMEM] * len(args),
            out_specs=[pl.BlockSpec(memory_space=out_space)] * len(outs),
            scratch_shapes=[pltpu.VMEM(shape, F32) if isinstance(shape, tuple) else shape for shape in scratch],
            compiler_params=pltpu.CompilerParams(vmem_limit_bytes=24 * 2**20),
            name=name,
        )(*args)

    return run


def both_ways(up, down, axis):
    count = lax.axis_size(axis)
    if axis != "gz":
        steps = [(i, (i + 1) % count) for i in range(count if axis == "gx" else count - 1)]
        return lax.ppermute(up, axis, steps), lax.ppermute(down, axis, [(j, i) for i, j in steps])
    even = lax.axis_index(axis) % 2 == 0
    one = lax.ppermute(jnp.where(even, up, down), axis, [(i, i ^ 1) for i in range(count) if i ^ 1 < count])
    swaps = [(i, i + 1) for i in range(1, count - 1, 2)]
    two = lax.ppermute(jnp.where(even, down, up), axis, swaps + [(j, i) for i, j in swaps])
    return jnp.where(even, two, one), jnp.where(even, one, two)


def total(x, axis):
    count = math.prod(lax.axis_size(name) for name in axis)
    spread = jnp.broadcast_to(x[None], (count,) + x.shape)
    return jnp.sum(lax.all_to_all(spread, axis, 0, 0, tiled=True), axis=0)


def on_device(b, d):
    block, fine, tiles = (NX, NY, NZ), (EX, EY, NZ), (3, ER, NZ)
    work = [(2, EX, EY + 2 * PAD, NZ)] * 2 + [(2, 3, ER + 2 * PAD, NZ)] * 2 + [(2, EC, ER, NZ)]
    bd = lax.optimization_barrier(jnp.stack([b, d]))
    v, up, down = call(start_kernel, [block] + [(COARSE + 2 * CY, NZ)] * 2, [(CX, NY, NZ)], name="start")(bd)
    mine = up
    before, after = both_ways(up, down, "gx")
    up, down = call(rows_kernel, [(2 * ROWS + 6 * HC, NZ)] * 2, name="rows")(b, v, mine, before, after)
    low, high = both_ways(up, down, "gy")
    be, ve, gm, vcm, up, down = call(
        lanes_kernel, [fine] * 2 + [tiles] * 2 + [(EY * TILES + 2 * ER, NZ)] * 2, name="lanes"
    )(b, v, mine, before, after, low, high)
    before, after = both_ways(up, down, "gz")
    p, q, qh, vh, vch, up, down, sums = call(
        first_kernel,
        [block] * 3 + [fine, tiles] + [(FACE + NY + 2 * CY, NZ)] * 2 + [(1, NZ)],
        [fine] + work + [(CX, NY, NZ)],
        name="first",
    )(b, d, be, ve, gm, vcm, before, after)
    mine = up
    before, after = both_ways(up, down, "gx")
    up, down = call(second_rows_kernel, [(WIDE + 24, NZ)] * 2, name="second_rows")(q, qh, mine, before, after)
    low, high = both_ways(up, down, "gy")
    m, im, sums = call(second_kernel, [block, block, (1, NZ)], [fine, fine] + work, name="second")(
        b, d, p, q, qh, ve, vh, vcm, vch, mine, before, after, low, high, sums
    )
    for axis in (("gx",), ("gy", "gz")):
        sums = total(sums, axis)
    return call(
        last_kernel,
        [block, block],
        [block, block, pltpu.SemaphoreType.DMA((2 * PARTS,))],
        name="last",
        out_space=pl.ANY,
    )(b, p, q, m, im, sums)


def solution(mesh):
    spec = P("gx", "gy", "gz")
    return jax.shard_map(on_device, mesh=mesh, in_specs=(spec, spec), out_specs=(spec, spec), check_vma=False)
```
